32 devices in a mesh: dp: 8 (over y, x, core), tensor: 4 (over z).
Axes of the slice: x: 2, y: 2, z: 4, core: 2. Of those that a mesh axis runs over, the one named last changes fastest.
Arguments:
- teacher_in: bfloat16 [8192, 1600], P(('dp', 'tensor')), may hold values from -6 to 6
- student_in: bfloat16 [8192, 768], P(('dp', 'tensor')), may hold values from -6 to 6
- resp_mask: int32 [8192], P(('dp', 'tensor')), may hold values from 0 to 1, as said below
- replay: int32 [8], P('dp'), may hold values from 0 to 1
- t_gains: float32 [2, 1600], replicated, may hold values from 0.5 to 1.5
- t_shifts: float32 [2, 1600], replicated, may hold values from -1.75 to 1.75
- t_qkv: bfloat16 [1600, 3, 1792], P(None, None, 'tensor'), may hold values from -0.15625 to 0.15625
- t_out: bfloat16 [1792, 1600], P('tensor'), may hold values from -0.4375 to 0.4375
- t_fc: bfloat16 [1600, 6400], P(None, 'tensor'), may hold values from -0.15625 to 0.15625
- t_proj: bfloat16 [6400, 1600], P('tensor'), may hold values from -0.078125 to 0.078125
- s_norms: float32 [4, 768], replicated, may hold values from 0.1 to 1.9
- s_qkv: float32 [768, 3, 768], P(None, None, 'tensor'), may hold values from -0.21875 to 0.21875
- s_out: float32 [768, 768], P('tensor'), may hold values from -0.625 to 0.625
- s_fc: float32 [768, 3072], P(None, 'tensor'), may hold values from -0.21875 to 0.21875
- s_proj: float32 [3072, 768], P('tensor'), may hold values from -0.109375 to 0.109375
- s_map: float32 [768, 1600], replicated, may hold values from -0.21875 to 0.21875
- mom_qkv: float32 [768, 3, 768], P(None, None, 'tensor'), may hold values from -543.058 to 543.058
- mom_out: float32 [768, 768], P('tensor'), may hold values from -543.058 to 543.058
- mom_fc: float32 [768, 3072], P(None, 'tensor'), may hold values from -543.058 to 543.058
- mom_proj: float32 [3072, 768], P('tensor'), may hold values from -271.529 to 271.529
- mom_map: float32 [768, 1600], replicated, may hold values from -1024 to 1024
- adam_first: float32 [4, 768], replicated, may hold values from -112 to 112
- adam_second: float32 [4, 768], replicated, may hold values from 32.768 to 131.072
Outputs:
- teacher_out: bfloat16 [8192, 1600], P(('dp', 'tensor'))
- student_out: bfloat16 [8192, 768], P(('dp', 'tensor'))
- input_grad: float32 [8192, 768], P(('dp', 'tensor'))
- loss: float32 [], replicated
- grad_qkv: float32 [768, 3, 768], P(None, None, 'tensor')
- grad_out: float32 [768, 768], P('tensor')
- grad_fc: float32 [768, 3072], P(None, 'tensor')
- grad_proj: float32 [3072, 768], P('tensor')
- grad_map: float32 [768, 1600], replicated
- moment_qkv: float32 [768, 3, 768], P(None, None, 'tensor')
- moment_out: float32 [768, 768], P('tensor')
- moment_fc: float32 [768, 3072], P(None, 'tensor')
- moment_proj: float32 [3072, 768], P('tensor')
- moment_map: float32 [768, 1600], replicated
- weight_qkv: float32 [768, 3, 768], P(None, None, 'tensor')
- weight_out: float32 [768, 768], P('tensor')
- weight_fc: float32 [768, 3072], P(None, 'tensor')
- weight_proj: float32 [3072, 768], P('tensor')
- weight_map: float32 [768, 1600], replicated
- norm_first: float32 [4, 768], replicated
- norm_second: float32 [4, 768], replicated
- norm_values: float32 [4, 768], replicated
The draws below stay inside these ranges and needn't reach their ends.
Inputs may be any that keep to these rules, and one draw needn't show every extreme that they name: `resp_mask`: the ones of each sequence form one run that ends at its last position and holds at least one token.
All inputs are finite; a program needn't handle non-finite values.
Results may differ from the reference program's by a relative error of at most 0.006.
The reference program's roundings to bfloat16 on the way count: a program that leaves them out, or rounds other values in their place, can miss the bound.
Values may be sent and summed in bfloat16 or wider, within the bound.
A program may use at most 256 MiB of HBM per device.

```python
import math
import jax
import jax.numpy as jnp
from jax import lax

DT = 1600
HT = 25
FT = 6400
DS = 768
HS = 12
FS = 3072
HEAD = 64
LEN = 1024
STEP = 10
QBLK = 512
SLOT = 7
TSLOTS = 28
SEQS = 8
TOKENS = 8192
N_TENSOR = 4


def draw_resp_mask(key, part):
    key = jax.random.fold_in(key, 11)
    seq_order = jnp.arange(SEQS, dtype=jnp.int32)
    least_len = LEN // 8 + LEN // 4 * seq_order // max(SEQS - 1, 1)
    answer = jax.random.randint(key, (SEQS,), least_len, 2 * least_len + 1)
    position = jnp.arange(LEN, dtype=jnp.int32)
    return (position[None, :] >= LEN - answer[:, None]).astype(jnp.int32).reshape(SEQS * LEN)


def rising_normal(key, shape, axis_num, scale, rise, divisor):
    base = jnp.clip(jax.random.normal(key, shape, jnp.float32), -3.0, 3.0)
    length = shape[axis_num]
    place = jnp.arange(length, dtype=jnp.float32) / max(length - 1, 1)
    ramp = (1.0 + rise * place) / divisor
    view = [1] * len(shape)
    view[axis_num] = length
    return scale * base * ramp.reshape(view)


def draw_mom_qkv(key, part):
    key = jax.random.fold_in(key, 21)
    return rising_normal(key, (DS, 3, DS), 2, TOKENS ** 0.5, 2.0, 2.0)


def draw_mom_out(key, part):
    key = jax.random.fold_in(key, 22)
    return rising_normal(key, (DS, DS), 0, TOKENS ** 0.5, 2.0, 2.0)


def draw_mom_fc(key, part):
    key = jax.random.fold_in(key, 23)
    return rising_normal(key, (DS, FS), 1, TOKENS ** 0.5, 2.0, 2.0)


def draw_mom_proj(key, part):
    key = jax.random.fold_in(key, 24)
    return rising_normal(key, (FS, DS), 0, 0.5 * TOKENS ** 0.5, 2.0, 2.0)


def plant(entries, stream_key, low, high):
    longest = entries.shape.index(max(entries.shape))
    spots = []
    for shift in (0, 1):
        where = [jax.random.randint(jax.random.fold_in(stream_key, axis), (), 0, length) for axis, length in enumerate(entries.shape)]
        where[longest] = (where[longest] + shift) % entries.shape[longest]
        spots.append(tuple(where))
    return entries.at[spots[0]].set(low).at[spots[1]].set(high)


def levels(rng, dims, cuts, least, largest):
    loudness = 1.0
    for dim, parts in cuts:
        heights = jax.random.uniform(jax.random.fold_in(jax.random.fold_in(rng, 6), dim), (parts,), jnp.float32, least / len(cuts), largest / len(cuts))
        loudness = loudness * jnp.repeat(jnp.exp(heights), dims[dim] // parts).reshape((-1,) + (1,) * (len(dims) - 1 - dim))
    return loudness


def noise(rng, shape, scale, bound, shards=(), held_as=jnp.bfloat16):
    level = levels(rng, shape, shards, -0.22, 0.18) if shards else 1.0
    values = jax.random.normal(rng, shape, jnp.float32) * scale * level
    return jnp.minimum(jnp.maximum(values, -bound), bound).astype(held_as)


def setup_inputs(seed: int = 0) -> dict:
    seeds = jax.random.split(jax.random.key(seed), 24)
    return {
        "teacher_in": noise(seeds[0], (TOKENS, DT), 1.0, 6.0, ((0, 32),)),
        "student_in": noise(seeds[1], (TOKENS, DS), 1.0, 6.0, ((0, 32),)),
        "resp_mask": draw_resp_mask(jax.random.fold_in(seeds[23], 71), 0),
        "replay": plant(jax.random.randint(seeds[3], (SEQS,), 0, 2), jax.random.fold_in(seeds[3], 1), 0, 1).astype(jnp.int32),
        "t_gains": jnp.clip(1.0 + 0.1 * jax.random.normal(seeds[4], (2, DT), jnp.float32), 0.5, 1.5),
        "t_shifts": noise(seeds[5], (2, DT), 0.3, 1.75, (), jnp.float32),
        "t_qkv": noise(seeds[6], (DT, 3, TSLOTS * HEAD), DT ** -0.5, 0.15625, ((2, 4),)),
        "t_out": noise(seeds[7], (TSLOTS * HEAD, DT), (DT // 8) ** -0.5, 0.4375, ((0, 4),)),
        "t_fc": noise(seeds[8], (DT, FT), DT ** -0.5, 0.15625, ((1, 4),)),
        "t_proj": noise(seeds[9], (FT, DT), FT ** -0.5, 0.078125, ((0, 4),)),
        "s_norms": jnp.clip(1.0 + 0.18 * jax.random.normal(seeds[10], (4, DS), jnp.float32), 0.1, 1.9),
        "s_qkv": noise(seeds[11], (DS, 3, DS), DS ** -0.5, 0.21875, ((2, 4),), jnp.float32),
        "s_out": noise(seeds[12], (DS, DS), (DS // 8) ** -0.5, 0.625, ((0, 4),), jnp.float32),
        "s_fc": noise(seeds[13], (DS, FS), DS ** -0.5, 0.21875, ((1, 4),), jnp.float32),
        "s_proj": noise(seeds[14], (FS, DS), FS ** -0.5, 0.109375, ((0, 4),), jnp.float32),
        "s_map": noise(seeds[15], (DS, DT), DS ** -0.5, 0.21875, (), jnp.float32),
        "mom_qkv": draw_mom_qkv(jax.random.fold_in(seeds[23], 71), 0),
        "mom_out": draw_mom_out(jax.random.fold_in(seeds[23], 71), 0),
        "mom_fc": draw_mom_fc(jax.random.fold_in(seeds[23], 71), 0),
        "mom_proj": draw_mom_proj(jax.random.fold_in(seeds[23], 71), 0),
        "mom_map": noise(seeds[20], (DS, DT), (2.0 * TOKENS ** 0.5), 1024.0, (), jnp.float32),
        "adam_first": noise(seeds[21], (4, DS), (0.2 * TOKENS ** 0.5), 112.0, (), jnp.float32),
        "adam_second": jnp.clip(jnp.exp(jax.random.uniform(seeds[22], (4, DS), jnp.float32, math.log(32.768), math.log(131.072))), 32.768, 131.072),
    }


EPS = 1e-05
NS_A = 3.4445
NS_B = -4.775
NS_C = 2.0315
MOMENTUM = 0.95
MUON_RATE = 0.5
MUON_DECAY = 0.01
ADAM_RATE = 0.3
BETA_ONE = 0.9
BETA_TWO = 0.999
ADAM_EPS = 1e-08
ADAM_DECAY = 0.01
REPLAY_CUT = 0.5
NEG_FILL = -1e+30
HIGH = lax.Precision.HIGHEST

@jax.custom_vjp
def low(v):
    return lax.optimization_barrier(v.astype(jnp.bfloat16)).astype(jnp.float32)

@jax.custom_vjp
def low_back(v):
    return v

def low_keep(v):
    return (low(v), None)

def low_pass(kept, grad):
    return (grad,)

def back_keep(v):
    return (v, None)

def back_low(kept, grad):
    return (low(grad),)
low.defvjp(low_keep, low_pass)
low_back.defvjp(back_keep, back_low)

def dot_high(left, right):
    return jnp.dot(left, right, precision=HIGH, preferred_element_type=jnp.float32)

def layer_norm(v, gain_vec, shift_vec):
    row_mean = lax.optimization_barrier(jnp.mean(v, axis=-1, keepdims=True))
    centred = v - row_mean
    row_var = lax.optimization_barrier(jnp.mean(centred * centred, axis=-1, keepdims=True))
    return centred * lax.rsqrt(row_var + EPS) * gain_vec + shift_vec

def smooth_gelu(v):
    return 0.5 * v * (1.0 + jnp.tanh(0.7978845608028654 * (v + 0.044715 * v * v * v)))

def attention(query, keys, values):
    head_count = query.shape[1]
    blocks = LEN // QBLK
    key_pos = jnp.arange(LEN).astype(jnp.int32)

    def one_block(block_args):
        query_block, row_start = block_args
        scores = jnp.einsum('qhe,khe->hqk', query_block, keys, precision=HIGH) * HEAD ** (-0.5)
        row_pos = row_start + jnp.arange(QBLK).astype(jnp.int32)
        scores = jnp.where(key_pos[None, None, :] <= row_pos[None, :, None], scores, NEG_FILL)
        scores = low_back(scores)
        exp_vals = jnp.exp(scores - lax.optimization_barrier(jnp.max(scores, axis=-1, keepdims=True)))
        prob_vals = low(exp_vals / lax.optimization_barrier(jnp.sum(exp_vals, axis=-1, keepdims=True)))
        return jnp.einsum('hqk,khe->qhe', prob_vals, values, precision=HIGH)
    starts = (jnp.arange(blocks) * QBLK).astype(jnp.int32)
    out_blocks = lax.map(jax.checkpoint(one_block), (query.reshape(blocks, QBLK, head_count, HEAD), starts))
    return out_blocks.reshape(LEN, head_count, HEAD)

def slot_live():
    slot_ids = jnp.arange(TSLOTS).astype(jnp.int32)
    slot_owner = slot_ids // SLOT
    slot_place = slot_ids % SLOT
    live_count = HT // N_TENSOR + (slot_owner < HT % N_TENSOR).astype(jnp.int32)
    return (slot_place < live_count).astype(jnp.float32)

def teacher_block(teacher_x, gains, shifts, w_qkv, w_out, w_fc, w_proj, live_slots):
    normed = low(layer_norm(teacher_x, gains[0], shifts[0]))
    mixed_qkv = low(dot_high(normed, w_qkv.reshape(DT, 3 * TSLOTS * HEAD))).reshape(LEN, 3, TSLOTS, HEAD)
    head_out = attention(mixed_qkv[:, 0], mixed_qkv[:, 1], mixed_qkv[:, 2]) * live_slots[None, :, None]
    head_out = low(head_out.reshape(LEN, TSLOTS * HEAD))
    resid = teacher_x + dot_high(head_out, w_out)
    normed_two = low(layer_norm(resid, gains[1], shifts[1]))
    hidden = low(smooth_gelu(dot_high(normed_two, w_fc)))
    return resid + dot_high(hidden, w_proj)

def student_block(student_x, params, target, weight, factor):
    norms, w_qkv, w_out, w_fc, w_proj, w_map = params
    normed = low(layer_norm(student_x, norms[0], norms[1]))
    mixed_qkv = dot_high(normed, low(w_qkv).reshape(DS, 3 * DS)).reshape(LEN, 3, HS, HEAD)
    mixed_qkv = low_back(low(mixed_qkv))
    head_out = attention(mixed_qkv[:, 0], mixed_qkv[:, 1], mixed_qkv[:, 2])
    head_out = low_back(low(head_out.reshape(LEN, DS)))
    resid = student_x + low_back(dot_high(head_out, low(w_out)))
    normed_two = low(layer_norm(resid, norms[2], norms[3]))
    before = low_back(dot_high(normed_two, low(w_fc)))
    hidden = low(smooth_gelu(before))
    output = resid + low_back(dot_high(hidden, low(w_proj)))
    guess_vec = low_back(dot_high(low(output), low(w_map)))
    miss_vec = guess_vec - target
    loss_sum = jnp.sum(weight[:, None] * miss_vec * miss_vec)
    return (factor * loss_sum, (output, loss_sum))

def qkv_stack(mat):
    shard_width = DS // N_TENSOR
    return mat.reshape(DS, 3, N_TENSOR, shard_width).transpose(2, 0, 1, 3).reshape(N_TENSOR, DS, 3 * shard_width)

def qkv_unstack(stacked):
    shard_width = DS // N_TENSOR
    return stacked.reshape(N_TENSOR, DS, 3, shard_width).transpose(1, 2, 0, 3).reshape(DS, 3, DS)

def column_stack(mat):
    return mat.reshape(mat.shape[0], N_TENSOR, mat.shape[1] // N_TENSOR).transpose(1, 0, 2)

def column_unstack(stacked):
    return stacked.transpose(1, 0, 2).reshape(stacked.shape[1], -1)

def muon(grad_mat, old_moment, weight_mat, stacked_fn, unstack_fn, gain_val):
    moment = MOMENTUM * old_moment + grad_mat
    pieces = stacked_fn(moment)
    iterate = pieces / (jnp.sqrt(jnp.sum(pieces * pieces)) + 1e-07)
    for sweep_index in range(5):
        gram_sum = lax.optimization_barrier(jnp.sum(jnp.einsum('psc,ptc->pst', iterate, iterate, precision=HIGH), axis=0))
        square = dot_high(gram_sum, gram_sum)
        poly_mat = NS_B * gram_sum + NS_C * square
        iterate = NS_A * iterate + jnp.einsum('st,ptc->psc', poly_mat, iterate, precision=HIGH)
    renewed = (1.0 - MUON_RATE * MUON_DECAY) * weight_mat - MUON_RATE * gain_val * unstack_fn(iterate)
    return (moment, renewed)

def reference(teacher_in, student_in, resp_mask, replay, t_gains, t_shifts, t_qkv, t_out, t_fc, t_proj, s_norms, s_qkv, s_out, s_fc, s_proj, s_map, mom_qkv, mom_out, mom_fc, mom_proj, mom_map, adam_first, adam_second):
    live_slots = slot_live()
    teacher_w = (t_qkv.astype(jnp.float32), t_out.astype(jnp.float32), t_fc.astype(jnp.float32), t_proj.astype(jnp.float32))

    def teacher_seq(teacher_x):
        return teacher_block(teacher_x, t_gains, t_shifts, *teacher_w, live_slots).astype(jnp.bfloat16)
    teacher_out = lax.map(teacher_seq, teacher_in.astype(jnp.float32).reshape(SEQS, LEN, DT))
    targets = teacher_out.astype(jnp.float32)
    count = jnp.sum(resp_mask)
    factor = TOKENS / (2.0 * count.astype(jnp.float32))
    flag_tok = jnp.repeat(replay.astype(jnp.float32), LEN)
    weights = (resp_mask.astype(jnp.float32) * (1.0 - REPLAY_CUT * flag_tok)).reshape(SEQS, LEN)
    params = (s_norms, s_qkv, s_out, s_fc, s_proj, s_map)

    def seq_step(total, seq_args):
        student_x, target, weight = seq_args

        def objective(x_in, param_in):
            return student_block(x_in, param_in, target, weight, factor)
        value, pull_back, extra = jax.vjp(objective, student_x, params, has_aux=True)
        grad_x, grad_params = pull_back(jnp.ones((), jnp.float32))
        total = jax.tree.map(jnp.add, total, grad_params)
        return (total, (extra[0].astype(jnp.bfloat16), grad_x, extra[1]))
    zero_acc = jax.tree.map(jnp.zeros_like, params)
    grads, (student_out, input_grad, loss_parts) = lax.scan(seq_step, zero_acc, (student_in.astype(jnp.float32).reshape(SEQS, LEN, DS), targets, weights))
    grad_norms, grad_qkv, grad_out, grad_fc, grad_proj, grad_map = grads
    loss = jnp.sum(loss_parts) / (count.astype(jnp.float32) * DT)
    moment_qkv, weight_qkv = muon(grad_qkv, mom_qkv, s_qkv, qkv_stack, qkv_unstack, math.sqrt(3.0))
    moment_out, weight_out = muon(grad_out, mom_out, s_out, lambda m: column_stack(m.T), lambda s: column_unstack(s).T, 1.0)
    moment_fc, weight_fc = muon(grad_fc, mom_fc, s_fc, column_stack, column_unstack, math.sqrt(FS / DS))
    moment_proj, weight_proj = muon(grad_proj, mom_proj, s_proj, lambda m: column_stack(m.T), lambda s: column_unstack(s).T, 1.0)
    moment_map, weight_map = muon(grad_map, mom_map, s_map, lambda m: m[None], lambda s: s[0], math.sqrt(DT / DS))
    norm_first = BETA_ONE * adam_first + (1.0 - BETA_ONE) * grad_norms
    norm_second = BETA_TWO * adam_second + (1.0 - BETA_TWO) * grad_norms * grad_norms
    fix_one = 1.0 - BETA_ONE ** STEP
    fix_two = 1.0 - BETA_TWO ** STEP
    norm_values = s_norms - ADAM_RATE * (norm_first / fix_one / (jnp.sqrt(norm_second / fix_two) + ADAM_EPS) + ADAM_DECAY * s_norms)
    return (teacher_out.reshape(TOKENS, DT), student_out.reshape(TOKENS, DS), input_grad.reshape(TOKENS, DS), loss, grad_qkv, grad_out, grad_fc, grad_proj, grad_map, moment_qkv, moment_out, moment_fc, moment_proj, moment_map, weight_qkv, weight_out, weight_fc, weight_proj, weight_map, norm_first, norm_second, norm_values)
```

```python
import functools
import math

import jax
import jax.numpy as jnp
from jax import lax
from jax.experimental import pallas as pl
from jax.experimental.pallas import tpu as pltpu
from jax.sharding import PartitionSpec as P

DT = 1600
HT = 25
DS = 768
FS = 3072
HEAD = 64
LEN = 1024
STEP = 10
ABLK = 256


EPS = 1e-05
NS_A = 3.4445
NS_B = -4.775
NS_C = 2.0315
MOMENTUM = 0.95
MUON_RATE = 0.5
MUON_DECAY = 0.01
ADAM_RATE = 0.3
BETA_ONE = 0.9
BETA_TWO = 0.999
ADAM_EPS = 1e-08
ADAM_DECAY = 0.01
REPLAY_CUT = 0.5
NEG_FILL = -1e30
HIGH = lax.Precision.HIGHEST


def norm_parts(v, gain_vec, shift_vec):
    row_mean = jnp.mean(v, axis=-1, keepdims=True)
    centred = v - row_mean
    row_var = jnp.mean(centred * centred, axis=-1, keepdims=True)
    inv_scale = lax.rsqrt(row_var + EPS)
    unit_val = centred * inv_scale
    return (unit_val * gain_vec + shift_vec, unit_val, inv_scale)


def norm_back(grad_norm, unit_val, inv_scale, gain_vec):
    grad_unit = grad_norm * gain_vec
    first_mean = jnp.mean(grad_unit, axis=-1, keepdims=True)
    second_mean = jnp.mean(grad_unit * unit_val, axis=-1, keepdims=True)
    return inv_scale * (grad_unit - first_mean - unit_val * second_mean)


def smooth_gelu(v):
    return 0.5 * v * (1.0 + jnp.tanh(0.7978845608028654 * (v + 0.044715 * v * v * v)))


def whole_vmem():
    return pl.BlockSpec(memory_space=pltpu.VMEM)


def nt_dot(left, right):
    return lax.dot_general(
        left, right, (((1,), (1,)), ((), ())), preferred_element_type=jnp.float32
    )


def tn_dot(left, right):
    return lax.dot_general(
        left, right, (((0,), (0,)), ((), ())), preferred_element_type=jnp.float32
    )


def plain_dot(left, right):
    return jnp.dot(left, right, preferred_element_type=jnp.float32)


def lower_mask():
    row_pos = lax.broadcasted_iota(jnp.int32, (ABLK, ABLK), 0)
    key_pos = lax.broadcasted_iota(jnp.int32, (ABLK, ABLK), 1)
    return key_pos <= row_pos


def attend_forward_kernel(head_count, qkv_ref, out_ref, log_ref):
    width = head_count * HEAD
    for head in range(head_count):
        cols = slice(head * HEAD, (head + 1) * HEAD)
        keys = qkv_ref[:, width + head * HEAD : width + (head + 1) * HEAD]
        values = qkv_ref[:, 2 * width + head * HEAD : 2 * width + (head + 1) * HEAD]
        for block in range(LEN // ABLK):
            low, high = block * ABLK, (block + 1) * ABLK
            query = qkv_ref[low:high, cols]
            near = nt_dot(query, keys[low:high]) * HEAD ** (-0.5)
            near = jnp.where(lower_mask(), near, NEG_FILL)
            row_top = jnp.max(near, axis=-1, keepdims=True)
            if block:
                far = nt_dot(query, keys[:low]) * HEAD ** (-0.5)
                row_top = jnp.maximum(row_top, jnp.max(far, axis=-1, keepdims=True))
            near = jnp.exp(near - row_top)
            row_total = jnp.sum(near, axis=-1, keepdims=True)
            if block:
                far = jnp.exp(far - row_top)
                row_total = row_total + jnp.sum(far, axis=-1, keepdims=True)
            inverse = 1.0 / row_total
            mixed = plain_dot((near * inverse).astype(jnp.bfloat16), values[low:high])
            if block:
                mixed = mixed + plain_dot((far * inverse).astype(jnp.bfloat16), values[:low])
            out_ref[low:high, cols] = mixed.astype(out_ref.dtype)
            log_ref[low:high, head : head + 1] = row_top + jnp.log(row_total)


def attend_forward(mixed_qkv, head_count):
    width = head_count * HEAD
    return pl.pallas_call(
        functools.partial(attend_forward_kernel, head_count),
        out_shape=(
            jax.ShapeDtypeStruct((LEN, width), jnp.bfloat16),
            jax.ShapeDtypeStruct((LEN, 128), jnp.float32),
        ),
        in_specs=[whole_vmem()],
        out_specs=(whole_vmem(), whole_vmem()),
        compiler_params=pltpu.CompilerParams(vmem_limit_bytes=40 * 2**20),
        cost_estimate=pl.CostEstimate(
            flops=4 * head_count * LEN * LEN * HEAD * 4,
            bytes_accessed=LEN * width * 8,
            transcendentals=head_count * LEN * LEN // 2,
        ),
    )(mixed_qkv)


def attend_backward_kernel(
    head_count, qkv_ref, log_ref, grad_ref, out_ref, key_acc, value_acc
):
    width = head_count * HEAD
    scale = HEAD ** (-0.5)
    for head in range(head_count):
        cols = slice(head * HEAD, (head + 1) * HEAD)
        key_cols = slice(width + head * HEAD, width + (head + 1) * HEAD)
        value_cols = slice(2 * width + head * HEAD, 2 * width + (head + 1) * HEAD)
        keys = qkv_ref[:, key_cols]
        values = qkv_ref[:, value_cols]
        for block in range(LEN // ABLK - 1, -1, -1):
            low, high = block * ABLK, (block + 1) * ABLK
            query = qkv_ref[low:high, cols]
            grad = grad_ref[low:high, cols]
            log_sum = log_ref[low:high, head : head + 1]
            near = nt_dot(query, keys[low:high]) * scale
            near = jnp.exp(jnp.where(lower_mask(), near, NEG_FILL) - log_sum)
            near_back = nt_dot(grad, values[low:high])
            inner = jnp.sum(near * near_back, axis=-1, keepdims=True)
            if block:
                far = jnp.exp(nt_dot(query, keys[:low]) * scale - log_sum)
                far_back = nt_dot(grad, values[:low])
                inner = inner + jnp.sum(far * far_back, axis=-1, keepdims=True)
            near_score = (near * (near_back - inner)).astype(jnp.bfloat16)
            grad_query = plain_dot(near_score, keys[low:high])
            near_key = tn_dot(near_score, query)
            near_value = tn_dot(near.astype(jnp.bfloat16), grad)
            if block == LEN // ABLK - 1:
                key_acc[low:high, :] = near_key
                value_acc[low:high, :] = near_value
            else:
                key_acc[low:high, :] += near_key
                value_acc[low:high, :] += near_value
            if block:
                far_score = (far * (far_back - inner)).astype(jnp.bfloat16)
                grad_query = grad_query + plain_dot(far_score, keys[:low])
                far_key = tn_dot(far_score, query)
                far_value = tn_dot(far.astype(jnp.bfloat16), grad)
                if block == LEN // ABLK - 1:
                    key_acc[:low, :] = far_key
                    value_acc[:low, :] = far_value
                else:
                    key_acc[:low, :] += far_key
                    value_acc[:low, :] += far_value
            out_ref[low:high, cols] = (grad_query * scale).astype(jnp.bfloat16)
        out_ref[:, key_cols] = (key_acc[...] * scale).astype(jnp.bfloat16)
        out_ref[:, value_cols] = value_acc[...].astype(jnp.bfloat16)


def attend_backward(mixed_qkv, log_sums, grad_heads, head_count):
    width = head_count * HEAD
    return pl.pallas_call(
        functools.partial(attend_backward_kernel, head_count),
        out_shape=jax.ShapeDtypeStruct((LEN, 3 * width), jnp.bfloat16),
        in_specs=[whole_vmem()] * 3,
        out_specs=whole_vmem(),
        scratch_shapes=[pltpu.VMEM((LEN, HEAD), jnp.float32)] * 2,
        compiler_params=pltpu.CompilerParams(vmem_limit_bytes=40 * 2**20),
        cost_estimate=pl.CostEstimate(
            flops=10 * head_count * LEN * LEN * HEAD * 4,
            bytes_accessed=LEN * width * 16,
            transcendentals=head_count * LEN * LEN // 2,
        ),
    )(mixed_qkv, log_sums, grad_heads)


MESH_ID = pl.DeviceIdType.MESH


def place_of():
    dp_count = lax.axis_size("dp")
    rank = lax.axis_index("dp")
    return dp_count // 2, rank // 2, rank % 2, lax.axis_index("tensor")


def greet(peers):
    barrier = pltpu.get_barrier_semaphore()
    for peer in peers:
        pl.semaphore_signal(barrier, inc=1, device_id=peer, device_id_type=MESH_ID)
    pl.semaphore_wait(barrier, len(peers))


def send_to(src, dst, send_sem, recv_sem, peer):
    return pltpu.make_async_remote_copy(
        src_ref=src,
        dst_ref=dst,
        send_sem=send_sem,
        recv_sem=recv_sem,
        device_id=peer,
        device_id_type=MESH_ID,
    )


def sum_small_kernel(
    x_ref, out_ref, pair, plane, line, pair_sems, plane_sems, line_sems
):
    chips, chip, core, depth = place_of()
    depths = lax.axis_size("tensor")
    sibling = (chip * 2 + 1 - core, depth)
    flat = [((lax.rem(chip + k, chips)) * 2 + core, depth) for k in range(1, chips)]
    deep = [(chip * 2 + core, lax.rem(depth + k, depths)) for k in range(1, depths)]
    greet([sibling] + flat + deep)
    copy = send_to(x_ref, pair, pair_sems.at[0], pair_sems.at[1], sibling)
    copy.start()
    copy.wait()
    plane[chip] = x_ref[...] + pair[...]
    copies = []
    for k in range(1, chips):
        copies.append(
            send_to(
                plane.at[chip], plane.at[chip], plane_sems.at[0, k], plane_sems.at[1, k], flat[k - 1]
            )
        )
    for copy in copies:
        copy.start()
    for copy in copies:
        copy.wait()
    total = plane[0]
    for k in range(1, chips):
        total = total + plane[k]
    line[depth] = total
    copies = []
    for k in range(1, depths):
        copies.append(
            send_to(
                line.at[depth], line.at[depth], line_sems.at[0, k], line_sems.at[1, k], deep[k - 1]
            )
        )
    for copy in copies:
        copy.start()
    for copy in copies:
        copy.wait()
    total = line[0]
    for k in range(1, depths):
        total = total + line[k]
    out_ref[...] = total


def sum_small(block, collective):
    chips, depths = lax.axis_size("dp") // 2, lax.axis_size("tensor")
    return pl.pallas_call(
        sum_small_kernel,
        out_shape=jax.ShapeDtypeStruct(block.shape, jnp.float32),
        in_specs=[whole_vmem()],
        out_specs=whole_vmem(),
        scratch_shapes=[
            pltpu.VMEM(block.shape, jnp.float32),
            pltpu.VMEM((chips,) + block.shape, jnp.float32),
            pltpu.VMEM((depths,) + block.shape, jnp.float32),
            pltpu.SemaphoreType.DMA((2,)),
            pltpu.SemaphoreType.DMA((2, chips)),
            pltpu.SemaphoreType.DMA((2, depths)),
        ],
        compiler_params=pltpu.CompilerParams(
            collective_id=collective, has_side_effects=True, vmem_limit_bytes=16 * 2**20
        ),
        cost_estimate=pl.CostEstimate(flops=10**10, bytes_accessed=10**6, transcendentals=0),
    )(block)


def sum_and_spread_kernel(
    x_ref,
    y_ref,
    x_out,
    y_out,
    pair_in,
    pair_sum,
    plane_in,
    total,
    pair_sems,
    plane_sems,
    spread_sems,
    share_sems,
):
    chips, chip, core, depth = place_of()
    rank = chip * 2 + core
    other = 1 - core
    sibling = (chip * 2 + other, depth)
    chip_at = [lax.rem(chip + k, chips) for k in range(chips)]
    flat = [(chip_at[k] * 2 + core, depth) for k in range(chips)]
    greet([sibling] + flat[1:])
    order = list(range(1, chips)) + [0]
    pair_copies, plane_copies = {}, {}
    for k in order:
        pair_copies[k] = send_to(
            x_ref.at[chip_at[k] * 2 + other],
            pair_in.at[k],
            pair_sems.at[0, k],
            pair_sems.at[1, k],
            sibling,
        )
        pair_copies[k].start()
    for k in order:
        pair_copies[k].wait_recv()
        pair_sum[k] = x_ref[chip_at[k] * 2 + core] + pair_in[k]
        if k:
            plane_copies[k] = send_to(
                pair_sum.at[k], plane_in.at[k], plane_sems.at[0, k], plane_sems.at[1, k], flat[k]
            )
            plane_copies[k].start()
    y_spread = start_spread(y_ref, y_out, spread_sems.at[0], flat, rank)
    y_out[rank] = y_ref[...]
    value = pair_sum[0]
    for k in range(1, chips):
        plane_copies[k].wait_recv()
        value = value + plane_in[k]
    total[...] = value
    x_spread = start_spread(total, x_out, spread_sems.at[1], flat, rank)
    x_out[rank] = value
    y_share = start_share(y_out, y_spread, share_sems.at[0], (chips, chip, core), sibling)
    x_share = start_share(x_out, x_spread, share_sems.at[1], (chips, chip, core), sibling)
    for k in range(chips):
        y_share[k].wait_recv()
        x_share[k].wait_recv()
    for copies in (pair_copies, plane_copies, y_spread, x_spread, y_share, x_share):
        for copy in copies.values():
            copy.wait_send()


def sum_and_spread(rows, slab_y, collective):
    dp_count = lax.axis_size("dp")
    chips = dp_count // 2
    count, width = rows.shape
    slab = (count // dp_count, width)
    out_x, out_y = pl.pallas_call(
        sum_and_spread_kernel,
        out_shape=(
            jax.ShapeDtypeStruct((dp_count,) + slab, jnp.float32),
            jax.ShapeDtypeStruct((dp_count,) + slab_y.shape, jnp.float32),
        ),
        in_specs=[whole_vmem()] * 2,
        out_specs=(whole_vmem(), whole_vmem()),
        scratch_shapes=[
            pltpu.VMEM((chips,) + slab, jnp.float32),
            pltpu.VMEM((chips,) + slab, jnp.float32),
            pltpu.VMEM((chips,) + slab, jnp.float32),
            pltpu.VMEM(slab, jnp.float32),
            pltpu.SemaphoreType.DMA((2, chips)),
            pltpu.SemaphoreType.DMA((2, chips)),
            pltpu.SemaphoreType.DMA((2, 2, chips)),
            pltpu.SemaphoreType.DMA((2, 2, chips)),
        ],
        compiler_params=pltpu.CompilerParams(
            collective_id=collective, has_side_effects=True, vmem_limit_bytes=32 * 2**20
        ),
        cost_estimate=pl.CostEstimate(
            flops=60 * 10**9, bytes_accessed=count * width * 16, transcendentals=0
        ),
    )(rows.reshape((dp_count,) + slab), slab_y)
    return out_x.reshape(count, width), out_y.reshape(-1, width)


def scatter_rows_kernel(
    x_ref, out_ref, pair_in, pair_sum, plane_in, pair_sems, plane_sems
):
    chips, chip, core, depth = place_of()
    other = 1 - core
    sibling = (chip * 2 + other, depth)
    chip_at = [lax.rem(chip + k, chips) for k in range(chips)]
    flat = [(chip_at[k] * 2 + core, depth) for k in range(chips)]
    greet([sibling] + flat[1:])
    order = list(range(1, chips)) + [0]
    pair_copies, plane_copies = {}, {}
    for k in order:
        pair_copies[k] = send_to(
            x_ref.at[chip_at[k] * 2 + other],
            pair_in.at[k],
            pair_sems.at[0, k],
            pair_sems.at[1, k],
            sibling,
        )
        pair_copies[k].start()
    for k in order:
        pair_copies[k].wait_recv()
        pair_sum[k] = x_ref[chip_at[k] * 2 + core] + pair_in[k]
        if k:
            plane_copies[k] = send_to(
                pair_sum.at[k], plane_in.at[k], plane_sems.at[0, k], plane_sems.at[1, k], flat[k]
            )
            plane_copies[k].start()
    value = pair_sum[0]
    for k in range(1, chips):
        plane_copies[k].wait_recv()
        value = value + plane_in[k]
    out_ref[...] = value
    for copies in (pair_copies, plane_copies):
        for copy in copies.values():
            copy.wait_send()


def pad_rows(rows, unit):
    have, width = rows.shape
    padded = -(-have // unit) * unit
    if padded == have:
        return rows
    return jnp.concatenate([rows, jnp.zeros((padded - have, width), rows.dtype)], axis=0)


def scatter_rows(rows, collective):
    dp_count = lax.axis_size("dp")
    chips = dp_count // 2
    slab = (rows.shape[0] // dp_count, rows.shape[1])
    return pl.pallas_call(
        scatter_rows_kernel,
        out_shape=jax.ShapeDtypeStruct(slab, jnp.float32),
        in_specs=[whole_vmem()],
        out_specs=whole_vmem(),
        scratch_shapes=[
            pltpu.VMEM((chips,) + slab, jnp.float32),
            pltpu.VMEM((chips,) + slab, jnp.float32),
            pltpu.VMEM((chips,) + slab, jnp.float32),
            pltpu.SemaphoreType.DMA((2, chips)),
            pltpu.SemaphoreType.DMA((2, chips)),
        ],
        compiler_params=pltpu.CompilerParams(
            collective_id=collective, has_side_effects=True, vmem_limit_bytes=32 * 2**20
        ),
        cost_estimate=pl.CostEstimate(
            flops=rows.shape[0] * 15 * 10**6,
            bytes_accessed=rows.shape[0] * rows.shape[1] * 4,
            transcendentals=0,
        ),
    )(rows.reshape((dp_count,) + slab))


def start_spread(src, out_ref, sems, flat, rank):
    copies = {}
    for k in range(1, len(flat)):
        copies[k] = send_to(src, out_ref.at[rank], sems.at[0, k], sems.at[1, k], flat[k])
        copies[k].start()
    return copies


def start_share(out_ref, spread_copies, sems, place, sibling):
    chips, chip, core = place
    copies = {}
    for k in range(chips):
        if k:
            spread_copies[k].wait_recv()
        held = lax.rem(chip + chips - k, chips) * 2 + core
        copies[k] = send_to(
            out_ref.at[held], out_ref.at[held], sems.at[0, k], sems.at[1, k], sibling
        )
        copies[k].start()
    return copies


def spread_and_line_kernel(
    x_ref, y_ref, x_out, y_out, line_in, line_sems, spread_sems, share_sems
):
    chips, chip, core, depth = place_of()
    depths = lax.axis_size("tensor")
    rank = chip * 2 + core
    sibling = (chip * 2 + 1 - core, depth)
    flat = [(lax.rem(chip + k, chips) * 2 + core, depth) for k in range(chips)]
    deep = [(rank, lax.rem(depth + k, depths)) for k in range(depths)]
    greet([sibling] + flat[1:] + deep[1:])
    part = y_ref.shape[0] // depths
    part_of = [
        pl.ds(pl.multiple_of(lax.rem(depth + k, depths) * part, 8), part) for k in range(depths)
    ]
    firsts, seconds = {}, {}
    for k in range(1, depths):
        firsts[k] = send_to(
            y_ref.at[part_of[k]], line_in.at[k], line_sems.at[0, k], line_sems.at[1, k], deep[k]
        )
        firsts[k].start()
    spread_copies = start_spread(x_ref, x_out, spread_sems, flat, rank)
    x_out[rank] = x_ref[...]
    value = y_ref[part_of[0]]
    for k in range(1, depths):
        firsts[k].wait_recv()
        value = value + line_in[k]
    y_out[part_of[0]] = value
    for k in range(1, depths):
        seconds[k] = send_to(
            y_out.at[part_of[0]],
            y_out.at[part_of[0]],
            line_sems.at[2, k],
            line_sems.at[3, k],
            deep[k],
        )
        seconds[k].start()
    share_copies = start_share(x_out, spread_copies, share_sems, (chips, chip, core), sibling)
    for k in range(1, depths):
        seconds[k].wait_recv()
    for k in range(chips):
        share_copies[k].wait_recv()
    for copies in (firsts, seconds, spread_copies, share_copies):
        for copy in copies.values():
            copy.wait_send()


def spread_and_line(slab, partial, collective):
    dp_count, depths = lax.axis_size("dp"), lax.axis_size("tensor")
    chips = dp_count // 2
    each, width = slab.shape
    full, total = pl.pallas_call(
        spread_and_line_kernel,
        out_shape=(
            jax.ShapeDtypeStruct((dp_count, each, width), jnp.float32),
            jax.ShapeDtypeStruct(partial.shape, jnp.float32),
        ),
        in_specs=[whole_vmem()] * 2,
        out_specs=(whole_vmem(), whole_vmem()),
        scratch_shapes=[
            pltpu.VMEM((depths, partial.shape[0] // depths, width), jnp.float32),
            pltpu.SemaphoreType.DMA((4, depths)),
            pltpu.SemaphoreType.DMA((2, chips)),
            pltpu.SemaphoreType.DMA((2, chips)),
        ],
        compiler_params=pltpu.CompilerParams(
            collective_id=collective, has_side_effects=True, vmem_limit_bytes=24 * 2**20
        ),
        cost_estimate=pl.CostEstimate(
            flops=35 * 10**9, bytes_accessed=dp_count * each * width * 4, transcendentals=0
        ),
    )(slab, partial)
    return full.reshape(dp_count * each, width), total


def line_gather_kernel(
    x_ref, out_ref, right_send, right_recv, left_send, left_recv
):
    rank = lax.axis_index("dp")
    depth = lax.axis_index("tensor")
    depths = lax.axis_size("tensor")
    last = depths - 1
    right, left = (rank, depth + 1), (rank, depth - 1)
    barrier = pltpu.get_barrier_semaphore()

    @pl.when(depth < last)
    def _():
        pl.semaphore_signal(barrier, inc=1, device_id=right, device_id_type=MESH_ID)

    @pl.when(depth > 0)
    def _():
        pl.semaphore_signal(barrier, inc=1, device_id=left, device_id_type=MESH_ID)

    @pl.when((depth > 0) & (depth < last))
    def _():
        pl.semaphore_wait(barrier, 2)

    @pl.when((depth == 0) | (depth == last))
    def _():
        pl.semaphore_wait(barrier, 1)

    def to_right(step):
        src = x_ref if step == 0 else out_ref.at[depth - step]
        return send_to(
            src, out_ref.at[depth - step], right_send.at[step], right_recv.at[step], right
        )

    def to_left(step):
        src = x_ref if step == 0 else out_ref.at[depth + step]
        return send_to(src, out_ref.at[depth + step], left_send.at[step], left_recv.at[step], left)

    for step in range(last):

        @pl.when((depth < last) & (depth >= step))
        def _():
            to_right(step).start()

        @pl.when((depth > 0) & (depth + step <= last))
        def _():
            to_left(step).start()

        if step == 0:
            out_ref[depth] = x_ref[...]

        @pl.when(depth - 1 >= step)
        def _():
            send_to(
                x_ref,
                out_ref.at[depth - 1 - step],
                right_send.at[step],
                right_recv.at[step],
                left,
            ).wait_recv()

        @pl.when(depth + 1 + step <= last)
        def _():
            send_to(
                x_ref, out_ref.at[depth + 1 + step], left_send.at[step], left_recv.at[step], right
            ).wait_recv()

    for step in range(last):

        @pl.when((depth < last) & (depth >= step))
        def _():
            to_right(step).wait_send()

        @pl.when((depth > 0) & (depth + step <= last))
        def _():
            to_left(step).wait_send()


def line_gather(block, collective):
    depths = lax.axis_size("tensor")
    rows, width = block.shape
    out = pl.pallas_call(
        line_gather_kernel,
        out_shape=jax.ShapeDtypeStruct((depths, rows, width), block.dtype),
        in_specs=[whole_vmem()],
        out_specs=whole_vmem(),
        scratch_shapes=[pltpu.SemaphoreType.DMA((depths,))] * 4,
        compiler_params=pltpu.CompilerParams(
            collective_id=collective, has_side_effects=True, vmem_limit_bytes=16 * 2**20
        ),
        cost_estimate=pl.CostEstimate(
            flops=25 * 10**9, bytes_accessed=depths * rows * width * 4, transcendentals=0
        ),
    )(block)
    return out.reshape(depths * rows, width)


NBLK = 256


def split_store(value, high_ref, low_ref, rows, cols):
    high = value.astype(jnp.bfloat16)
    high_ref[rows, cols] = high
    low_ref[rows, cols] = (value - high.astype(jnp.float32)).astype(jnp.bfloat16)


def polynomial_kernel(gram_ref, out_ref, full_g, full_h, full_m, *pairs):
    gram_pair, half_pair, poly_pair, prod_pair = (
        pairs[0:2], pairs[2:4], pairs[4:6], pairs[6:8]
    )
    size = gram_ref.shape[0]
    blocks = size // NBLK
    spans = [slice(i * NBLK, (i + 1) * NBLK) for i in range(blocks)]
    upper = [(i, j) for i in range(blocks) for j in range(i, blocks)]

    def eye(i, j):
        if i != j:
            return 0.0
        row = lax.broadcasted_iota(jnp.int32, (NBLK, NBLK), 0)
        col = lax.broadcasted_iota(jnp.int32, (NBLK, NBLK), 1)
        return jnp.where(row == col, 1.0, 0.0)

    def place(i, j, value, full, pair):
        if full is not None:
            full[spans[i], spans[j]] = value
        if pair is not None:
            split_store(value, *pair, spans[i], spans[j])
        if i != j:
            flip = value.T
            if full is not None:
                full[spans[j], spans[i]] = flip
            if pair is not None:
                split_store(flip, *pair, spans[j], spans[i])

    def product(left, right, i, j):
        return plain_dot(left[0][spans[i], :], right[0][:, spans[j]]) + (
            plain_dot(left[0][spans[i], :], right[1][:, spans[j]])
            + plain_dot(left[1][spans[i], :], right[0][:, spans[j]])
        )

    trace = 0.0
    for i in range(blocks):
        trace = trace + jnp.sum(gram_ref[spans[i], spans[i]] * eye(i, i))
    root = jnp.sqrt(jnp.full((1, 1), trace, jnp.float32)) + 1e-07
    inverse = 1.0 / root
    for i, j in upper:
        place(i, j, gram_ref[spans[i], spans[j]] * (inverse * inverse), full_g, gram_pair)

    def make_poly():
        for i, j in upper:
            value = NS_B * full_g[spans[i], spans[j]] + NS_C * product(gram_pair, gram_pair, i, j)
            place(i, j, value, None, poly_pair)

    def advance():
        for i, j in upper:
            value = NS_A * full_g[spans[i], spans[j]] + product(poly_pair, gram_pair, i, j)
            place(i, j, value, full_h, half_pair)
        for i, j in upper:
            value = NS_A * full_h[spans[i], spans[j]] + product(poly_pair, half_pair, i, j)
            place(i, j, value, full_g, gram_pair)

    make_poly()
    for i, j in upper:
        value = (
            poly_pair[0][spans[i], spans[j]].astype(jnp.float32)
            + poly_pair[1][spans[i], spans[j]].astype(jnp.float32)
            + NS_A * eye(i, j)
        )
        place(i, j, value, full_m, prod_pair)
    advance()

    def sweep(index, carry):
        make_poly()
        for i, j in upper:
            value = NS_A * full_m[spans[i], spans[j]] + product(poly_pair, prod_pair, i, j)
            place(i, j, value, full_h, None)
        for i in range(blocks):
            full_m[spans[i], :] = full_h[spans[i], :]
            split_store(full_h[spans[i], :], *prod_pair, spans[i], slice(None))
        advance()
        return carry

    lax.fori_loop(0, 3, sweep, 0)
    make_poly()
    for i, j in upper:
        value = NS_A * full_m[spans[i], spans[j]] + product(poly_pair, prod_pair, i, j)
        place(i, j, value * inverse, out_ref, None)


def orthogonal_factor(gram_mat):
    size = gram_mat.shape[0]
    return pl.pallas_call(
        polynomial_kernel,
        out_shape=jax.ShapeDtypeStruct((size, size), jnp.float32),
        in_specs=[whole_vmem()],
        out_specs=whole_vmem(),
        scratch_shapes=[pltpu.VMEM((size, size), jnp.float32)] * 3
        + [pltpu.VMEM((size, size), jnp.bfloat16)] * 8,
        compiler_params=pltpu.CompilerParams(vmem_limit_bytes=48 * 2**20),
        cost_estimate=pl.CostEstimate(
            flops=17 * 2 * 2 * size**3, bytes_accessed=8 * size * size, transcendentals=0
        ),
    )(gram_mat)


def contract_rows(left, right):
    return lax.dot_general(
        left, right, (((0,), (0,)), ((), ())), preferred_element_type=jnp.float32
    )


def contract_cols(left, right):
    return lax.dot_general(
        left, right, (((1,), (1,)), ((), ())), preferred_element_type=jnp.float32
    )


def body(
    teacher_in,
    student_in,
    resp_mask,
    replay,
    t_gains,
    t_shifts,
    t_qkv,
    t_out,
    t_fc,
    t_proj,
    s_norms,
    s_qkv,
    s_out,
    s_fc,
    s_proj,
    s_map,
    mom_qkv,
    mom_out,
    mom_fc,
    mom_proj,
    mom_map,
    adam_first,
    adam_second,
):
    groups = lax.axis_size("tensor")
    tensor_rank = lax.axis_index("tensor")
    row_count = student_in.shape[0]
    seq_count = replay.shape[0]
    total_rows = row_count * groups
    count_block = jnp.full((8, 128), jnp.sum(resp_mask), jnp.int32).astype(jnp.float32)
    count_val = sum_small(count_block, 0)[0, 0]
    tokens_all = lax.axis_size("dp") * seq_count * LEN
    factor = tokens_all / (2.0 * count_val)

    def teacher_gather(local_rows):
        return lax.all_gather(local_rows, "tensor", axis=0, tiled=True)

    def teacher_reduce(left, right):
        return lax.psum_scatter(
            jnp.dot(left, right, preferred_element_type=jnp.float32).astype(jnp.bfloat16),
            "tensor",
            scatter_dimension=0,
            tiled=True,
        ).astype(jnp.float32)

    def student_gather(local_rows):
        return lax.all_gather(local_rows, "tensor", axis=0, tiled=True)

    def student_reduce(left, right, right_dim):
        return lax.psum_scatter(
            lax.dot_general(
                left, right, (((1,), (right_dim,)), ((), ())), preferred_element_type=jnp.float32
            ).astype(jnp.bfloat16),
            "tensor",
            scatter_dimension=0,
            tiled=True,
        ).astype(jnp.float32)

    teacher_x = teacher_in.astype(jnp.float32)
    slot_width = t_qkv.shape[2]
    slot_count = slot_width // HEAD
    live_count = HT // groups + (tensor_rank < HT % groups).astype(jnp.int32)
    live_slots = (jnp.arange(slot_count, dtype=jnp.int32) < live_count).astype(jnp.float32)
    teacher_normed = norm_parts(teacher_x, t_gains[0], t_shifts[0])[0].astype(jnp.bfloat16)
    teacher_all = teacher_gather(teacher_normed)
    teacher_mixed = jnp.dot(
        teacher_all, t_qkv.reshape(DT, 3 * slot_width), preferred_element_type=jnp.float32
    ).astype(jnp.bfloat16)
    teacher_head_out = attend_forward(teacher_mixed, slot_count)[0]
    slot_mask = jnp.repeat(live_slots, HEAD)[None, :] > 0.0
    teacher_head_out = jnp.where(slot_mask, teacher_head_out, jnp.zeros_like(teacher_head_out))
    student_x = student_in.astype(jnp.float32)
    shard_width = s_qkv.shape[2]
    shard_hidden = s_fc.shape[1]
    head_count = shard_width // HEAD
    w_qkv = s_qkv.astype(jnp.bfloat16).reshape(DS, 3 * shard_width)
    w_out = s_out.astype(jnp.bfloat16)
    w_fc = s_fc.astype(jnp.bfloat16)
    w_proj = s_proj.astype(jnp.bfloat16)
    w_map = s_map.astype(jnp.bfloat16)
    normed_one, unit_one, scale_one = norm_parts(student_x, s_norms[0], s_norms[1])
    low_one = normed_one.astype(jnp.bfloat16)
    rows_one = line_gather(low_one, 5)
    mixed_qkv = jnp.dot(rows_one, w_qkv, preferred_element_type=jnp.float32).astype(jnp.bfloat16)
    head_out, log_sums = attend_forward(mixed_qkv, head_count)
    resid = student_x + student_reduce(head_out, w_out, 0)
    normed_two, unit_two, scale_two = norm_parts(resid, s_norms[2], s_norms[3])
    low_two = normed_two.astype(jnp.bfloat16)
    rows_two = line_gather(low_two, 6)
    attn_part = teacher_reduce(teacher_head_out, t_out)
    attn_part, rows_two = lax.optimization_barrier((attn_part, rows_two))
    teacher_resid = teacher_x + attn_part
    teacher_normed_two = norm_parts(teacher_resid, t_gains[1], t_shifts[1])[0].astype(jnp.bfloat16)
    teacher_hidden = smooth_gelu(
        jnp.dot(teacher_gather(teacher_normed_two), t_fc, preferred_element_type=jnp.float32)
    ).astype(jnp.bfloat16)
    teacher_out = (teacher_resid + teacher_reduce(teacher_hidden, t_proj)).astype(jnp.bfloat16)
    before = jnp.dot(rows_two, w_fc, preferred_element_type=jnp.float32)
    before, hidden = (before, smooth_gelu(before).astype(jnp.bfloat16))
    output = resid + student_reduce(hidden, w_proj, 0)
    student_out = output.astype(jnp.bfloat16)
    guess_vec = jnp.dot(student_out, w_map, preferred_element_type=jnp.float32)
    miss_vec = guess_vec - teacher_out.astype(jnp.float32)
    position = tensor_rank * row_count + jnp.arange(row_count, dtype=jnp.int32)
    seq_owner = position // LEN
    seq_pick = (seq_owner[:, None] == jnp.arange(seq_count, dtype=jnp.int32)[None, :]).astype(
        jnp.float32
    )
    flag_tok = jnp.sum(seq_pick * replay.astype(jnp.float32)[None, :], axis=1)
    weight = resp_mask.astype(jnp.float32) * (1.0 - REPLAY_CUT * flag_tok)
    loss_part = jnp.sum(weight[:, None] * miss_vec * miss_vec)
    grad_guess = (2.0 * factor * weight[:, None] * miss_vec).astype(jnp.bfloat16)
    row_unit = 8 * lax.axis_size("dp") * groups
    map_slab = scatter_rows(pad_rows(contract_rows(grad_guess, student_out), row_unit), 1)
    grad_output = contract_cols(grad_guess, w_map)
    rows_two_back, before_back, hidden_back = (rows_two, before, hidden)
    rows_one_back, mixed_back, heads_back, logs_back = (rows_one, mixed_qkv, head_out, log_sums)
    grad_mlp = student_gather(grad_output.astype(jnp.bfloat16))
    grad_mlp, map_slab = lax.optimization_barrier((grad_mlp, map_slab))
    grad_proj = contract_rows(hidden_back, grad_mlp)
    grad_hidden = contract_cols(grad_mlp, w_proj)
    gelu_vals, gelu_pull = jax.vjp(smooth_gelu, before_back)
    grad_before = gelu_pull(grad_hidden)[0].astype(jnp.bfloat16)
    grad_fc = contract_rows(rows_two_back, grad_before).reshape(-1, DS)
    mlp_slab = scatter_rows(jnp.concatenate([grad_proj, grad_fc], axis=0), 2)
    grad_normed_two = student_reduce(grad_before, w_fc, 1)
    grad_normed_two, mlp_slab = lax.optimization_barrier((grad_normed_two, mlp_slab))
    grad_resid = grad_output + norm_back(grad_normed_two, unit_two, scale_two, s_norms[2])
    grad_attn = student_gather(grad_resid.astype(jnp.bfloat16))
    grad_mlp_rows, map_slab = spread_and_line(mlp_slab, map_slab, 7)
    grad_attn, grad_mlp_rows, map_slab = lax.optimization_barrier(
        (grad_attn, grad_mlp_rows, map_slab)
    )
    grad_proj, grad_fc = grad_mlp_rows[:shard_hidden], grad_mlp_rows[shard_hidden:]
    grad_out = contract_rows(heads_back, grad_attn)
    grad_heads = contract_cols(grad_attn, w_out).astype(jnp.bfloat16)

    grad_mixed = attend_backward(mixed_back, logs_back, grad_heads, head_count)
    grad_qkv = contract_rows(grad_mixed, rows_one_back)
    grad_attn_rows, grad_map = sum_and_spread(
        jnp.concatenate([grad_out, grad_qkv], axis=0), map_slab, 3
    )
    grad_map = grad_map[:DT]
    grad_out, grad_qkv = grad_attn_rows[:shard_width], grad_attn_rows[shard_width:]
    grad_fc = grad_fc.reshape(DS, shard_hidden)
    grad_normed_one = student_reduce(grad_mixed, w_qkv, 1)
    grad_normed_one, grad_out, grad_qkv, grad_map = lax.optimization_barrier(
        (grad_normed_one, grad_out, grad_qkv, grad_map)
    )
    input_grad = grad_resid + norm_back(grad_normed_one, unit_one, scale_one, s_norms[0])
    norm_grads = jnp.stack(
        [
            jnp.sum(grad_normed_one * unit_one, axis=0),
            jnp.sum(grad_normed_one, axis=0),
            jnp.sum(grad_normed_two * unit_two, axis=0),
            jnp.sum(grad_normed_two, axis=0),
        ]
    )
    small = jnp.concatenate(
        [norm_grads, jnp.full((4, DS), loss_part, jnp.float32)], axis=0
    )
    small = sum_small(small, 4)
    norm_grads = small[:4]
    loss = small[4, 0] / (count_val * DT)

    def to_tall(mat):
        return mat.transpose(1, 2, 0).reshape(-1, DS)

    def from_tall(mat):
        return mat.reshape(3, shard_width, DS).transpose(2, 0, 1)

    moments = [
        MOMENTUM * to_tall(mom_qkv) + grad_qkv,
        MOMENTUM * mom_out + grad_out,
        MOMENTUM * mom_fc + grad_fc,
        MOMENTUM * mom_proj + grad_proj,
    ]
    moment_map = MOMENTUM * mom_map.T + grad_map
    dp_count = lax.axis_size("dp")
    dp_rank = lax.axis_index("dp")
    slice_rows = DS // dp_count
    first_row = dp_rank * slice_rows
    talls = [moments[0], moments[1], moments[2], moments[3], moment_map]
    sums = [0, 0, 1, 0, 0]

    def gram_rows(tall, axis):
        return lax.dot_general(
            lax.dynamic_slice_in_dim(tall, first_row, slice_rows, 1 - axis),
            tall,
            (((axis,), (axis,)), ((), ())),
            precision=HIGH,
            preferred_element_type=jnp.float32,
        )

    parts = jnp.concatenate([gram_rows(talls[i], sums[i]) for i in range(4)], axis=0)
    own_rows = lax.psum_scatter(parts, "tensor", scatter_dimension=0, tiled=True)
    both_rows = jnp.concatenate([own_rows[None], gram_rows(talls[4], sums[4])[None]], axis=0)
    both_rows = lax.all_gather(both_rows, "dp", axis=1, tiled=True)
    mine = dp_rank % 2
    factor_mat = orthogonal_factor(jnp.where(mine == 0, both_rows[0], both_rows[1]))
    pair_rows = lax.dynamic_slice_in_dim(factor_mat, (dp_rank // 2) * 2 * slice_rows, 2 * slice_rows, 0)
    other_rows = lax.ppermute(
        pair_rows, "dp", [(i, i ^ 1) for i in range(dp_count)]
    )
    even_rows = jnp.where(mine == 0, pair_rows, other_rows)
    odd_rows = jnp.where(mine == 0, other_rows, pair_rows)
    even_rows = lax.dynamic_slice_in_dim(even_rows, mine * slice_rows, slice_rows, 0)
    odd_rows = lax.dynamic_slice_in_dim(odd_rows, mine * slice_rows, slice_rows, 0)
    factor_rows = lax.all_gather(even_rows, "tensor", axis=0)
    pieces = [
        lax.dot_general(
            factor_rows[i] if i < 4 else odd_rows,
            talls[i],
            (((1,), (1 - sums[i],)), ((), ())),
            precision=lax.Precision.HIGH,
            preferred_element_type=jnp.float32,
        ).astype(jnp.bfloat16)
        for i in range(5)
    ]
    widths = [piece.shape[1] for piece in pieces]
    iterate_all = lax.all_gather(jnp.concatenate(pieces, axis=1), "dp", axis=0, tiled=True)
    iterates = []
    offset = 0
    for index, width in enumerate(widths):
        piece = iterate_all[:, offset : offset + width]
        iterates.append(piece if index == 2 else piece.T)
        offset += width
    iterates = [
        piece.astype(jnp.float32) for piece in lax.optimization_barrier(tuple(iterates))
    ]
    keep_rate = 1.0 - MUON_RATE * MUON_DECAY
    weight_qkv = keep_rate * to_tall(s_qkv) - MUON_RATE * math.sqrt(3.0) * iterates[0]
    weight_out = keep_rate * s_out - MUON_RATE * iterates[1]
    weight_fc = keep_rate * s_fc - MUON_RATE * math.sqrt(FS / DS) * iterates[2]
    weight_proj = keep_rate * s_proj - MUON_RATE * iterates[3]
    weight_map = keep_rate * s_map.T - MUON_RATE * math.sqrt(DT / DS) * iterates[4]
    norm_first = BETA_ONE * adam_first + (1.0 - BETA_ONE) * norm_grads
    norm_second = BETA_TWO * adam_second + (1.0 - BETA_TWO) * norm_grads * norm_grads
    fix_one = 1.0 - BETA_ONE**STEP
    fix_two = 1.0 - BETA_TWO**STEP
    norm_values = s_norms - ADAM_RATE * (
        norm_first / fix_one / (jnp.sqrt(norm_second / fix_two) + ADAM_EPS) + ADAM_DECAY * s_norms
    )
    return (
        teacher_out,
        student_out,
        input_grad,
        loss,
        from_tall(grad_qkv),
        grad_out,
        grad_fc,
        grad_proj,
        grad_map.T,
        from_tall(moments[0]),
        moments[1],
        moments[2],
        moments[3],
        moment_map.T,
        from_tall(weight_qkv),
        weight_out,
        weight_fc,
        weight_proj,
        weight_map.T,
        norm_first,
        norm_second,
        norm_values,
    )


def solution(mesh):
    return jax.shard_map(
        body,
        mesh=mesh,
        in_specs=(
            P(("dp", "tensor"), None),
            P(("dp", "tensor"), None),
            P(("dp", "tensor")),
            P("dp"),
            P(),
            P(),
            P(None, None, "tensor"),
            P("tensor", None),
            P(None, "tensor"),
            P("tensor", None),
            P(),
            P(None, None, "tensor"),
            P("tensor", None),
            P(None, "tensor"),
            P("tensor", None),
            P(),
            P(None, None, "tensor"),
            P("tensor", None),
            P(None, "tensor"),
            P("tensor", None),
            P(),
            P(),
            P(),
        ),
        out_specs=(
            P(("dp", "tensor"), None),
            P(("dp", "tensor"), None),
            P(("dp", "tensor"), None),
            P(),
            P(None, None, "tensor"),
            P("tensor", None),
            P(None, "tensor"),
            P("tensor", None),
            P(),
            P(None, None, "tensor"),
            P("tensor", None),
            P(None, "tensor"),
            P("tensor", None),
            P(),
            P(None, None, "tensor"),
            P("tensor", None),
            P(None, "tensor"),
            P("tensor", None),
            P(),
            P(),
            P(),
            P(),
        ),
        check_vma=False,
    )
```

```python
import functools
import math

import jax
import jax.numpy as jnp
from jax import lax
from jax.experimental import pallas as pl
from jax.experimental.pallas import tpu as pltpu
from jax.sharding import PartitionSpec as P

DT = 1600
HT = 25
DS = 768
FS = 3072
HEAD = 64
LEN = 1024
STEP = 10
ABLK = 256


EPS = 1e-05
NS_A = 3.4445
NS_B = -4.775
NS_C = 2.0315
MOMENTUM = 0.95
MUON_RATE = 0.5
MUON_DECAY = 0.01
ADAM_RATE = 0.3
BETA_ONE = 0.9
BETA_TWO = 0.999
ADAM_EPS = 1e-08
ADAM_DECAY = 0.01
REPLAY_CUT = 0.5
NEG_FILL = -1e30
HIGH = lax.Precision.HIGHEST


def norm_parts(v, gain_vec, shift_vec):
    row_mean = jnp.mean(v, axis=-1, keepdims=True)
    centred = v - row_mean
    row_var = jnp.mean(centred * centred, axis=-1, keepdims=True)
    inv_scale = lax.rsqrt(row_var + EPS)
    unit_val = centred * inv_scale
    return (unit_val * gain_vec + shift_vec, unit_val, inv_scale)


def norm_back(grad_norm, unit_val, inv_scale, gain_vec):
    grad_unit = grad_norm * gain_vec
    first_mean = jnp.mean(grad_unit, axis=-1, keepdims=True)
    second_mean = jnp.mean(grad_unit * unit_val, axis=-1, keepdims=True)
    return inv_scale * (grad_unit - first_mean - unit_val * second_mean)


def smooth_gelu(v):
    return 0.5 * v * (1.0 + jnp.tanh(0.7978845608028654 * (v + 0.044715 * v * v * v)))


def whole_vmem():
    return pl.BlockSpec(memory_space=pltpu.VMEM)


def nt_dot(left, right):
    return lax.dot_general(
        left, right, (((1,), (1,)), ((), ())), preferred_element_type=jnp.float32
    )


def tn_dot(left, right):
    return lax.dot_general(
        left, right, (((0,), (0,)), ((), ())), preferred_element_type=jnp.float32
    )


def plain_dot(left, right):
    return jnp.dot(left, right, preferred_element_type=jnp.float32)


def lower_mask():
    row_pos = lax.broadcasted_iota(jnp.int32, (ABLK, ABLK), 0)
    key_pos = lax.broadcasted_iota(jnp.int32, (ABLK, ABLK), 1)
    return key_pos <= row_pos


def attend_forward_kernel(head_count, qkv_ref, out_ref, log_ref):
    width = head_count * HEAD
    for head in range(head_count):
        cols = slice(head * HEAD, (head + 1) * HEAD)
        keys = qkv_ref[:, width + head * HEAD : width + (head + 1) * HEAD]
        values = qkv_ref[:, 2 * width + head * HEAD : 2 * width + (head + 1) * HEAD]
        for block in range(LEN // ABLK):
            low, high = block * ABLK, (block + 1) * ABLK
            query = qkv_ref[low:high, cols]
            near = nt_dot(query, keys[low:high]) * HEAD ** (-0.5)
            near = jnp.where(lower_mask(), near, NEG_FILL)
            row_top = jnp.max(near, axis=-1, keepdims=True)
            if block:
                far = nt_dot(query, keys[:low]) * HEAD ** (-0.5)
                row_top = jnp.maximum(row_top, jnp.max(far, axis=-1, keepdims=True))
            near = jnp.exp(near - row_top)
            row_total = jnp.sum(near, axis=-1, keepdims=True)
            if block:
                far = jnp.exp(far - row_top)
                row_total = row_total + jnp.sum(far, axis=-1, keepdims=True)
            inverse = 1.0 / row_total
            mixed = plain_dot((near * inverse).astype(jnp.bfloat16), values[low:high])
            if block:
                mixed = mixed + plain_dot((far * inverse).astype(jnp.bfloat16), values[:low])
            out_ref[low:high, cols] = mixed.astype(out_ref.dtype)
            log_ref[low:high, head : head + 1] = row_top + jnp.log(row_total)


def attend_forward(mixed_qkv, head_count):
    width = head_count * HEAD
    return pl.pallas_call(
        functools.partial(attend_forward_kernel, head_count),
        out_shape=(
            jax.ShapeDtypeStruct((LEN, width), jnp.bfloat16),
            jax.ShapeDtypeStruct((LEN, 128), jnp.float32),
        ),
        in_specs=[whole_vmem()],
        out_specs=(whole_vmem(), whole_vmem()),
        compiler_params=pltpu.CompilerParams(vmem_limit_bytes=40 * 2**20),
        cost_estimate=pl.CostEstimate(
            flops=4 * head_count * LEN * LEN * HEAD * 4,
            bytes_accessed=LEN * width * 8,
            transcendentals=head_count * LEN * LEN // 2,
        ),
    )(mixed_qkv)


def attend_backward_kernel(
    head_count, qkv_ref, log_ref, grad_ref, out_ref, key_acc, value_acc
):
    width = head_count * HEAD
    scale = HEAD ** (-0.5)
    for head in range(head_count):
        cols = slice(head * HEAD, (head + 1) * HEAD)
        key_cols = slice(width + head * HEAD, width + (head + 1) * HEAD)
        value_cols = slice(2 * width + head * HEAD, 2 * width + (head + 1) * HEAD)
        keys = qkv_ref[:, key_cols]
        values = qkv_ref[:, value_cols]
        for block in range(LEN // ABLK - 1, -1, -1):
            low, high = block * ABLK, (block + 1) * ABLK
            query = qkv_ref[low:high, cols]
            grad = grad_ref[low:high, cols]
            log_sum = log_ref[low:high, head : head + 1]
            near = nt_dot(query, keys[low:high]) * scale
            near = jnp.exp(jnp.where(lower_mask(), near, NEG_FILL) - log_sum)
            near_back = nt_dot(grad, values[low:high])
            inner = jnp.sum(near * near_back, axis=-1, keepdims=True)
            if block:
                far = jnp.exp(nt_dot(query, keys[:low]) * scale - log_sum)
                far_back = nt_dot(grad, values[:low])
                inner = inner + jnp.sum(far * far_back, axis=-1, keepdims=True)
            near_score = (near * (near_back - inner)).astype(jnp.bfloat16)
            grad_query = plain_dot(near_score, keys[low:high])
            near_key = tn_dot(near_score, query)
            near_value = tn_dot(near.astype(jnp.bfloat16), grad)
            if block == LEN // ABLK - 1:
                key_acc[low:high, :] = near_key
                value_acc[low:high, :] = near_value
            else:
                key_acc[low:high, :] += near_key
                value_acc[low:high, :] += near_value
            if block:
                far_score = (far * (far_back - inner)).astype(jnp.bfloat16)
                grad_query = grad_query + plain_dot(far_score, keys[:low])
                far_key = tn_dot(far_score, query)
                far_value = tn_dot(far.astype(jnp.bfloat16), grad)
                if block == LEN // ABLK - 1:
                    key_acc[:low, :] = far_key
                    value_acc[:low, :] = far_value
                else:
                    key_acc[:low, :] += far_key
                    value_acc[:low, :] += far_value
            out_ref[low:high, cols] = (grad_query * scale).astype(jnp.bfloat16)
        out_ref[:, key_cols] = (key_acc[...] * scale).astype(jnp.bfloat16)
        out_ref[:, value_cols] = value_acc[...].astype(jnp.bfloat16)


def attend_backward(mixed_qkv, log_sums, grad_heads, head_count):
    width = head_count * HEAD
    return pl.pallas_call(
        functools.partial(attend_backward_kernel, head_count),
        out_shape=jax.ShapeDtypeStruct((LEN, 3 * width), jnp.bfloat16),
        in_specs=[whole_vmem()] * 3,
        out_specs=whole_vmem(),
        scratch_shapes=[pltpu.VMEM((LEN, HEAD), jnp.float32)] * 2,
        compiler_params=pltpu.CompilerParams(vmem_limit_bytes=40 * 2**20),
        cost_estimate=pl.CostEstimate(
            flops=10 * head_count * LEN * LEN * HEAD * 4,
            bytes_accessed=LEN * width * 16,
            transcendentals=head_count * LEN * LEN // 2,
        ),
    )(mixed_qkv, log_sums, grad_heads)


MESH_ID = pl.DeviceIdType.MESH


def place_of():
    dp_count = lax.axis_size("dp")
    rank = lax.axis_index("dp")
    return dp_count // 2, rank // 2, rank % 2, lax.axis_index("tensor")


def greet(peers):
    barrier = pltpu.get_barrier_semaphore()
    for peer in peers:
        pl.semaphore_signal(barrier, inc=1, device_id=peer, device_id_type=MESH_ID)
    pl.semaphore_wait(barrier, len(peers))


def send_to(src, dst, send_sem, recv_sem, peer):
    return pltpu.make_async_remote_copy(
        src_ref=src,
        dst_ref=dst,
        send_sem=send_sem,
        recv_sem=recv_sem,
        device_id=peer,
        device_id_type=MESH_ID,
    )


def sum_small_kernel(
    x_ref, out_ref, pair, plane, line, pair_sems, plane_sems, line_sems
):
    chips, chip, core, depth = place_of()
    depths = lax.axis_size("tensor")
    sibling = (chip * 2 + 1 - core, depth)
    flat = [((lax.rem(chip + k, chips)) * 2 + core, depth) for k in range(1, chips)]
    deep = [(chip * 2 + core, lax.rem(depth + k, depths)) for k in range(1, depths)]
    greet([sibling] + flat + deep)
    copy = send_to(x_ref, pair, pair_sems.at[0], pair_sems.at[1], sibling)
    copy.start()
    copy.wait()
    plane[chip] = x_ref[...] + pair[...]
    copies = []
    for k in range(1, chips):
        copies.append(
            send_to(
                plane.at[chip], plane.at[chip], plane_sems.at[0, k], plane_sems.at[1, k], flat[k - 1]
            )
        )
    for copy in copies:
        copy.start()
    for copy in copies:
        copy.wait()
    total = plane[0]
    for k in range(1, chips):
        total = total + plane[k]
    line[depth] = total
    copies = []
    for k in range(1, depths):
        copies.append(
            send_to(
                line.at[depth], line.at[depth], line_sems.at[0, k], line_sems.at[1, k], deep[k - 1]
            )
        )
    for copy in copies:
        copy.start()
    for copy in copies:
        copy.wait()
    total = line[0]
    for k in range(1, depths):
        total = total + line[k]
    out_ref[...] = total


def sum_small(block, collective):
    chips, depths = lax.axis_size("dp") // 2, lax.axis_size("tensor")
    return pl.pallas_call(
        sum_small_kernel,
        out_shape=jax.ShapeDtypeStruct(block.shape, jnp.float32),
        in_specs=[whole_vmem()],
        out_specs=whole_vmem(),
        scratch_shapes=[
            pltpu.VMEM(block.shape, jnp.float32),
            pltpu.VMEM((chips,) + block.shape, jnp.float32),
            pltpu.VMEM((depths,) + block.shape, jnp.float32),
            pltpu.SemaphoreType.DMA((2,)),
            pltpu.SemaphoreType.DMA((2, chips)),
            pltpu.SemaphoreType.DMA((2, depths)),
        ],
        compiler_params=pltpu.CompilerParams(
            collective_id=collective, has_side_effects=True, vmem_limit_bytes=16 * 2**20
        ),
        cost_estimate=pl.CostEstimate(flops=10**10, bytes_accessed=10**6, transcendentals=0),
    )(block)


def sum_and_spread_kernel(
    x_ref,
    y_ref,
    x_out,
    y_out,
    pair_in,
    pair_sum,
    plane_in,
    total,
    line_in,
    line_out,
    pair_sems,
    plane_sems,
    line_sems,
    spread_sems,
    share_sems,
):
    chips, chip, core, depth = place_of()
    depths = lax.axis_size("tensor")
    rank = chip * 2 + core
    other = 1 - core
    sibling = (chip * 2 + other, depth)
    chip_at = [lax.rem(chip + k, chips) for k in range(chips)]
    flat = [(chip_at[k] * 2 + core, depth) for k in range(chips)]
    deep = [(rank, lax.rem(depth + k, depths)) for k in range(depths)]
    greet([sibling] + flat[1:] + deep[1:])
    part = y_ref.shape[0] // depths
    part_of = [
        pl.ds(pl.multiple_of(lax.rem(depth + k, depths) * part, 8), part) for k in range(depths)
    ]
    firsts, seconds = {}, {}
    for k in range(1, depths):
        firsts[k] = send_to(
            y_ref.at[part_of[k]], line_in.at[k], line_sems.at[0, k], line_sems.at[1, k], deep[k]
        )
        firsts[k].start()
    order = list(range(1, chips)) + [0]
    pair_copies, plane_copies = {}, {}
    for k in order:
        pair_copies[k] = send_to(
            x_ref.at[chip_at[k] * 2 + other],
            pair_in.at[k],
            pair_sems.at[0, k],
            pair_sems.at[1, k],
            sibling,
        )
        pair_copies[k].start()
    for k in order:
        pair_copies[k].wait_recv()
        pair_sum[k] = x_ref[chip_at[k] * 2 + core] + pair_in[k]
        if k:
            plane_copies[k] = send_to(
                pair_sum.at[k], plane_in.at[k], plane_sems.at[0, k], plane_sems.at[1, k], flat[k]
            )
            plane_copies[k].start()
    value = y_ref[part_of[0]]
    for k in range(1, depths):
        firsts[k].wait_recv()
        value = value + line_in[k]
    line_out[part_of[0]] = value
    for k in range(1, depths):
        seconds[k] = send_to(
            line_out.at[part_of[0]],
            line_out.at[part_of[0]],
            line_sems.at[2, k],
            line_sems.at[3, k],
            deep[k],
        )
        seconds[k].start()
    value = pair_sum[0]
    for k in range(1, chips):
        plane_copies[k].wait_recv()
        value = value + plane_in[k]
    total[...] = value
    x_spread = start_spread(total, x_out, spread_sems.at[1], flat, rank)
    x_out[rank] = value
    for k in range(1, depths):
        seconds[k].wait_recv()
    y_spread = start_spread(line_out, y_out, spread_sems.at[0], flat, rank)
    y_out[rank] = line_out[...]
    x_share = start_share(x_out, x_spread, share_sems.at[1], (chips, chip, core), sibling)
    y_share = start_share(y_out, y_spread, share_sems.at[0], (chips, chip, core), sibling)
    for k in range(chips):
        y_share[k].wait_recv()
        x_share[k].wait_recv()
    for copies in (
        pair_copies,
        plane_copies,
        firsts,
        seconds,
        y_spread,
        x_spread,
        y_share,
        x_share,
    ):
        for copy in copies.values():
            copy.wait_send()


def sum_and_spread(rows, slab_y, collective):
    dp_count, depths = lax.axis_size("dp"), lax.axis_size("tensor")
    chips = dp_count // 2
    count, width = rows.shape
    slab = (count // dp_count, width)
    out_x, out_y = pl.pallas_call(
        sum_and_spread_kernel,
        out_shape=(
            jax.ShapeDtypeStruct((dp_count,) + slab, jnp.float32),
            jax.ShapeDtypeStruct((dp_count,) + slab_y.shape, jnp.float32),
        ),
        in_specs=[whole_vmem()] * 2,
        out_specs=(whole_vmem(), whole_vmem()),
        scratch_shapes=[
            pltpu.VMEM((chips,) + slab, jnp.float32),
            pltpu.VMEM((chips,) + slab, jnp.float32),
            pltpu.VMEM((chips,) + slab, jnp.float32),
            pltpu.VMEM(slab, jnp.float32),
            pltpu.VMEM((depths, slab_y.shape[0] // depths, width), jnp.float32),
            pltpu.VMEM(slab_y.shape, jnp.float32),
            pltpu.SemaphoreType.DMA((2, chips)),
            pltpu.SemaphoreType.DMA((2, chips)),
            pltpu.SemaphoreType.DMA((4, depths)),
            pltpu.SemaphoreType.DMA((2, 2, chips)),
            pltpu.SemaphoreType.DMA((2, 2, chips)),
        ],
        compiler_params=pltpu.CompilerParams(
            collective_id=collective, has_side_effects=True, vmem_limit_bytes=32 * 2**20
        ),
        cost_estimate=pl.CostEstimate(
            flops=60 * 10**9, bytes_accessed=count * width * 16, transcendentals=0
        ),
    )(rows.reshape((dp_count,) + slab), slab_y)
    return out_x.reshape(count, width), out_y.reshape(-1, width)


def scatter_rows_kernel(
    x_ref, out_ref, pair_in, pair_sum, plane_in, pair_sems, plane_sems
):
    chips, chip, core, depth = place_of()
    other = 1 - core
    sibling = (chip * 2 + other, depth)
    chip_at = [lax.rem(chip + k, chips) for k in range(chips)]
    flat = [(chip_at[k] * 2 + core, depth) for k in range(chips)]
    greet([sibling] + flat[1:])
    order = list(range(1, chips)) + [0]
    pair_copies, plane_copies = {}, {}
    for k in order:
        pair_copies[k] = send_to(
            x_ref.at[chip_at[k] * 2 + other],
            pair_in.at[k],
            pair_sems.at[0, k],
            pair_sems.at[1, k],
            sibling,
        )
        pair_copies[k].start()
    for k in order:
        pair_copies[k].wait_recv()
        pair_sum[k] = x_ref[chip_at[k] * 2 + core] + pair_in[k]
        if k:
            plane_copies[k] = send_to(
                pair_sum.at[k], plane_in.at[k], plane_sems.at[0, k], plane_sems.at[1, k], flat[k]
            )
            plane_copies[k].start()
    value = pair_sum[0]
    for k in range(1, chips):
        plane_copies[k].wait_recv()
        value = value + plane_in[k]
    out_ref[...] = value
    for copies in (pair_copies, plane_copies):
        for copy in copies.values():
            copy.wait_send()


def pad_rows(rows, unit):
    have, width = rows.shape
    padded = -(-have // unit) * unit
    if padded == have:
        return rows
    return jnp.concatenate([rows, jnp.zeros((padded - have, width), rows.dtype)], axis=0)


def scatter_rows(rows, collective):
    dp_count = lax.axis_size("dp")
    chips = dp_count // 2
    slab = (rows.shape[0] // dp_count, rows.shape[1])
    return pl.pallas_call(
        scatter_rows_kernel,
        out_shape=jax.ShapeDtypeStruct(slab, jnp.float32),
        in_specs=[whole_vmem()],
        out_specs=whole_vmem(),
        scratch_shapes=[
            pltpu.VMEM((chips,) + slab, jnp.float32),
            pltpu.VMEM((chips,) + slab, jnp.float32),
            pltpu.VMEM((chips,) + slab, jnp.float32),
            pltpu.SemaphoreType.DMA((2, chips)),
            pltpu.SemaphoreType.DMA((2, chips)),
        ],
        compiler_params=pltpu.CompilerParams(
            collective_id=collective, has_side_effects=True, vmem_limit_bytes=32 * 2**20
        ),
        cost_estimate=pl.CostEstimate(
            flops=rows.shape[0] * 15 * 10**6,
            bytes_accessed=rows.shape[0] * rows.shape[1] * 4,
            transcendentals=0,
        ),
    )(rows.reshape((dp_count,) + slab))


def start_spread(src, out_ref, sems, flat, rank):
    copies = {}
    for k in range(1, len(flat)):
        copies[k] = send_to(src, out_ref.at[rank], sems.at[0, k], sems.at[1, k], flat[k])
        copies[k].start()
    return copies


def start_share(out_ref, spread_copies, sems, place, sibling):
    chips, chip, core = place
    copies = {}
    for k in range(chips):
        if k:
            spread_copies[k].wait_recv()
        held = lax.rem(chip + chips - k, chips) * 2 + core
        copies[k] = send_to(
            out_ref.at[held], out_ref.at[held], sems.at[0, k], sems.at[1, k], sibling
        )
        copies[k].start()
    return copies


def spread_kernel(x_ref, out_ref, spread_sems, share_sems):
    chips, chip, core, depth = place_of()
    rank = chip * 2 + core
    sibling = (chip * 2 + 1 - core, depth)
    flat = [(lax.rem(chip + k, chips) * 2 + core, depth) for k in range(chips)]
    greet([sibling] + flat[1:])
    spread_copies = start_spread(x_ref, out_ref, spread_sems, flat, rank)
    out_ref[rank] = x_ref[...]
    share_copies = start_share(out_ref, spread_copies, share_sems, (chips, chip, core), sibling)
    for k in range(chips):
        share_copies[k].wait_recv()
    for copies in (spread_copies, share_copies):
        for copy in copies.values():
            copy.wait_send()


def spread(slab, collective):
    dp_count = lax.axis_size("dp")
    chips = dp_count // 2
    each, width = slab.shape
    full = pl.pallas_call(
        spread_kernel,
        out_shape=jax.ShapeDtypeStruct((dp_count, each, width), slab.dtype),
        in_specs=[whole_vmem()],
        out_specs=whole_vmem(),
        scratch_shapes=[
            pltpu.SemaphoreType.DMA((2, chips)),
            pltpu.SemaphoreType.DMA((2, chips)),
        ],
        compiler_params=pltpu.CompilerParams(
            collective_id=collective, has_side_effects=True, vmem_limit_bytes=16 * 2**20
        ),
        cost_estimate=pl.CostEstimate(
            flops=35 * 10**9, bytes_accessed=dp_count * each * width * 4, transcendentals=0
        ),
    )(slab)
    return full.reshape(dp_count * each, width)


def line_gather_kernel(
    x_ref, out_ref, right_send, right_recv, left_send, left_recv
):
    rank = lax.axis_index("dp")
    depth = lax.axis_index("tensor")
    depths = lax.axis_size("tensor")
    last = depths - 1
    right, left = (rank, depth + 1), (rank, depth - 1)
    barrier = pltpu.get_barrier_semaphore()

    @pl.when(depth < last)
    def _():
        pl.semaphore_signal(barrier, inc=1, device_id=right, device_id_type=MESH_ID)

    @pl.when(depth > 0)
    def _():
        pl.semaphore_signal(barrier, inc=1, device_id=left, device_id_type=MESH_ID)

    @pl.when((depth > 0) & (depth < last))
    def _():
        pl.semaphore_wait(barrier, 2)

    @pl.when((depth == 0) | (depth == last))
    def _():
        pl.semaphore_wait(barrier, 1)

    def to_right(step):
        src = x_ref if step == 0 else out_ref.at[depth - step]
        return send_to(
            src, out_ref.at[depth - step], right_send.at[step], right_recv.at[step], right
        )

    def to_left(step):
        src = x_ref if step == 0 else out_ref.at[depth + step]
        return send_to(src, out_ref.at[depth + step], left_send.at[step], left_recv.at[step], left)

    for step in range(last):

        @pl.when((depth < last) & (depth >= step))
        def _():
            to_right(step).start()

        @pl.when((depth > 0) & (depth + step <= last))
        def _():
            to_left(step).start()

        if step == 0:
            out_ref[depth] = x_ref[...]

        @pl.when(depth - 1 >= step)
        def _():
            send_to(
                x_ref,
                out_ref.at[depth - 1 - step],
                right_send.at[step],
                right_recv.at[step],
                left,
            ).wait_recv()

        @pl.when(depth + 1 + step <= last)
        def _():
            send_to(
                x_ref, out_ref.at[depth + 1 + step], left_send.at[step], left_recv.at[step], right
            ).wait_recv()

    for step in range(last):

        @pl.when((depth < last) & (depth >= step))
        def _():
            to_right(step).wait_send()

        @pl.when((depth > 0) & (depth + step <= last))
        def _():
            to_left(step).wait_send()


def line_gather(block, collective):
    depths = lax.axis_size("tensor")
    rows, width = block.shape
    out = pl.pallas_call(
        line_gather_kernel,
        out_shape=jax.ShapeDtypeStruct((depths, rows, width), block.dtype),
        in_specs=[whole_vmem()],
        out_specs=whole_vmem(),
        scratch_shapes=[pltpu.SemaphoreType.DMA((depths,))] * 4,
        compiler_params=pltpu.CompilerParams(
            collective_id=collective, has_side_effects=True, vmem_limit_bytes=16 * 2**20
        ),
        cost_estimate=pl.CostEstimate(
            flops=25 * 10**9, bytes_accessed=depths * rows * width * 4, transcendentals=0
        ),
    )(block)
    return out.reshape(depths * rows, width)


def renew_kernel(widths, flips, gains, iterate_ref, *refs):
    olds, news = refs[: len(widths)], refs[len(widths) :]
    keep_rate = 1.0 - MUON_RATE * MUON_DECAY
    offset = 0
    for width, flip, gain, old, new in zip(widths, flips, gains, olds, news):
        if flip:
            for first in range(0, width, 128):
                size = min(128, width - first)
                piece = iterate_ref[:, offset + first : offset + first + size]
                rows = slice(first, first + size)
                new[rows, :] = keep_rate * old[rows, :] - MUON_RATE * gain * (
                    piece.astype(jnp.float32).T
                )
        else:
            for first in range(0, old.shape[0], 128):
                rows = slice(first, first + 128)
                piece = iterate_ref[rows, offset : offset + width]
                new[rows, :] = keep_rate * old[rows, :] - MUON_RATE * gain * (
                    piece.astype(jnp.float32)
                )
        offset += width


def renew(iterate, olds, widths, flips, gains):
    return pl.pallas_call(
        functools.partial(renew_kernel, widths, flips, gains),
        out_shape=tuple(jax.ShapeDtypeStruct(old.shape, jnp.float32) for old in olds),
        in_specs=[whole_vmem()] * (1 + len(olds)),
        out_specs=tuple(whole_vmem() for _ in olds),
        compiler_params=pltpu.CompilerParams(vmem_limit_bytes=48 * 2**20),
        cost_estimate=pl.CostEstimate(
            flops=10**9, bytes_accessed=iterate.size * 10, transcendentals=0
        ),
    )(iterate, *olds)


HALF = 128


def greet_line(depth, last, rank):
    barrier = pltpu.get_barrier_semaphore()

    @pl.when(depth < last)
    def _():
        pl.semaphore_signal(
            barrier, inc=1, device_id=(rank, depth + 1), device_id_type=MESH_ID
        )

    @pl.when(depth > 0)
    def _():
        pl.semaphore_signal(
            barrier, inc=1, device_id=(rank, depth - 1), device_id_type=MESH_ID
        )

    @pl.when((depth > 0) & (depth < last))
    def _():
        pl.semaphore_wait(barrier, 2)

    @pl.when((depth == 0) | (depth == last))
    def _():
        pl.semaphore_wait(barrier, 1)


def line_mlp_kernel(
    x_ref,
    first_ref,
    second_ref,
    out_ref,
    rows,
    parts,
    from_left,
    from_right,
    stage,
    right_sems,
    left_sems,
    row_sems,
    sum_sems,
    from_left_sems,
    from_right_sems,
):
    rank = lax.axis_index("dp")
    depth = lax.axis_index("tensor")
    last = lax.axis_size("tensor") - 1
    right, left = (rank, depth + 1), (rank, depth - 1)
    greet_line(depth, last, rank)

    def rows_right(j, h):
        return send_to(rows.at[j, h], rows.at[j, h], right_sems.at[j, h], row_sems.at[j, h], right)

    def rows_left(j, h):
        return send_to(rows.at[j, h], rows.at[j, h], left_sems.at[j, h], row_sems.at[j, h], left)

    def sum_right(j, h):
        return send_to(
            stage.at[j, h], from_left.at[j, h], sum_sems.at[j, h], from_left_sems.at[j, h], right
        )

    def sum_left(j, h):
        return send_to(
            stage.at[j, h], from_right.at[j, h], sum_sems.at[j, h], from_right_sems.at[j, h], left
        )

    for h in range(2):
        rows[depth, h] = x_ref[h * HALF : (h + 1) * HALF, :]

        @pl.when(depth < last)
        def _():
            rows_right(depth, h).start()

        @pl.when(depth > 0)
        def _():
            rows_left(depth, h).start()

    inner = depth * (last - depth) // 2
    side = depth // 2
    for step, shift in enumerate((1, 1, -2, 0)):
        base = step + inner * shift
        j = base + side * (last - 2 * base)

        def half_step(h, carry):
            if step:

                @pl.when(j < depth)
                def _():
                    rows_right(j, h).wait_recv()

                @pl.when(j > depth)
                def _():
                    rows_left(j, h).wait_recv()

                @pl.when((j < depth) & (depth < last))
                def _():
                    rows_right(j, h).start()

                @pl.when((j > depth) & (depth > 0))
                def _():
                    rows_left(j, h).start()

            hidden = smooth_gelu(plain_dot(rows[j, h], first_ref[...])).astype(jnp.bfloat16)
            part = plain_dot(hidden, second_ref[...])
            parts[j, h] = part
            if step:

                @pl.when((depth == 0) | (depth == last))
                def _():
                    stage[j, h] = part.astype(jnp.bfloat16)

                @pl.when(depth == 0)
                def _():
                    sum_right(j, h).start()

                @pl.when(depth == last)
                def _():
                    sum_left(j, h).start()

            return carry

        lax.fori_loop(0, 2, half_step, 0)

    def relay_right(j):
        for h in range(2):
            sum_right(j, h).wait_recv()
            stage[j, h] = (parts[j, h] + from_left[j, h].astype(jnp.float32)).astype(jnp.bfloat16)
            sum_right(j, h).start()

    def relay_left(j):
        for h in range(2):
            sum_left(j, h).wait_recv()
            stage[j, h] = (parts[j, h] + from_right[j, h].astype(jnp.float32)).astype(jnp.bfloat16)
            sum_left(j, h).start()

    @pl.when(depth == 1)
    def _():
        relay_right(2)
        relay_right(3)
        relay_left(0)

    @pl.when(depth == 2)
    def _():
        relay_left(1)
        relay_left(0)
        relay_right(3)

    for h in range(2):
        span = slice(h * HALF, (h + 1) * HALF)
        out_ref[span, :] = parts[depth, h]

        @pl.when(depth > 0)
        def _():
            sum_right(depth, h).wait_recv()
            out_ref[span, :] += from_left[depth, h].astype(jnp.float32)

        @pl.when(depth < last)
        def _():
            sum_left(depth, h).wait_recv()
            out_ref[span, :] += from_right[depth, h].astype(jnp.float32)

    for j in range(4):
        for h in range(2):

            @pl.when((depth >= j) & (depth < last))
            def _():
                rows_right(j, h).wait_send()

            @pl.when((depth <= j) & (depth > 0))
            def _():
                rows_left(j, h).wait_send()

            @pl.when(depth < j)
            def _():
                sum_right(j, h).wait_send()

            @pl.when(depth > j)
            def _():
                sum_left(j, h).wait_send()


def line_mlp(block, first, second, collective):
    count, width = block.shape
    slots = (4, 2, HALF, width)
    return pl.pallas_call(
        line_mlp_kernel,
        out_shape=jax.ShapeDtypeStruct((count, width), jnp.float32),
        in_specs=[whole_vmem()] * 3,
        out_specs=whole_vmem(),
        scratch_shapes=[
            pltpu.VMEM(slots, jnp.bfloat16),
            pltpu.VMEM(slots, jnp.float32),
            pltpu.VMEM(slots, jnp.bfloat16),
            pltpu.VMEM(slots, jnp.bfloat16),
            pltpu.VMEM(slots, jnp.bfloat16),
        ]
        + [pltpu.SemaphoreType.DMA((4, 2))] * 6,
        compiler_params=pltpu.CompilerParams(
            collective_id=collective, has_side_effects=True, vmem_limit_bytes=48 * 2**20
        ),
        cost_estimate=pl.CostEstimate(
            flops=16 * count * width * first.shape[1] * 4,
            bytes_accessed=16 * count * width,
            transcendentals=4 * count * first.shape[1],
        ),
    )(block, first, second)


NBLK = 256


def split_store(value, high_ref, low_ref, rows, cols):
    high = value.astype(jnp.bfloat16)
    high_ref[rows, cols] = high
    low_ref[rows, cols] = (value - high.astype(jnp.float32)).astype(jnp.bfloat16)


def polynomial_kernel(gram_ref, out_ref, full_g, full_h, full_m, *pairs):
    gram_pair, half_pair, poly_pair, prod_pair = (
        pairs[0:2], pairs[2:4], pairs[4:6], pairs[6:8]
    )
    size = gram_ref.shape[0]
    blocks = size // NBLK
    spans = [slice(i * NBLK, (i + 1) * NBLK) for i in range(blocks)]
    upper = [(i, j) for i in range(blocks) for j in range(i, blocks)]

    def eye(i, j):
        if i != j:
            return 0.0
        row = lax.broadcasted_iota(jnp.int32, (NBLK, NBLK), 0)
        col = lax.broadcasted_iota(jnp.int32, (NBLK, NBLK), 1)
        return jnp.where(row == col, 1.0, 0.0)

    def place(i, j, value, full, pair):
        if full is not None:
            full[spans[i], spans[j]] = value
        if pair is not None:
            split_store(value, *pair, spans[i], spans[j])
        if i != j:
            flip = value.T
            if full is not None:
                full[spans[j], spans[i]] = flip
            if pair is not None:
                split_store(flip, *pair, spans[j], spans[i])

    def product(left, right, i, j):
        return plain_dot(left[0][spans[i], :], right[0][:, spans[j]]) + (
            plain_dot(left[0][spans[i], :], right[1][:, spans[j]])
            + plain_dot(left[1][spans[i], :], right[0][:, spans[j]])
        )

    trace = 0.0
    for i in range(blocks):
        trace = trace + jnp.sum(gram_ref[spans[i], spans[i]] * eye(i, i))
    root = jnp.sqrt(jnp.full((1, 1), trace, jnp.float32)) + 1e-07
    inverse = 1.0 / root
    for i, j in upper:
        place(i, j, gram_ref[spans[i], spans[j]] * (inverse * inverse), full_g, gram_pair)

    def make_poly():
        for i, j in upper:
            value = NS_B * full_g[spans[i], spans[j]] + NS_C * product(gram_pair, gram_pair, i, j)
            place(i, j, value, None, poly_pair)

    def advance():
        for i, j in upper:
            value = NS_A * full_g[spans[i], spans[j]] + product(poly_pair, gram_pair, i, j)
            place(i, j, value, full_h, half_pair)
        for i, j in upper:
            value = NS_A * full_h[spans[i], spans[j]] + product(poly_pair, half_pair, i, j)
            place(i, j, value, full_g, gram_pair)

    make_poly()
    for i, j in upper:
        value = (
            poly_pair[0][spans[i], spans[j]].astype(jnp.float32)
            + poly_pair[1][spans[i], spans[j]].astype(jnp.float32)
            + NS_A * eye(i, j)
        )
        place(i, j, value, full_m, prod_pair)
    advance()

    def sweep(index, carry):
        make_poly()
        for i, j in upper:
            value = NS_A * full_m[spans[i], spans[j]] + product(poly_pair, prod_pair, i, j)
            place(i, j, value, full_h, None)
        for i in range(blocks):
            full_m[spans[i], :] = full_h[spans[i], :]
            split_store(full_h[spans[i], :], *prod_pair, spans[i], slice(None))
        advance()
        return carry

    lax.fori_loop(0, 3, sweep, 0)
    make_poly()
    for i, j in upper:
        value = NS_A * full_m[spans[i], spans[j]] + product(poly_pair, prod_pair, i, j)
        place(i, j, value * inverse, out_ref, None)


def orthogonal_factor(gram_mat):
    size = gram_mat.shape[0]
    return pl.pallas_call(
        polynomial_kernel,
        out_shape=jax.ShapeDtypeStruct((size, size), jnp.float32),
        in_specs=[whole_vmem()],
        out_specs=whole_vmem(),
        scratch_shapes=[pltpu.VMEM((size, size), jnp.float32)] * 3
        + [pltpu.VMEM((size, size), jnp.bfloat16)] * 8,
        compiler_params=pltpu.CompilerParams(vmem_limit_bytes=48 * 2**20),
        cost_estimate=pl.CostEstimate(
            flops=17 * 2 * 2 * size**3, bytes_accessed=8 * size * size, transcendentals=0
        ),
    )(gram_mat)


def contract_rows(left, right):
    return lax.dot_general(
        left, right, (((0,), (0,)), ((), ())), preferred_element_type=jnp.float32
    )


def contract_cols(left, right):
    return lax.dot_general(
        left, right, (((1,), (1,)), ((), ())), preferred_element_type=jnp.float32
    )


def body(
    teacher_in,
    student_in,
    resp_mask,
    replay,
    t_gains,
    t_shifts,
    t_qkv,
    t_out,
    t_fc,
    t_proj,
    s_norms,
    s_qkv,
    s_out,
    s_fc,
    s_proj,
    s_map,
    mom_qkv,
    mom_out,
    mom_fc,
    mom_proj,
    mom_map,
    adam_first,
    adam_second,
):
    groups = lax.axis_size("tensor")
    tensor_rank = lax.axis_index("tensor")
    row_count = student_in.shape[0]
    seq_count = replay.shape[0]
    total_rows = row_count * groups
    count_block = jnp.full((8, 128), jnp.sum(resp_mask), jnp.int32).astype(jnp.float32)
    count_val = sum_small(count_block, 0)[0, 0]
    tokens_all = lax.axis_size("dp") * seq_count * LEN
    factor = tokens_all / (2.0 * count_val)

    def teacher_gather(local_rows):
        return lax.all_gather(local_rows, "tensor", axis=0, tiled=True)

    def teacher_reduce(left, right):
        return lax.psum_scatter(
            jnp.dot(left, right, preferred_element_type=jnp.float32).astype(jnp.bfloat16),
            "tensor",
            scatter_dimension=0,
            tiled=True,
        ).astype(jnp.float32)

    def student_gather(local_rows):
        return lax.all_gather(local_rows, "tensor", axis=0, tiled=True)

    def student_reduce(left, right, right_dim):
        return lax.psum_scatter(
            lax.dot_general(
                left, right, (((1,), (right_dim,)), ((), ())), preferred_element_type=jnp.float32
            ).astype(jnp.bfloat16),
            "tensor",
            scatter_dimension=0,
            tiled=True,
        ).astype(jnp.float32)

    teacher_x = teacher_in.astype(jnp.float32)
    slot_width = t_qkv.shape[2]
    slot_count = slot_width // HEAD
    live_count = HT // groups + (tensor_rank < HT % groups).astype(jnp.int32)
    live_slots = (jnp.arange(slot_count, dtype=jnp.int32) < live_count).astype(jnp.float32)
    teacher_normed = norm_parts(teacher_x, t_gains[0], t_shifts[0])[0].astype(jnp.bfloat16)
    teacher_all = teacher_gather(teacher_normed)
    teacher_mixed = jnp.dot(
        teacher_all, t_qkv.reshape(DT, 3 * slot_width), preferred_element_type=jnp.float32
    ).astype(jnp.bfloat16)
    teacher_head_out = attend_forward(teacher_mixed, slot_count)[0]
    slot_mask = jnp.repeat(live_slots, HEAD)[None, :] > 0.0
    teacher_head_out = jnp.where(slot_mask, teacher_head_out, jnp.zeros_like(teacher_head_out))
    student_x = student_in.astype(jnp.float32)
    shard_width = s_qkv.shape[2]
    shard_hidden = s_fc.shape[1]
    head_count = shard_width // HEAD
    w_qkv = s_qkv.astype(jnp.bfloat16).reshape(DS, 3 * shard_width)
    w_out = s_out.astype(jnp.bfloat16)
    w_fc = s_fc.astype(jnp.bfloat16)
    w_proj = s_proj.astype(jnp.bfloat16)
    w_map = s_map.astype(jnp.bfloat16)
    normed_one, unit_one, scale_one = norm_parts(student_x, s_norms[0], s_norms[1])
    low_one = normed_one.astype(jnp.bfloat16)
    rows_one = line_gather(low_one, 5)
    mixed_qkv = jnp.dot(rows_one, w_qkv, preferred_element_type=jnp.float32).astype(jnp.bfloat16)
    head_out, log_sums = attend_forward(mixed_qkv, head_count)
    resid = student_x + student_reduce(head_out, w_out, 0)
    normed_two, unit_two, scale_two = norm_parts(resid, s_norms[2], s_norms[3])
    low_two = normed_two.astype(jnp.bfloat16)
    rows_two = line_gather(low_two, 6)
    attn_part = teacher_reduce(teacher_head_out, t_out)
    attn_part, rows_two = lax.optimization_barrier((attn_part, rows_two))
    teacher_resid = teacher_x + attn_part
    teacher_normed_two = norm_parts(teacher_resid, t_gains[1], t_shifts[1])[0].astype(jnp.bfloat16)
    mlp_part = line_mlp(teacher_normed_two, t_fc, t_proj, 8)
    teacher_out = (teacher_resid + mlp_part).astype(jnp.bfloat16)
    before = jnp.dot(rows_two, w_fc, preferred_element_type=jnp.float32)
    before, hidden = (before, smooth_gelu(before).astype(jnp.bfloat16))
    output = resid + student_reduce(hidden, w_proj, 0)
    student_out = output.astype(jnp.bfloat16)
    guess_vec = jnp.dot(student_out, w_map, preferred_element_type=jnp.float32)
    miss_vec = guess_vec - teacher_out.astype(jnp.float32)
    position = tensor_rank * row_count + jnp.arange(row_count, dtype=jnp.int32)
    seq_owner = position // LEN
    seq_pick = (seq_owner[:, None] == jnp.arange(seq_count, dtype=jnp.int32)[None, :]).astype(
        jnp.float32
    )
    flag_tok = jnp.sum(seq_pick * replay.astype(jnp.float32)[None, :], axis=1)
    weight = resp_mask.astype(jnp.float32) * (1.0 - REPLAY_CUT * flag_tok)
    loss_part = jnp.sum(weight[:, None] * miss_vec * miss_vec)
    grad_guess = (2.0 * factor * weight[:, None] * miss_vec).astype(jnp.bfloat16)
    row_unit = 8 * lax.axis_size("dp") * groups
    map_slab = scatter_rows(pad_rows(contract_rows(grad_guess, student_out), row_unit), 1)
    grad_output = contract_cols(grad_guess, w_map)
    rows_two_back, before_back, hidden_back = (rows_two, before, hidden)
    rows_one_back, mixed_back, heads_back, logs_back = (rows_one, mixed_qkv, head_out, log_sums)
    grad_mlp = student_gather(grad_output.astype(jnp.bfloat16))
    grad_mlp, map_slab = lax.optimization_barrier((grad_mlp, map_slab))
    grad_proj = contract_rows(hidden_back, grad_mlp)
    grad_hidden = contract_cols(grad_mlp, w_proj)
    gelu_vals, gelu_pull = jax.vjp(smooth_gelu, before_back)
    grad_before = gelu_pull(grad_hidden)[0].astype(jnp.bfloat16)
    grad_fc = contract_rows(rows_two_back, grad_before).reshape(-1, DS)
    mlp_slab = scatter_rows(jnp.concatenate([grad_proj, grad_fc], axis=0), 2)
    grad_normed_two = student_reduce(grad_before, w_fc, 1)
    grad_normed_two, mlp_slab = lax.optimization_barrier((grad_normed_two, mlp_slab))
    grad_resid = grad_output + norm_back(grad_normed_two, unit_two, scale_two, s_norms[2])
    grad_attn = student_gather(grad_resid.astype(jnp.bfloat16))
    grad_mlp_rows = spread(mlp_slab, 7)
    grad_attn, grad_mlp_rows = lax.optimization_barrier((grad_attn, grad_mlp_rows))
    grad_proj, grad_fc = grad_mlp_rows[:shard_hidden], grad_mlp_rows[shard_hidden:]
    grad_out = contract_rows(heads_back, grad_attn)
    grad_heads = contract_cols(grad_attn, w_out).astype(jnp.bfloat16)

    grad_mixed = attend_backward(mixed_back, logs_back, grad_heads, head_count)
    grad_qkv = contract_rows(grad_mixed, rows_one_back)
    grad_attn_rows, grad_map = sum_and_spread(
        jnp.concatenate([grad_out, grad_qkv], axis=0), map_slab, 3
    )
    grad_map = grad_map[:DT]
    grad_out, grad_qkv = grad_attn_rows[:shard_width], grad_attn_rows[shard_width:]
    grad_fc = grad_fc.reshape(DS, shard_hidden)
    def to_tall(mat):
        return mat.transpose(1, 2, 0).reshape(-1, DS)

    def from_tall(mat):
        return mat.reshape(3, shard_width, DS).transpose(2, 0, 1)

    moments = [
        MOMENTUM * to_tall(mom_qkv) + grad_qkv,
        MOMENTUM * mom_out + grad_out,
        MOMENTUM * mom_fc + grad_fc,
        MOMENTUM * mom_proj + grad_proj,
    ]
    moment_map = MOMENTUM * mom_map.T + grad_map
    dp_count = lax.axis_size("dp")
    dp_rank = lax.axis_index("dp")
    slice_rows = DS // dp_count
    first_row = dp_rank * slice_rows
    talls = [moments[0], moments[1], moments[2], moments[3], moment_map]
    sums = [0, 0, 1, 0, 0]

    def gram_rows(tall, axis):
        return lax.dot_general(
            lax.dynamic_slice_in_dim(tall, first_row, slice_rows, 1 - axis),
            tall,
            (((axis,), (axis,)), ((), ())),
            precision=HIGH,
            preferred_element_type=jnp.float32,
        )

    parts = jnp.concatenate([gram_rows(talls[i], sums[i]) for i in range(4)], axis=0)
    own_rows = lax.psum_scatter(parts, "tensor", scatter_dimension=0, tiled=True)
    both_rows = jnp.concatenate([own_rows[None], gram_rows(talls[4], sums[4])[None]], axis=0)
    both_rows = lax.all_gather(both_rows, "dp", axis=1, tiled=True)
    both_rows, grad_mixed = lax.optimization_barrier((both_rows, grad_mixed))
    grad_normed_one = student_reduce(grad_mixed, w_qkv, 1)
    mine = dp_rank % 2
    factor_mat = orthogonal_factor(jnp.where(mine == 0, both_rows[0], both_rows[1]))
    pair_rows = lax.dynamic_slice_in_dim(factor_mat, (dp_rank // 2) * 2 * slice_rows, 2 * slice_rows, 0)
    other_rows = lax.ppermute(
        pair_rows, "dp", [(i, i ^ 1) for i in range(dp_count)]
    )
    even_rows = jnp.where(mine == 0, pair_rows, other_rows)
    odd_rows = jnp.where(mine == 0, other_rows, pair_rows)
    even_rows = lax.dynamic_slice_in_dim(even_rows, mine * slice_rows, slice_rows, 0)
    odd_rows = lax.dynamic_slice_in_dim(odd_rows, mine * slice_rows, slice_rows, 0)
    even_rows, grad_normed_one = lax.optimization_barrier((even_rows, grad_normed_one))
    factor_rows = lax.all_gather(even_rows, "tensor", axis=0)
    input_grad = grad_resid + norm_back(grad_normed_one, unit_one, scale_one, s_norms[0])
    norm_grads = jnp.stack(
        [
            jnp.sum(grad_normed_one * unit_one, axis=0),
            jnp.sum(grad_normed_one, axis=0),
            jnp.sum(grad_normed_two * unit_two, axis=0),
            jnp.sum(grad_normed_two, axis=0),
        ]
    )
    small = jnp.concatenate(
        [norm_grads, jnp.full((4, DS), loss_part, jnp.float32)], axis=0
    )
    small = sum_small(small, 4)
    norm_grads = small[:4]
    loss = small[4, 0] / (count_val * DT)

    pieces = [
        lax.dot_general(
            factor_rows[i] if i < 4 else odd_rows,
            talls[i],
            (((1,), (1 - sums[i],)), ((), ())),
            precision=lax.Precision.HIGH,
            preferred_element_type=jnp.float32,
        ).astype(jnp.bfloat16)
        for i in (2, 3, 1, 0, 4)
    ]
    iterate_all = lax.all_gather(jnp.concatenate(pieces, axis=1), "dp", axis=0, tiled=True)
    weight_fc, weight_proj, weight_out, weight_qkv, weight_map = renew(
        iterate_all,
        (s_fc, s_proj, s_out, to_tall(s_qkv), s_map.T),
        [piece.shape[1] for piece in pieces],
        [False, True, True, True, True],
        [math.sqrt(FS / DS), 1.0, 1.0, math.sqrt(3.0), math.sqrt(DT / DS)],
    )
    norm_first = BETA_ONE * adam_first + (1.0 - BETA_ONE) * norm_grads
    norm_second = BETA_TWO * adam_second + (1.0 - BETA_TWO) * norm_grads * norm_grads
    fix_one = 1.0 - BETA_ONE**STEP
    fix_two = 1.0 - BETA_TWO**STEP
    norm_values = s_norms - ADAM_RATE * (
        norm_first / fix_one / (jnp.sqrt(norm_second / fix_two) + ADAM_EPS) + ADAM_DECAY * s_norms
    )
    return (
        teacher_out,
        student_out,
        input_grad,
        loss,
        from_tall(grad_qkv),
        grad_out,
        grad_fc,
        grad_proj,
        grad_map.T,
        from_tall(moments[0]),
        moments[1],
        moments[2],
        moments[3],
        moment_map.T,
        from_tall(weight_qkv),
        weight_out,
        weight_fc,
        weight_proj,
        weight_map.T,
        norm_first,
        norm_second,
        norm_values,
    )


def solution(mesh):
    return jax.shard_map(
        body,
        mesh=mesh,
        in_specs=(
            P(("dp", "tensor"), None),
            P(("dp", "tensor"), None),
            P(("dp", "tensor")),
            P("dp"),
            P(),
            P(),
            P(None, None, "tensor"),
            P("tensor", None),
            P(None, "tensor"),
            P("tensor", None),
            P(),
            P(None, None, "tensor"),
            P("tensor", None),
            P(None, "tensor"),
            P("tensor", None),
            P(),
            P(None, None, "tensor"),
            P("tensor", None),
            P(None, "tensor"),
            P("tensor", None),
            P(),
            P(),
            P(),
        ),
        out_specs=(
            P(("dp", "tensor"), None),
            P(("dp", "tensor"), None),
            P(("dp", "tensor"), None),
            P(),
            P(None, None, "tensor"),
            P("tensor", None),
            P(None, "tensor"),
            P("tensor", None),
            P(),
            P(None, None, "tensor"),
            P("tensor", None),
            P(None, "tensor"),
            P("tensor", None),
            P(),
            P(None, None, "tensor"),
            P("tensor", None),
            P(None, "tensor"),
            P("tensor", None),
            P(),
            P(),
            P(),
            P(),
        ),
        check_vma=False,
    )
```

```python
import functools
import math

import jax
import jax.numpy as jnp
from jax import lax
from jax.experimental import pallas as pl
from jax.experimental.pallas import tpu as pltpu
from jax.sharding import PartitionSpec as P

DT = 1600
HT = 25
DS = 768
FS = 3072
HEAD = 64
LEN = 1024
STEP = 10
ABLK = 256


EPS = 1e-05
NS_A = 3.4445
NS_B = -4.775
NS_C = 2.0315
MOMENTUM = 0.95
MUON_RATE = 0.5
MUON_DECAY = 0.01
ADAM_RATE = 0.3
BETA_ONE = 0.9
BETA_TWO = 0.999
ADAM_EPS = 1e-08
ADAM_DECAY = 0.01
REPLAY_CUT = 0.5
NEG_FILL = -1e30
HIGH = lax.Precision.HIGHEST


def norm_parts(v, gain_vec, shift_vec):
    row_mean = jnp.mean(v, axis=-1, keepdims=True)
    centred = v - row_mean
    row_var = jnp.mean(centred * centred, axis=-1, keepdims=True)
    inv_scale = lax.rsqrt(row_var + EPS)
    unit_val = centred * inv_scale
    return (unit_val * gain_vec + shift_vec, unit_val, inv_scale)


def norm_back(grad_norm, unit_val, inv_scale, gain_vec):
    grad_unit = grad_norm * gain_vec
    first_mean = jnp.mean(grad_unit, axis=-1, keepdims=True)
    second_mean = jnp.mean(grad_unit * unit_val, axis=-1, keepdims=True)
    return inv_scale * (grad_unit - first_mean - unit_val * second_mean)


def smooth_gelu(v):
    return 0.5 * v * (1.0 + jnp.tanh(0.7978845608028654 * (v + 0.044715 * v * v * v)))


def whole_vmem():
    return pl.BlockSpec(memory_space=pltpu.VMEM)


def nt_dot(left, right):
    return lax.dot_general(
        left, right, (((1,), (1,)), ((), ())), preferred_element_type=jnp.float32
    )


def tn_dot(left, right):
    return lax.dot_general(
        left, right, (((0,), (0,)), ((), ())), preferred_element_type=jnp.float32
    )


def plain_dot(left, right):
    return jnp.dot(left, right, preferred_element_type=jnp.float32)


def lower_mask():
    row_pos = lax.broadcasted_iota(jnp.int32, (ABLK, ABLK), 0)
    key_pos = lax.broadcasted_iota(jnp.int32, (ABLK, ABLK), 1)
    return key_pos <= row_pos


def attend_forward_kernel(head_count, qkv_ref, out_ref, log_ref):
    width = head_count * HEAD
    for head in range(head_count):
        cols = slice(head * HEAD, (head + 1) * HEAD)
        keys = qkv_ref[:, width + head * HEAD : width + (head + 1) * HEAD]
        values = qkv_ref[:, 2 * width + head * HEAD : 2 * width + (head + 1) * HEAD]
        for block in range(LEN // ABLK):
            low, high = block * ABLK, (block + 1) * ABLK
            query = qkv_ref[low:high, cols]
            near = nt_dot(query, keys[low:high]) * HEAD ** (-0.5)
            near = jnp.where(lower_mask(), near, NEG_FILL)
            row_top = jnp.max(near, axis=-1, keepdims=True)
            if block:
                far = nt_dot(query, keys[:low]) * HEAD ** (-0.5)
                row_top = jnp.maximum(row_top, jnp.max(far, axis=-1, keepdims=True))
            near = jnp.exp(near - row_top)
            row_total = jnp.sum(near, axis=-1, keepdims=True)
            if block:
                far = jnp.exp(far - row_top)
                row_total = row_total + jnp.sum(far, axis=-1, keepdims=True)
            inverse = 1.0 / row_total
            mixed = plain_dot((near * inverse).astype(jnp.bfloat16), values[low:high])
            if block:
                mixed = mixed + plain_dot((far * inverse).astype(jnp.bfloat16), values[:low])
            out_ref[low:high, cols] = mixed.astype(out_ref.dtype)
            log_ref[low:high, head : head + 1] = row_top + jnp.log(row_total)


def attend_forward(mixed_qkv, head_count):
    width = head_count * HEAD
    return pl.pallas_call(
        functools.partial(attend_forward_kernel, head_count),
        out_shape=(
            jax.ShapeDtypeStruct((LEN, width), jnp.bfloat16),
            jax.ShapeDtypeStruct((LEN, 128), jnp.float32),
        ),
        in_specs=[whole_vmem()],
        out_specs=(whole_vmem(), whole_vmem()),
        compiler_params=pltpu.CompilerParams(vmem_limit_bytes=40 * 2**20),
        cost_estimate=pl.CostEstimate(
            flops=4 * head_count * LEN * LEN * HEAD * 4,
            bytes_accessed=LEN * width * 8,
            transcendentals=head_count * LEN * LEN // 2,
        ),
    )(mixed_qkv)


def attend_backward_kernel(
    head_count, qkv_ref, log_ref, grad_ref, out_ref, key_acc, value_acc
):
    width = head_count * HEAD
    scale = HEAD ** (-0.5)
    for head in range(head_count):
        cols = slice(head * HEAD, (head + 1) * HEAD)
        key_cols = slice(width + head * HEAD, width + (head + 1) * HEAD)
        value_cols = slice(2 * width + head * HEAD, 2 * width + (head + 1) * HEAD)
        keys = qkv_ref[:, key_cols]
        values = qkv_ref[:, value_cols]
        for block in range(LEN // ABLK - 1, -1, -1):
            low, high = block * ABLK, (block + 1) * ABLK
            query = qkv_ref[low:high, cols]
            grad = grad_ref[low:high, cols]
            log_sum = log_ref[low:high, head : head + 1]
            near = nt_dot(query, keys[low:high]) * scale
            near = jnp.exp(jnp.where(lower_mask(), near, NEG_FILL) - log_sum)
            near_back = nt_dot(grad, values[low:high])
            inner = jnp.sum(near * near_back, axis=-1, keepdims=True)
            if block:
                far = jnp.exp(nt_dot(query, keys[:low]) * scale - log_sum)
                far_back = nt_dot(grad, values[:low])
                inner = inner + jnp.sum(far * far_back, axis=-1, keepdims=True)
            near_score = (near * (near_back - inner)).astype(jnp.bfloat16)
            grad_query = plain_dot(near_score, keys[low:high])
            near_key = tn_dot(near_score, query)
            near_value = tn_dot(near.astype(jnp.bfloat16), grad)
            if block == LEN // ABLK - 1:
                key_acc[low:high, :] = near_key
                value_acc[low:high, :] = near_value
            else:
                key_acc[low:high, :] += near_key
                value_acc[low:high, :] += near_value
            if block:
                far_score = (far * (far_back - inner)).astype(jnp.bfloat16)
                grad_query = grad_query + plain_dot(far_score, keys[:low])
                far_key = tn_dot(far_score, query)
                far_value = tn_dot(far.astype(jnp.bfloat16), grad)
                if block == LEN // ABLK - 1:
                    key_acc[:low, :] = far_key
                    value_acc[:low, :] = far_value
                else:
                    key_acc[:low, :] += far_key
                    value_acc[:low, :] += far_value
            out_ref[low:high, cols] = (grad_query * scale).astype(jnp.bfloat16)
        out_ref[:, key_cols] = (key_acc[...] * scale).astype(jnp.bfloat16)
        out_ref[:, value_cols] = value_acc[...].astype(jnp.bfloat16)


def attend_backward(mixed_qkv, log_sums, grad_heads, head_count):
    width = head_count * HEAD
    return pl.pallas_call(
        functools.partial(attend_backward_kernel, head_count),
        out_shape=jax.ShapeDtypeStruct((LEN, 3 * width), jnp.bfloat16),
        in_specs=[whole_vmem()] * 3,
        out_specs=whole_vmem(),
        scratch_shapes=[pltpu.VMEM((LEN, HEAD), jnp.float32)] * 2,
        compiler_params=pltpu.CompilerParams(vmem_limit_bytes=40 * 2**20),
        cost_estimate=pl.CostEstimate(
            flops=10 * head_count * LEN * LEN * HEAD * 4,
            bytes_accessed=LEN * width * 16,
            transcendentals=head_count * LEN * LEN // 2,
        ),
    )(mixed_qkv, log_sums, grad_heads)


MESH_ID = pl.DeviceIdType.MESH


def place_of():
    dp_count = lax.axis_size("dp")
    rank = lax.axis_index("dp")
    return dp_count // 2, rank // 2, rank % 2, lax.axis_index("tensor")


def greet(peers):
    barrier = pltpu.get_barrier_semaphore()
    for peer in peers:
        pl.semaphore_signal(barrier, inc=1, device_id=peer, device_id_type=MESH_ID)
    pl.semaphore_wait(barrier, len(peers))


def send_to(src, dst, send_sem, recv_sem, peer):
    return pltpu.make_async_remote_copy(
        src_ref=src,
        dst_ref=dst,
        send_sem=send_sem,
        recv_sem=recv_sem,
        device_id=peer,
        device_id_type=MESH_ID,
    )


def small_peers():
    chips, chip, core, depth = place_of()
    depths = lax.axis_size("tensor")
    flat = [((lax.rem(chip + k, chips)) * 2 + core, depth) for k in range(1, chips)]
    deep = [(chip * 2 + core, lax.rem(depth + k, depths)) for k in range(1, depths)]
    return [(chip * 2 + 1 - core, depth)] + flat + deep


def exchange_small(
    x_ref, out_ref, pair, plane, line, pair_sems, plane_sems, line_sems
):
    chips, chip, core, depth = place_of()
    depths = lax.axis_size("tensor")
    sibling = (chip * 2 + 1 - core, depth)
    flat = [((lax.rem(chip + k, chips)) * 2 + core, depth) for k in range(1, chips)]
    deep = [(chip * 2 + core, lax.rem(depth + k, depths)) for k in range(1, depths)]
    copy = send_to(x_ref, pair, pair_sems.at[0], pair_sems.at[1], sibling)
    copy.start()
    copy.wait()
    plane[chip] = x_ref[...] + pair[...]
    copies = []
    for k in range(1, chips):
        copies.append(
            send_to(
                plane.at[chip], plane.at[chip], plane_sems.at[0, k], plane_sems.at[1, k], flat[k - 1]
            )
        )
    for copy in copies:
        copy.start()
    for copy in copies:
        copy.wait()
    total = plane[0]
    for k in range(1, chips):
        total = total + plane[k]
    line[depth] = total
    copies = []
    for k in range(1, depths):
        copies.append(
            send_to(
                line.at[depth], line.at[depth], line_sems.at[0, k], line_sems.at[1, k], deep[k - 1]
            )
        )
    for copy in copies:
        copy.start()
    for copy in copies:
        copy.wait()
    total = line[0]
    for k in range(1, depths):
        total = total + line[k]
    out_ref[...] = total


def sum_small_kernel(*refs):
    greet(small_peers())
    exchange_small(*refs)


def small_scratch(shape, chips, depths):
    return [
        pltpu.VMEM(shape, jnp.float32),
        pltpu.VMEM((chips,) + shape, jnp.float32),
        pltpu.VMEM((depths,) + shape, jnp.float32),
        pltpu.SemaphoreType.DMA((2,)),
        pltpu.SemaphoreType.DMA((2, chips)),
        pltpu.SemaphoreType.DMA((2, depths)),
    ]


def sum_small(block, collective):
    chips, depths = lax.axis_size("dp") // 2, lax.axis_size("tensor")
    return pl.pallas_call(
        sum_small_kernel,
        out_shape=jax.ShapeDtypeStruct(block.shape, jnp.float32),
        in_specs=[whole_vmem()],
        out_specs=whole_vmem(),
        scratch_shapes=small_scratch(block.shape, chips, depths),
        compiler_params=pltpu.CompilerParams(
            collective_id=collective, has_side_effects=True, vmem_limit_bytes=16 * 2**20
        ),
        cost_estimate=pl.CostEstimate(flops=10**10, bytes_accessed=10**6, transcendentals=0),
    )(block)


def sum_and_spread_kernel(
    x_ref,
    y_ref,
    x_out,
    y_out,
    pair_in,
    pair_sum,
    plane_in,
    total,
    line_in,
    line_out,
    pair_sems,
    plane_sems,
    line_sems,
    spread_sems,
    share_sems,
):
    chips, chip, core, depth = place_of()
    depths = lax.axis_size("tensor")
    rank = chip * 2 + core
    other = 1 - core
    sibling = (chip * 2 + other, depth)
    chip_at = [lax.rem(chip + k, chips) for k in range(chips)]
    flat = [(chip_at[k] * 2 + core, depth) for k in range(chips)]
    deep = [(rank, lax.rem(depth + k, depths)) for k in range(depths)]
    greet([sibling] + flat[1:] + deep[1:])
    part = y_ref.shape[0] // depths
    part_of = [
        pl.ds(pl.multiple_of(lax.rem(depth + k, depths) * part, 8), part) for k in range(depths)
    ]
    halves = [slice(0, y_ref.shape[1] // 2), slice(y_ref.shape[1] // 2, y_ref.shape[1])]
    firsts, seconds = {}, {}
    for c in range(2):
        for k in range(1, depths):
            firsts[c, k] = send_to(
                y_ref.at[part_of[k], halves[c]],
                line_in.at[k, :, halves[c]],
                line_sems.at[c, 0, k],
                line_sems.at[c, 1, k],
                deep[k],
            )
            firsts[c, k].start()
    order = list(range(1, chips)) + [0]
    pair_copies, plane_copies = {}, {}
    for k in order:
        pair_copies[k] = send_to(
            x_ref.at[chip_at[k] * 2 + other],
            pair_in.at[k],
            pair_sems.at[0, k],
            pair_sems.at[1, k],
            sibling,
        )
        pair_copies[k].start()
    for k in order:
        pair_copies[k].wait_recv()
        pair_sum[k] = x_ref[chip_at[k] * 2 + core] + pair_in[k]
        if k:
            plane_copies[k] = send_to(
                pair_sum.at[k], plane_in.at[k], plane_sems.at[0, k], plane_sems.at[1, k], flat[k]
            )
            plane_copies[k].start()
    for c in range(2):
        value = y_ref[part_of[0], halves[c]]
        for k in range(1, depths):
            firsts[c, k].wait_recv()
            value = value + line_in[k, :, halves[c]]
        line_out[part_of[0], halves[c]] = value
        for k in range(1, depths):
            seconds[c, k] = send_to(
                line_out.at[part_of[0], halves[c]],
                line_out.at[part_of[0], halves[c]],
                line_sems.at[c, 2, k],
                line_sems.at[c, 3, k],
                deep[k],
            )
            seconds[c, k].start()
    value = pair_sum[0]
    for k in range(1, chips):
        plane_copies[k].wait_recv()
        value = value + plane_in[k]
    total[...] = value
    x_spread = start_spread(total, x_out, spread_sems.at[2], flat, rank)
    x_out[rank] = value
    y_spread, y_share = {}, {}
    for c in range(2):
        for k in range(1, depths):
            seconds[c, k].wait_recv()
        y_spread[c] = start_spread(
            line_out, y_out, spread_sems.at[c], flat, rank, halves[c]
        )
        y_out[rank, :, halves[c]] = line_out[:, halves[c]]
    place = (chips, chip, core)
    x_share = start_share(x_out, x_spread, share_sems.at[2], place, sibling)
    for c in range(2):
        y_share[c] = start_share(
            y_out, y_spread[c], share_sems.at[c], place, sibling, halves[c]
        )
    for k in range(chips):
        x_share[k].wait_recv()
        y_share[0][k].wait_recv()
        y_share[1][k].wait_recv()
    for copies in (
        pair_copies,
        plane_copies,
        firsts,
        seconds,
        y_spread[0],
        y_spread[1],
        x_spread,
        y_share[0],
        y_share[1],
        x_share,
    ):
        for copy in copies.values():
            copy.wait_send()


def sum_and_spread(rows, slab_y, collective):
    dp_count, depths = lax.axis_size("dp"), lax.axis_size("tensor")
    chips = dp_count // 2
    count, width = rows.shape
    slab = (count // dp_count, width)
    out_x, out_y = pl.pallas_call(
        sum_and_spread_kernel,
        out_shape=(
            jax.ShapeDtypeStruct((dp_count,) + slab, jnp.float32),
            jax.ShapeDtypeStruct((dp_count,) + slab_y.shape, jnp.float32),
        ),
        in_specs=[whole_vmem()] * 2,
        out_specs=(whole_vmem(), whole_vmem()),
        scratch_shapes=[
            pltpu.VMEM((chips,) + slab, jnp.float32),
            pltpu.VMEM((chips,) + slab, jnp.float32),
            pltpu.VMEM((chips,) + slab, jnp.float32),
            pltpu.VMEM(slab, jnp.float32),
            pltpu.VMEM((depths, slab_y.shape[0] // depths, width), jnp.float32),
            pltpu.VMEM(slab_y.shape, jnp.float32),
            pltpu.SemaphoreType.DMA((2, chips)),
            pltpu.SemaphoreType.DMA((2, chips)),
            pltpu.SemaphoreType.DMA((2, 4, depths)),
            pltpu.SemaphoreType.DMA((3, 2, chips)),
            pltpu.SemaphoreType.DMA((3, 2, chips)),
        ],
        compiler_params=pltpu.CompilerParams(
            collective_id=collective, has_side_effects=True, vmem_limit_bytes=32 * 2**20
        ),
        cost_estimate=pl.CostEstimate(
            flops=60 * 10**9, bytes_accessed=count * width * 16, transcendentals=0
        ),
    )(rows.reshape((dp_count,) + slab), slab_y)
    return out_x.reshape(count, width), out_y.reshape(-1, width)


def scatter_rows_kernel(
    x_ref, out_ref, pair_in, pair_sum, plane_in, pair_sems, plane_sems
):
    chips, chip, core, depth = place_of()
    other = 1 - core
    sibling = (chip * 2 + other, depth)
    chip_at = [lax.rem(chip + k, chips) for k in range(chips)]
    flat = [(chip_at[k] * 2 + core, depth) for k in range(chips)]
    greet([sibling] + flat[1:])
    order = list(range(1, chips)) + [0]
    pair_copies, plane_copies = {}, {}
    for k in order:
        pair_copies[k] = send_to(
            x_ref.at[chip_at[k] * 2 + other],
            pair_in.at[k],
            pair_sems.at[0, k],
            pair_sems.at[1, k],
            sibling,
        )
        pair_copies[k].start()
    for k in order:
        pair_copies[k].wait_recv()
        pair_sum[k] = x_ref[chip_at[k] * 2 + core] + pair_in[k]
        if k:
            plane_copies[k] = send_to(
                pair_sum.at[k], plane_in.at[k], plane_sems.at[0, k], plane_sems.at[1, k], flat[k]
            )
            plane_copies[k].start()
    value = pair_sum[0]
    for k in range(1, chips):
        plane_copies[k].wait_recv()
        value = value + plane_in[k]
    out_ref[...] = value
    for copies in (pair_copies, plane_copies):
        for copy in copies.values():
            copy.wait_send()


def pad_rows(rows, unit):
    have, width = rows.shape
    padded = -(-have // unit) * unit
    if padded == have:
        return rows
    return jnp.concatenate([rows, jnp.zeros((padded - have, width), rows.dtype)], axis=0)


def scatter_rows(rows, collective):
    dp_count = lax.axis_size("dp")
    chips = dp_count // 2
    slab = (rows.shape[0] // dp_count, rows.shape[1])
    return pl.pallas_call(
        scatter_rows_kernel,
        out_shape=jax.ShapeDtypeStruct(slab, jnp.float32),
        in_specs=[whole_vmem()],
        out_specs=whole_vmem(),
        scratch_shapes=[
            pltpu.VMEM((chips,) + slab, jnp.float32),
            pltpu.VMEM((chips,) + slab, jnp.float32),
            pltpu.VMEM((chips,) + slab, jnp.float32),
            pltpu.SemaphoreType.DMA((2, chips)),
            pltpu.SemaphoreType.DMA((2, chips)),
        ],
        compiler_params=pltpu.CompilerParams(
            collective_id=collective, has_side_effects=True, vmem_limit_bytes=32 * 2**20
        ),
        cost_estimate=pl.CostEstimate(
            flops=rows.shape[0] * 15 * 10**6,
            bytes_accessed=rows.shape[0] * rows.shape[1] * 4,
            transcendentals=0,
        ),
    )(rows.reshape((dp_count,) + slab))


def start_spread(src, out_ref, sems, flat, rank, cols=slice(None)):
    copies = {}
    for k in range(1, len(flat)):
        copies[k] = send_to(
            src.at[:, cols], out_ref.at[rank, :, cols], sems.at[0, k], sems.at[1, k], flat[k]
        )
        copies[k].start()
    return copies


def start_share(out_ref, spread_copies, sems, place, sibling, cols=slice(None)):
    chips, chip, core = place
    copies = {}
    for k in range(chips):
        if k:
            spread_copies[k].wait_recv()
        held = lax.rem(chip + chips - k, chips) * 2 + core
        copies[k] = send_to(
            out_ref.at[held, :, cols],
            out_ref.at[held, :, cols],
            sems.at[0, k],
            sems.at[1, k],
            sibling,
        )
        copies[k].start()
    return copies


def spread_kernel(x_ref, out_ref, spread_sems, share_sems):
    chips, chip, core, depth = place_of()
    rank = chip * 2 + core
    sibling = (chip * 2 + 1 - core, depth)
    flat = [(lax.rem(chip + k, chips) * 2 + core, depth) for k in range(chips)]
    greet([sibling] + flat[1:])
    spread_copies = start_spread(x_ref, out_ref, spread_sems, flat, rank)
    out_ref[rank] = x_ref[...]
    share_copies = start_share(out_ref, spread_copies, share_sems, (chips, chip, core), sibling)
    for k in range(chips):
        share_copies[k].wait_recv()
    for copies in (spread_copies, share_copies):
        for copy in copies.values():
            copy.wait_send()


def spread(slab, collective):
    dp_count = lax.axis_size("dp")
    chips = dp_count // 2
    each, width = slab.shape
    full = pl.pallas_call(
        spread_kernel,
        out_shape=jax.ShapeDtypeStruct((dp_count, each, width), slab.dtype),
        in_specs=[whole_vmem()],
        out_specs=whole_vmem(),
        scratch_shapes=[
            pltpu.SemaphoreType.DMA((2, chips)),
            pltpu.SemaphoreType.DMA((2, chips)),
        ],
        compiler_params=pltpu.CompilerParams(
            collective_id=collective, has_side_effects=True, vmem_limit_bytes=16 * 2**20
        ),
        cost_estimate=pl.CostEstimate(
            flops=35 * 10**9, bytes_accessed=dp_count * each * width * 4, transcendentals=0
        ),
    )(slab)
    return full.reshape(dp_count * each, width)


def line_gather_body(
    small, x_ref, out_ref, right_send, right_recv, left_send, left_recv
):
    rank = lax.axis_index("dp")
    depth = lax.axis_index("tensor")
    depths = lax.axis_size("tensor")
    last = depths - 1
    right, left = (rank, depth + 1), (rank, depth - 1)
    if small is None:
        greet_line(depth, last, rank)
    else:
        greet(small_peers())

    def to_right(step):
        src = x_ref if step == 0 else out_ref.at[depth - step]
        return send_to(
            src, out_ref.at[depth - step], right_send.at[step], right_recv.at[step], right
        )

    def to_left(step):
        src = x_ref if step == 0 else out_ref.at[depth + step]
        return send_to(src, out_ref.at[depth + step], left_send.at[step], left_recv.at[step], left)

    for step in range(last):

        @pl.when((depth < last) & (depth >= step))
        def _():
            to_right(step).start()

        @pl.when((depth > 0) & (depth + step <= last))
        def _():
            to_left(step).start()

        if step == 0:
            out_ref[depth] = x_ref[...]
            if small is not None:
                exchange_small(*small)

        @pl.when(depth - 1 >= step)
        def _():
            send_to(
                x_ref,
                out_ref.at[depth - 1 - step],
                right_send.at[step],
                right_recv.at[step],
                left,
            ).wait_recv()

        @pl.when(depth + 1 + step <= last)
        def _():
            send_to(
                x_ref, out_ref.at[depth + 1 + step], left_send.at[step], left_recv.at[step], right
            ).wait_recv()

    for step in range(last):

        @pl.when((depth < last) & (depth >= step))
        def _():
            to_right(step).wait_send()

        @pl.when((depth > 0) & (depth + step <= last))
        def _():
            to_left(step).wait_send()


def line_gather_kernel(x_ref, out_ref, *sems):
    line_gather_body(None, x_ref, out_ref, *sems)


def line_gather_small_kernel(
    x_ref, y_ref, out_ref, small_ref, pair, plane, line, pair_sems, plane_sems, line_sems, *sems
):
    small = (y_ref, small_ref, pair, plane, line, pair_sems, plane_sems, line_sems)
    line_gather_body(small, x_ref, out_ref, *sems)


def line_gather_small(block, small, collective):
    chips, depths = lax.axis_size("dp") // 2, lax.axis_size("tensor")
    rows, width = block.shape
    out, total = pl.pallas_call(
        line_gather_small_kernel,
        out_shape=(
            jax.ShapeDtypeStruct((depths, rows, width), block.dtype),
            jax.ShapeDtypeStruct(small.shape, jnp.float32),
        ),
        in_specs=[whole_vmem()] * 2,
        out_specs=(whole_vmem(), whole_vmem()),
        scratch_shapes=small_scratch(small.shape, chips, depths)
        + [pltpu.SemaphoreType.DMA((depths,))] * 4,
        compiler_params=pltpu.CompilerParams(
            collective_id=collective, has_side_effects=True, vmem_limit_bytes=16 * 2**20
        ),
        cost_estimate=pl.CostEstimate(
            flops=25 * 10**9, bytes_accessed=depths * rows * width * 4, transcendentals=0
        ),
    )(block, small)
    return out.reshape(depths * rows, width), total


def line_gather(block, collective):
    depths = lax.axis_size("tensor")
    rows, width = block.shape
    out = pl.pallas_call(
        line_gather_kernel,
        out_shape=jax.ShapeDtypeStruct((depths, rows, width), block.dtype),
        in_specs=[whole_vmem()],
        out_specs=whole_vmem(),
        scratch_shapes=[pltpu.SemaphoreType.DMA((depths,))] * 4,
        compiler_params=pltpu.CompilerParams(
            collective_id=collective, has_side_effects=True, vmem_limit_bytes=16 * 2**20
        ),
        cost_estimate=pl.CostEstimate(
            flops=25 * 10**9, bytes_accessed=depths * rows * width * 4, transcendentals=0
        ),
    )(block)
    return out.reshape(depths * rows, width)


def renew_kernel(widths, flips, gains, group_ref, map_ref, *refs):
    olds, news = refs[: len(widths)], refs[len(widths) :]
    keep_rate = 1.0 - MUON_RATE * MUON_DECAY
    offset = 0
    total = group_ref.shape[1]
    for width, flip, gain, old, new in zip(widths, flips, gains, olds, news):
        iterate_ref = group_ref
        if offset == total:
            iterate_ref, offset = map_ref, 0
        if flip:
            for first in range(0, width, 128):
                size = min(128, width - first)
                piece = iterate_ref[:, offset + first : offset + first + size]
                rows = slice(first, first + size)
                new[rows, :] = keep_rate * old[rows, :] - MUON_RATE * gain * (
                    piece.astype(jnp.float32).T
                )
        else:
            for first in range(0, old.shape[0], 128):
                rows = slice(first, first + 128)
                piece = iterate_ref[rows, offset : offset + width]
                new[rows, :] = keep_rate * old[rows, :] - MUON_RATE * gain * (
                    piece.astype(jnp.float32)
                )
        offset += width


def renew(iterate, map_iterate, olds, widths, flips, gains):
    return pl.pallas_call(
        functools.partial(renew_kernel, widths, flips, gains),
        out_shape=tuple(jax.ShapeDtypeStruct(old.shape, jnp.float32) for old in olds),
        in_specs=[whole_vmem()] * (2 + len(olds)),
        out_specs=tuple(whole_vmem() for _ in olds),
        compiler_params=pltpu.CompilerParams(vmem_limit_bytes=48 * 2**20),
        cost_estimate=pl.CostEstimate(
            flops=10**9, bytes_accessed=iterate.size * 10, transcendentals=0
        ),
    )(iterate, map_iterate, *olds)


HALF = 128


def greet_line(depth, last, rank):
    barrier = pltpu.get_barrier_semaphore()

    @pl.when(depth < last)
    def _():
        pl.semaphore_signal(
            barrier, inc=1, device_id=(rank, depth + 1), device_id_type=MESH_ID
        )

    @pl.when(depth > 0)
    def _():
        pl.semaphore_signal(
            barrier, inc=1, device_id=(rank, depth - 1), device_id_type=MESH_ID
        )

    @pl.when((depth > 0) & (depth < last))
    def _():
        pl.semaphore_wait(barrier, 2)

    @pl.when((depth == 0) | (depth == last))
    def _():
        pl.semaphore_wait(barrier, 1)


def line_mlp_kernel(
    x_ref,
    first_ref,
    second_ref,
    out_ref,
    rows,
    parts,
    from_left,
    from_right,
    stage,
    right_sems,
    left_sems,
    row_sems,
    sum_sems,
    from_left_sems,
    from_right_sems,
):
    rank = lax.axis_index("dp")
    depth = lax.axis_index("tensor")
    last = lax.axis_size("tensor") - 1
    right, left = (rank, depth + 1), (rank, depth - 1)
    greet_line(depth, last, rank)

    def rows_right(j, h):
        return send_to(rows.at[j, h], rows.at[j, h], right_sems.at[j, h], row_sems.at[j, h], right)

    def rows_left(j, h):
        return send_to(rows.at[j, h], rows.at[j, h], left_sems.at[j, h], row_sems.at[j, h], left)

    def sum_right(j, h):
        return send_to(
            stage.at[j, h], from_left.at[j, h], sum_sems.at[j, h], from_left_sems.at[j, h], right
        )

    def sum_left(j, h):
        return send_to(
            stage.at[j, h], from_right.at[j, h], sum_sems.at[j, h], from_right_sems.at[j, h], left
        )

    for h in range(2):
        rows[depth, h] = x_ref[h * HALF : (h + 1) * HALF, :]

        @pl.when(depth < last)
        def _():
            rows_right(depth, h).start()

        @pl.when(depth > 0)
        def _():
            rows_left(depth, h).start()

    inner = depth * (last - depth) // 2
    side = depth // 2
    for step, shift in enumerate((1, 1, -2, 0)):
        base = step + inner * shift
        j = base + side * (last - 2 * base)

        def half_step(h, carry):
            if step:

                @pl.when(j < depth)
                def _():
                    rows_right(j, h).wait_recv()

                @pl.when(j > depth)
                def _():
                    rows_left(j, h).wait_recv()

                @pl.when((j < depth) & (depth < last))
                def _():
                    rows_right(j, h).start()

                @pl.when((j > depth) & (depth > 0))
                def _():
                    rows_left(j, h).start()

            hidden = smooth_gelu(plain_dot(rows[j, h], first_ref[...])).astype(jnp.bfloat16)
            part = plain_dot(hidden, second_ref[...])
            parts[j, h] = part
            if step:

                @pl.when((depth == 0) | (depth == last))
                def _():
                    stage[j, h] = part.astype(jnp.bfloat16)

                @pl.when(depth == 0)
                def _():
                    sum_right(j, h).start()

                @pl.when(depth == last)
                def _():
                    sum_left(j, h).start()

            return carry

        lax.fori_loop(0, 2, half_step, 0)

    def relay_right(j):
        for h in range(2):
            sum_right(j, h).wait_recv()
            stage[j, h] = (parts[j, h] + from_left[j, h].astype(jnp.float32)).astype(jnp.bfloat16)
            sum_right(j, h).start()

    def relay_left(j):
        for h in range(2):
            sum_left(j, h).wait_recv()
            stage[j, h] = (parts[j, h] + from_right[j, h].astype(jnp.float32)).astype(jnp.bfloat16)
            sum_left(j, h).start()

    @pl.when(depth == 1)
    def _():
        relay_right(2)
        relay_right(3)
        relay_left(0)

    @pl.when(depth == 2)
    def _():
        relay_left(1)
        relay_left(0)
        relay_right(3)

    for h in range(2):
        span = slice(h * HALF, (h + 1) * HALF)
        out_ref[span, :] = parts[depth, h]

        @pl.when(depth > 0)
        def _():
            sum_right(depth, h).wait_recv()
            out_ref[span, :] += from_left[depth, h].astype(jnp.float32)

        @pl.when(depth < last)
        def _():
            sum_left(depth, h).wait_recv()
            out_ref[span, :] += from_right[depth, h].astype(jnp.float32)

    for j in range(4):
        for h in range(2):

            @pl.when((depth >= j) & (depth < last))
            def _():
                rows_right(j, h).wait_send()

            @pl.when((depth <= j) & (depth > 0))
            def _():
                rows_left(j, h).wait_send()

            @pl.when(depth < j)
            def _():
                sum_right(j, h).wait_send()

            @pl.when(depth > j)
            def _():
                sum_left(j, h).wait_send()


def line_mlp(block, first, second, collective):
    count, width = block.shape
    slots = (4, 2, HALF, width)
    return pl.pallas_call(
        line_mlp_kernel,
        out_shape=jax.ShapeDtypeStruct((count, width), jnp.float32),
        in_specs=[whole_vmem()] * 3,
        out_specs=whole_vmem(),
        scratch_shapes=[
            pltpu.VMEM(slots, jnp.bfloat16),
            pltpu.VMEM(slots, jnp.float32),
            pltpu.VMEM(slots, jnp.bfloat16),
            pltpu.VMEM(slots, jnp.bfloat16),
            pltpu.VMEM(slots, jnp.bfloat16),
        ]
        + [pltpu.SemaphoreType.DMA((4, 2))] * 6,
        compiler_params=pltpu.CompilerParams(
            collective_id=collective, has_side_effects=True, vmem_limit_bytes=48 * 2**20
        ),
        cost_estimate=pl.CostEstimate(
            flops=16 * count * width * first.shape[1] * 4,
            bytes_accessed=16 * count * width,
            transcendentals=4 * count * first.shape[1],
        ),
    )(block, first, second)


def share_gram_kernel(
    parts_ref, extra_ref, out_ref, line_in, pair_in, line_sems, pair_sems, plane_sems
):
    chips, chip, core, depth = place_of()
    depths = lax.axis_size("tensor")
    rank = chip * 2 + core
    sibling = (chip * 2 + 1 - core, depth)
    flat = [(lax.rem(chip + k, chips) * 2 + core, depth) for k in range(chips)]
    line = [lax.rem(depth + k, depths) for k in range(depths)]
    deep = [(rank, line[k]) for k in range(depths)]
    greet([sibling] + flat[1:] + deep[1:])
    copies = {}
    for k in range(1, depths):
        copies[k] = send_to(
            parts_ref.at[line[k]], line_in.at[k], line_sems.at[0, k], line_sems.at[1, k], deep[k]
        )
        copies[k].start()
    extra = send_to(extra_ref, out_ref.at[rank], pair_sems.at[0], pair_sems.at[1], sibling)
    main = send_to(pair_in, out_ref.at[rank], pair_sems.at[2], pair_sems.at[3], sibling)
    plane = {}
    for k in range(1, chips):
        plane[k] = [
            send_to(
                out_ref.at[chip * 2 + i],
                out_ref.at[chip * 2 + i],
                plane_sems.at[0, i, k],
                plane_sems.at[1, i, k],
                flat[k],
            )
            for i in range(2)
        ]

    @pl.when(core == 0)
    def _():
        extra.start()

    @pl.when(core == 1)
    def _():
        out_ref[rank] = extra_ref[...]
        extra.wait_recv()
        for k in range(1, chips):
            for i in range(2):
                plane[k][i].start()

    value = parts_ref[depth]
    for k in range(1, depths):
        copies[k].wait_recv()
        value = value + line_in[k]

    @pl.when(core == 1)
    def _():
        pair_in[...] = value
        main.start()

    @pl.when(core == 0)
    def _():
        out_ref[rank] = value
        main.wait_recv()
        for k in range(1, chips):
            for i in range(2):
                plane[k][i].start()

    for k in range(1, chips):
        for i in range(2):
            plane[k][i].wait_recv()
    for k in range(1, chips):
        for i in range(2):
            plane[k][i].wait_send()
    for k in range(1, depths):
        copies[k].wait_send()

    @pl.when(core == 0)
    def _():
        extra.wait_send()

    @pl.when(core == 1)
    def _():
        main.wait_send()


def share_gram(parts, extra, collective):
    dp_count, depths = lax.axis_size("dp"), lax.axis_size("tensor")
    chips = dp_count // 2
    slab = extra.shape
    out = pl.pallas_call(
        share_gram_kernel,
        out_shape=jax.ShapeDtypeStruct((dp_count,) + slab, jnp.float32),
        in_specs=[whole_vmem()] * 2,
        out_specs=whole_vmem(),
        scratch_shapes=[
            pltpu.VMEM((depths,) + slab, jnp.float32),
            pltpu.VMEM(slab, jnp.float32),
            pltpu.SemaphoreType.DMA((2, depths)),
            pltpu.SemaphoreType.DMA((4,)),
            pltpu.SemaphoreType.DMA((2, 2, chips)),
        ],
        compiler_params=pltpu.CompilerParams(
            collective_id=collective, has_side_effects=True, vmem_limit_bytes=16 * 2**20
        ),
        cost_estimate=pl.CostEstimate(
            flops=45 * 10**9, bytes_accessed=dp_count * slab[0] * slab[1] * 8, transcendentals=0
        ),
    )(parts.reshape((depths,) + slab), extra)
    return out.reshape(dp_count * slab[0], slab[1])


def line_exchange_kernel(
    heads_ref,
    weight_ref,
    x_ref,
    sum_ref,
    all_ref,
    y_ref,
    from_left,
    from_right,
    stage,
    right_sems,
    left_sems,
    row_sems,
    sum_sems,
    from_left_sems,
    from_right_sems,
):
    rank = lax.axis_index("dp")
    depth = lax.axis_index("tensor")
    last = lax.axis_size("tensor") - 1
    right, left = (rank, depth + 1), (rank, depth - 1)
    greet_line(depth, last, rank)

    def rows_right(j):
        return send_to(all_ref.at[j], all_ref.at[j], right_sems.at[j], row_sems.at[j], right)

    def rows_left(j):
        return send_to(all_ref.at[j], all_ref.at[j], left_sems.at[j], row_sems.at[j], left)

    def sum_right(j, h, src):
        return send_to(
            src.at[j, h], from_left.at[j, h], sum_sems.at[j, h], from_left_sems.at[j, h], right
        )

    def sum_left(j, h, src):
        return send_to(
            src.at[j, h], from_right.at[j, h], sum_sems.at[j, h], from_right_sems.at[j, h], left
        )

    all_ref[depth] = x_ref[...]

    @pl.when(depth < last)
    def _():
        rows_right(depth).start()

    @pl.when(depth > 0)
    def _():
        rows_left(depth).start()

    for j in range(4):
        for h in range(2):
            first = (2 * j + h) * HALF
            y_ref[j, h] = plain_dot(
                heads_ref[first : first + HALF, :], weight_ref[...]
            ).astype(jnp.bfloat16)

    @pl.when(depth == 0)
    def _():
        for j in (3, 2, 1):
            for h in range(2):
                sum_right(j, h, y_ref).start()
        for j in (1, 2, 3):
            rows_left(j).wait_recv()

    @pl.when(depth == last)
    def _():
        for j in (0, 1, 2):
            for h in range(2):
                sum_left(j, h, y_ref).start()
        for j in (2, 1, 0):
            rows_right(j).wait_recv()

    def relay_right(j):
        for h in range(2):
            sum_right(j, h, stage).wait_recv()
            stage[j, h] = (
                y_ref[j, h].astype(jnp.float32) + from_left[j, h].astype(jnp.float32)
            ).astype(jnp.bfloat16)
            sum_right(j, h, stage).start()

    def relay_left(j):
        for h in range(2):
            sum_left(j, h, stage).wait_recv()
            stage[j, h] = (
                y_ref[j, h].astype(jnp.float32) + from_right[j, h].astype(jnp.float32)
            ).astype(jnp.bfloat16)
            sum_left(j, h, stage).start()

    def pass_right(j):
        rows_right(j).wait_recv()
        rows_right(j).start()

    def pass_left(j):
        rows_left(j).wait_recv()
        rows_left(j).start()

    @pl.when(depth == 1)
    def _():
        pass_left(2)
        pass_right(0)
        relay_right(3)
        pass_left(3)
        relay_left(0)
        relay_right(2)

    @pl.when(depth == 2)
    def _():
        pass_right(1)
        pass_left(3)
        relay_left(0)
        pass_right(0)
        relay_right(3)
        relay_left(1)

    for h in range(2):
        span = slice(h * HALF, (h + 1) * HALF)
        sum_ref[span, :] = y_ref[depth, h].astype(jnp.float32)

        @pl.when(depth > 0)
        def _():
            sum_right(depth, h, stage).wait_recv()
            sum_ref[span, :] += from_left[depth, h].astype(jnp.float32)

        @pl.when(depth < last)
        def _():
            sum_left(depth, h, stage).wait_recv()
            sum_ref[span, :] += from_right[depth, h].astype(jnp.float32)

    for j in range(4):

        @pl.when((depth >= j) & (depth < last))
        def _():
            rows_right(j).wait_send()

        @pl.when((depth <= j) & (depth > 0))
        def _():
            rows_left(j).wait_send()

        for h in range(2):

            @pl.when(depth < j)
            def _():
                sum_right(j, h, stage).wait_send()

            @pl.when(depth > j)
            def _():
                sum_left(j, h, stage).wait_send()


def line_exchange(heads, weight, block, collective):
    width = weight.shape[1]
    slots = (4, 2, HALF, width)
    total, rows = pl.pallas_call(
        line_exchange_kernel,
        out_shape=(
            jax.ShapeDtypeStruct((2 * HALF, width), jnp.float32),
            jax.ShapeDtypeStruct((4,) + block.shape, block.dtype),
        ),
        in_specs=[whole_vmem()] * 3,
        out_specs=(whole_vmem(), whole_vmem()),
        scratch_shapes=[pltpu.VMEM(slots, jnp.bfloat16)] * 4
        + [pltpu.SemaphoreType.DMA((4,))] * 3
        + [pltpu.SemaphoreType.DMA((4, 2))] * 3,
        compiler_params=pltpu.CompilerParams(
            collective_id=collective, has_side_effects=True, vmem_limit_bytes=32 * 2**20
        ),
        cost_estimate=pl.CostEstimate(
            flops=60 * 10**9, bytes_accessed=heads.size * 16, transcendentals=0
        ),
    )(heads, weight, block)
    return total, rows.reshape(-1, block.shape[1])


NBLK = 256


def split_store(value, high_ref, low_ref, rows, cols):
    high = value.astype(jnp.bfloat16)
    high_ref[rows, cols] = high
    low_ref[rows, cols] = (value - high.astype(jnp.float32)).astype(jnp.bfloat16)


def polynomial_kernel(gram_ref, out_ref, full_g, full_h, full_m, *pairs):
    gram_pair, half_pair, poly_pair, prod_pair = (
        pairs[0:2], pairs[2:4], pairs[4:6], pairs[6:8]
    )
    size = gram_ref.shape[0]
    blocks = size // NBLK
    spans = [slice(i * NBLK, (i + 1) * NBLK) for i in range(blocks)]
    upper = [(i, j) for i in range(blocks) for j in range(i, blocks)]

    def eye(i, j):
        if i != j:
            return 0.0
        row = lax.broadcasted_iota(jnp.int32, (NBLK, NBLK), 0)
        col = lax.broadcasted_iota(jnp.int32, (NBLK, NBLK), 1)
        return jnp.where(row == col, 1.0, 0.0)

    def place(i, j, value, full, pair):
        if full is not None:
            full[spans[i], spans[j]] = value
        if pair is not None:
            split_store(value, *pair, spans[i], spans[j])
        if i != j:
            flip = value.T
            if full is not None:
                full[spans[j], spans[i]] = flip
            if pair is not None:
                split_store(flip, *pair, spans[j], spans[i])

    def product(left, right, i, j):
        return plain_dot(left[0][spans[i], :], right[0][:, spans[j]]) + (
            plain_dot(left[0][spans[i], :], right[1][:, spans[j]])
            + plain_dot(left[1][spans[i], :], right[0][:, spans[j]])
        )

    trace = 0.0
    for i in range(blocks):
        trace = trace + jnp.sum(gram_ref[spans[i], spans[i]] * eye(i, i))
    root = jnp.sqrt(jnp.full((1, 1), trace, jnp.float32)) + 1e-07
    inverse = 1.0 / root
    for i, j in upper:
        place(i, j, gram_ref[spans[i], spans[j]] * (inverse * inverse), full_g, gram_pair)

    def make_poly():
        for i, j in upper:
            value = NS_B * full_g[spans[i], spans[j]] + NS_C * product(gram_pair, gram_pair, i, j)
            place(i, j, value, None, poly_pair)

    def advance():
        for i, j in upper:
            value = NS_A * full_g[spans[i], spans[j]] + product(poly_pair, gram_pair, i, j)
            place(i, j, value, full_h, half_pair)
        for i, j in upper:
            value = NS_A * full_h[spans[i], spans[j]] + product(poly_pair, half_pair, i, j)
            place(i, j, value, full_g, gram_pair)

    make_poly()
    for i, j in upper:
        value = (
            poly_pair[0][spans[i], spans[j]].astype(jnp.float32)
            + poly_pair[1][spans[i], spans[j]].astype(jnp.float32)
            + NS_A * eye(i, j)
        )
        place(i, j, value, full_m, prod_pair)
    advance()

    def sweep(index, carry):
        make_poly()
        for i, j in upper:
            value = NS_A * full_m[spans[i], spans[j]] + product(poly_pair, prod_pair, i, j)
            place(i, j, value, full_h, None)
        for i in range(blocks):
            full_m[spans[i], :] = full_h[spans[i], :]
            split_store(full_h[spans[i], :], *prod_pair, spans[i], slice(None))
        advance()
        return carry

    lax.fori_loop(0, 3, sweep, 0)
    make_poly()
    for i, j in upper:
        value = NS_A * full_m[spans[i], spans[j]] + product(poly_pair, prod_pair, i, j)
        place(i, j, value * inverse, out_ref, None)


def orthogonal_factor(gram_mat):
    size = gram_mat.shape[0]
    return pl.pallas_call(
        polynomial_kernel,
        out_shape=jax.ShapeDtypeStruct((size, size), jnp.float32),
        in_specs=[whole_vmem()],
        out_specs=whole_vmem(),
        scratch_shapes=[pltpu.VMEM((size, size), jnp.float32)] * 3
        + [pltpu.VMEM((size, size), jnp.bfloat16)] * 8,
        compiler_params=pltpu.CompilerParams(vmem_limit_bytes=48 * 2**20),
        cost_estimate=pl.CostEstimate(
            flops=17 * 2 * 2 * size**3, bytes_accessed=8 * size * size, transcendentals=0
        ),
    )(gram_mat)


def contract_rows(left, right):
    return lax.dot_general(
        left, right, (((0,), (0,)), ((), ())), preferred_element_type=jnp.float32
    )


def contract_cols(left, right):
    return lax.dot_general(
        left, right, (((1,), (1,)), ((), ())), preferred_element_type=jnp.float32
    )


def body(
    teacher_in,
    student_in,
    resp_mask,
    replay,
    t_gains,
    t_shifts,
    t_qkv,
    t_out,
    t_fc,
    t_proj,
    s_norms,
    s_qkv,
    s_out,
    s_fc,
    s_proj,
    s_map,
    mom_qkv,
    mom_out,
    mom_fc,
    mom_proj,
    mom_map,
    adam_first,
    adam_second,
):
    groups = lax.axis_size("tensor")
    tensor_rank = lax.axis_index("tensor")
    row_count = student_in.shape[0]
    seq_count = replay.shape[0]
    total_rows = row_count * groups
    count_block = jnp.full((8, 128), jnp.sum(resp_mask), jnp.int32).astype(jnp.float32)
    tokens_all = lax.axis_size("dp") * seq_count * LEN

    def teacher_gather(local_rows):
        return lax.all_gather(local_rows, "tensor", axis=0, tiled=True)

    def student_gather(local_rows):
        return lax.all_gather(local_rows, "tensor", axis=0, tiled=True)

    def student_reduce(left, right, right_dim):
        return lax.psum_scatter(
            lax.dot_general(
                left, right, (((1,), (right_dim,)), ((), ())), preferred_element_type=jnp.float32
            ).astype(jnp.bfloat16),
            "tensor",
            scatter_dimension=0,
            tiled=True,
        ).astype(jnp.float32)

    teacher_x = teacher_in.astype(jnp.float32)
    slot_width = t_qkv.shape[2]
    slot_count = slot_width // HEAD
    live_count = HT // groups + (tensor_rank < HT % groups).astype(jnp.int32)
    live_slots = (jnp.arange(slot_count, dtype=jnp.int32) < live_count).astype(jnp.float32)
    teacher_normed = norm_parts(teacher_x, t_gains[0], t_shifts[0])[0].astype(jnp.bfloat16)
    teacher_all = teacher_gather(teacher_normed)
    student_x = student_in.astype(jnp.float32)
    shard_width = s_qkv.shape[2]
    shard_hidden = s_fc.shape[1]
    head_count = shard_width // HEAD
    w_qkv = s_qkv.astype(jnp.bfloat16).reshape(DS, 3 * shard_width)
    w_out = s_out.astype(jnp.bfloat16)
    w_fc = s_fc.astype(jnp.bfloat16)
    w_proj = s_proj.astype(jnp.bfloat16)
    w_map = s_map.astype(jnp.bfloat16)
    normed_one, unit_one, scale_one = norm_parts(student_x, s_norms[0], s_norms[1])
    low_one = normed_one.astype(jnp.bfloat16)
    rows_one, count_sum = line_gather_small(low_one, count_block, 5)
    count_val = count_sum[0, 0]
    factor = tokens_all / (2.0 * count_val)
    mixed_qkv = jnp.dot(rows_one, w_qkv, preferred_element_type=jnp.float32).astype(jnp.bfloat16)
    head_out, log_sums = attend_forward(mixed_qkv, head_count)
    teacher_all, head_out = lax.optimization_barrier((teacher_all, head_out))
    resid = student_x + student_reduce(head_out, w_out, 0)
    teacher_mixed = jnp.dot(
        teacher_all, t_qkv.reshape(DT, 3 * slot_width), preferred_element_type=jnp.float32
    ).astype(jnp.bfloat16)
    teacher_head_out = attend_forward(teacher_mixed, slot_count)[0]
    slot_mask = jnp.repeat(live_slots, HEAD)[None, :] > 0.0
    teacher_head_out = jnp.where(slot_mask, teacher_head_out, jnp.zeros_like(teacher_head_out))
    normed_two, unit_two, scale_two = norm_parts(resid, s_norms[2], s_norms[3])
    low_two = normed_two.astype(jnp.bfloat16)
    attn_part, rows_two = line_exchange(teacher_head_out, t_out, low_two, 6)
    teacher_resid = teacher_x + attn_part
    teacher_normed_two = norm_parts(teacher_resid, t_gains[1], t_shifts[1])[0].astype(jnp.bfloat16)
    mlp_part = line_mlp(teacher_normed_two, t_fc, t_proj, 8)
    teacher_out = (teacher_resid + mlp_part).astype(jnp.bfloat16)
    before = jnp.dot(rows_two, w_fc, preferred_element_type=jnp.float32)
    before, hidden = (before, smooth_gelu(before).astype(jnp.bfloat16))
    output = resid + student_reduce(hidden, w_proj, 0)
    student_out = output.astype(jnp.bfloat16)
    guess_vec = jnp.dot(student_out, w_map, preferred_element_type=jnp.float32)
    miss_vec = guess_vec - teacher_out.astype(jnp.float32)
    position = tensor_rank * row_count + jnp.arange(row_count, dtype=jnp.int32)
    seq_owner = position // LEN
    seq_pick = (seq_owner[:, None] == jnp.arange(seq_count, dtype=jnp.int32)[None, :]).astype(
        jnp.float32
    )
    flag_tok = jnp.sum(seq_pick * replay.astype(jnp.float32)[None, :], axis=1)
    weight = resp_mask.astype(jnp.float32) * (1.0 - REPLAY_CUT * flag_tok)
    loss_part = jnp.sum(weight[:, None] * miss_vec * miss_vec)
    grad_guess = (2.0 * factor * weight[:, None] * miss_vec).astype(jnp.bfloat16)
    row_unit = 8 * lax.axis_size("dp") * groups
    map_slab = scatter_rows(pad_rows(contract_rows(grad_guess, student_out), row_unit), 1)
    grad_output = contract_cols(grad_guess, w_map)
    rows_two_back, before_back, hidden_back = (rows_two, before, hidden)
    rows_one_back, mixed_back, heads_back, logs_back = (rows_one, mixed_qkv, head_out, log_sums)
    grad_mlp = student_gather(grad_output.astype(jnp.bfloat16))
    grad_mlp, map_slab = lax.optimization_barrier((grad_mlp, map_slab))
    grad_proj = contract_rows(hidden_back, grad_mlp)
    grad_hidden = contract_cols(grad_mlp, w_proj)
    gelu_vals, gelu_pull = jax.vjp(smooth_gelu, before_back)
    grad_before = gelu_pull(grad_hidden)[0].astype(jnp.bfloat16)
    grad_fc = contract_rows(rows_two_back, grad_before).reshape(-1, DS)
    mlp_slab = scatter_rows(jnp.concatenate([grad_proj, grad_fc], axis=0), 2)
    grad_normed_two = student_reduce(grad_before, w_fc, 1)
    grad_normed_two, mlp_slab = lax.optimization_barrier((grad_normed_two, mlp_slab))
    grad_resid = grad_output + norm_back(grad_normed_two, unit_two, scale_two, s_norms[2])
    grad_attn = student_gather(grad_resid.astype(jnp.bfloat16))
    grad_mlp_rows = spread(mlp_slab, 7)
    grad_attn, grad_mlp_rows = lax.optimization_barrier((grad_attn, grad_mlp_rows))
    grad_proj, grad_fc = grad_mlp_rows[:shard_hidden], grad_mlp_rows[shard_hidden:]
    grad_out = contract_rows(heads_back, grad_attn)
    grad_heads = contract_cols(grad_attn, w_out).astype(jnp.bfloat16)

    grad_mixed = attend_backward(mixed_back, logs_back, grad_heads, head_count)
    grad_qkv = contract_rows(grad_mixed, rows_one_back)
    grad_attn_rows, grad_map = sum_and_spread(
        jnp.concatenate([grad_out, grad_qkv], axis=0), map_slab, 3
    )
    grad_map = grad_map[:DT]
    grad_out, grad_qkv = grad_attn_rows[:shard_width], grad_attn_rows[shard_width:]
    grad_fc = grad_fc.reshape(DS, shard_hidden)
    def to_tall(mat):
        return mat.transpose(1, 2, 0).reshape(-1, DS)

    def from_tall(mat):
        return mat.reshape(3, shard_width, DS).transpose(2, 0, 1)

    moments = [
        MOMENTUM * to_tall(mom_qkv) + grad_qkv,
        MOMENTUM * mom_out + grad_out,
        MOMENTUM * mom_fc + grad_fc,
        MOMENTUM * mom_proj + grad_proj,
    ]
    moment_map = MOMENTUM * mom_map.T + grad_map
    dp_count = lax.axis_size("dp")
    dp_rank = lax.axis_index("dp")
    slice_rows = DS // dp_count
    first_row = dp_rank * slice_rows
    talls = [moments[0], moments[1], moments[2], moments[3], moment_map]
    sums = [0, 0, 1, 0, 0]

    def gram_rows(tall, axis):
        return lax.dot_general(
            lax.dynamic_slice_in_dim(tall, first_row, slice_rows, 1 - axis),
            tall,
            (((axis,), (axis,)), ((), ())),
            precision=HIGH,
            preferred_element_type=jnp.float32,
        )

    parts = jnp.concatenate([gram_rows(talls[i], sums[i]) for i in range(4)], axis=0)
    gram_mat = share_gram(parts, gram_rows(talls[4], sums[4]), 9)
    gram_mat, grad_mixed = lax.optimization_barrier((gram_mat, grad_mixed))
    grad_normed_one = student_reduce(grad_mixed, w_qkv, 1)
    mine = dp_rank % 2
    factor_mat = orthogonal_factor(gram_mat)
    pair_rows = lax.dynamic_slice_in_dim(factor_mat, (dp_rank // 2) * 2 * slice_rows, 2 * slice_rows, 0)
    other_rows = lax.ppermute(
        pair_rows, "dp", [(i, i ^ 1) for i in range(dp_count)]
    )
    even_rows = jnp.where(mine == 0, pair_rows, other_rows)
    odd_rows = jnp.where(mine == 0, other_rows, pair_rows)
    even_rows = lax.dynamic_slice_in_dim(even_rows, mine * slice_rows, slice_rows, 0)
    odd_rows = lax.dynamic_slice_in_dim(odd_rows, mine * slice_rows, slice_rows, 0)
    even_rows, grad_normed_one = lax.optimization_barrier((even_rows, grad_normed_one))
    factor_rows = line_gather(even_rows, 10).reshape(groups, slice_rows, DS)
    input_grad = grad_resid + norm_back(grad_normed_one, unit_one, scale_one, s_norms[0])
    norm_grads = jnp.stack(
        [
            jnp.sum(grad_normed_one * unit_one, axis=0),
            jnp.sum(grad_normed_one, axis=0),
            jnp.sum(grad_normed_two * unit_two, axis=0),
            jnp.sum(grad_normed_two, axis=0),
        ]
    )
    small = jnp.concatenate(
        [norm_grads, jnp.full((4, DS), loss_part, jnp.float32)], axis=0
    )
    small = sum_small(small, 4)
    norm_grads = small[:4]
    loss = small[4, 0] / (count_val * DT)

    def piece_of(index, rows):
        return lax.dot_general(
            rows,
            talls[index],
            (((1,), (1 - sums[index],)), ((), ())),
            precision=lax.Precision.HIGH,
            preferred_element_type=jnp.float32,
        ).astype(jnp.bfloat16)

    map_all = lax.all_gather(piece_of(4, odd_rows), "dp", axis=0, tiled=True)
    pieces = [piece_of(i, factor_rows[i]) for i in (2, 3, 1, 0)]
    iterate_all = lax.all_gather(jnp.concatenate(pieces, axis=1), "dp", axis=0, tiled=True)
    weight_fc, weight_proj, weight_out, weight_qkv, weight_map = renew(
        iterate_all,
        map_all,
        (s_fc, s_proj, s_out, to_tall(s_qkv), s_map.T),
        [piece.shape[1] for piece in pieces] + [DT],
        [False, True, True, True, True],
        [math.sqrt(FS / DS), 1.0, 1.0, math.sqrt(3.0), math.sqrt(DT / DS)],
    )
    norm_first = BETA_ONE * adam_first + (1.0 - BETA_ONE) * norm_grads
    norm_second = BETA_TWO * adam_second + (1.0 - BETA_TWO) * norm_grads * norm_grads
    fix_one = 1.0 - BETA_ONE**STEP
    fix_two = 1.0 - BETA_TWO**STEP
    norm_values = s_norms - ADAM_RATE * (
        norm_first / fix_one / (jnp.sqrt(norm_second / fix_two) + ADAM_EPS) + ADAM_DECAY * s_norms
    )
    return (
        teacher_out,
        student_out,
        input_grad,
        loss,
        from_tall(grad_qkv),
        grad_out,
        grad_fc,
        grad_proj,
        grad_map.T,
        from_tall(moments[0]),
        moments[1],
        moments[2],
        moments[3],
        moment_map.T,
        from_tall(weight_qkv),
        weight_out,
        weight_fc,
        weight_proj,
        weight_map.T,
        norm_first,
        norm_second,
        norm_values,
    )


def solution(mesh):
    return jax.shard_map(
        body,
        mesh=mesh,
        in_specs=(
            P(("dp", "tensor"), None),
            P(("dp", "tensor"), None),
            P(("dp", "tensor")),
            P("dp"),
            P(),
            P(),
            P(None, None, "tensor"),
            P("tensor", None),
            P(None, "tensor"),
            P("tensor", None),
            P(),
            P(None, None, "tensor"),
            P("tensor", None),
            P(None, "tensor"),
            P("tensor", None),
            P(),
            P(None, None, "tensor"),
            P("tensor", None),
            P(None, "tensor"),
            P("tensor", None),
            P(),
            P(),
            P(),
        ),
        out_specs=(
            P(("dp", "tensor"), None),
            P(("dp", "tensor"), None),
            P(("dp", "tensor"), None),
            P(),
            P(None, None, "tensor"),
            P("tensor", None),
            P(None, "tensor"),
            P("tensor", None),
            P(),
            P(None, None, "tensor"),
            P("tensor", None),
            P(None, "tensor"),
            P("tensor", None),
            P(),
            P(None, None, "tensor"),
            P("tensor", None),
            P(None, "tensor"),
            P("tensor", None),
            P(),
            P(),
            P(),
            P(),
        ),
        check_vma=False,
    )
```

```python
import functools
import math

import jax
import jax.numpy as jnp
from jax import lax
from jax.experimental import pallas as pl
from jax.experimental.pallas import tpu as pltpu
from jax.sharding import PartitionSpec as P

DT = 1600
HT = 25
DS = 768
FS = 3072
HEAD = 64
LEN = 1024
STEP = 10
ABLK = 256


EPS = 1e-05
NS_A = 3.4445
NS_B = -4.775
NS_C = 2.0315
MOMENTUM = 0.95
MUON_RATE = 0.5
MUON_DECAY = 0.01
ADAM_RATE = 0.3
BETA_ONE = 0.9
BETA_TWO = 0.999
ADAM_EPS = 1e-08
ADAM_DECAY = 0.01
REPLAY_CUT = 0.5
NEG_FILL = -1e30
HIGH = lax.Precision.HIGHEST


def norm_parts(v, gain_vec, shift_vec):
    row_mean = jnp.mean(v, axis=-1, keepdims=True)
    centred = v - row_mean
    row_var = jnp.mean(centred * centred, axis=-1, keepdims=True)
    inv_scale = lax.rsqrt(row_var + EPS)
    unit_val = centred * inv_scale
    return (unit_val * gain_vec + shift_vec, unit_val, inv_scale)


def norm_back(grad_norm, unit_val, inv_scale, gain_vec):
    grad_unit = grad_norm * gain_vec
    first_mean = jnp.mean(grad_unit, axis=-1, keepdims=True)
    second_mean = jnp.mean(grad_unit * unit_val, axis=-1, keepdims=True)
    return inv_scale * (grad_unit - first_mean - unit_val * second_mean)


def smooth_gelu(v):
    return 0.5 * v * (1.0 + jnp.tanh(0.7978845608028654 * (v + 0.044715 * v * v * v)))


def whole_vmem():
    return pl.BlockSpec(memory_space=pltpu.VMEM)


def nt_dot(left, right):
    return lax.dot_general(
        left, right, (((1,), (1,)), ((), ())), preferred_element_type=jnp.float32
    )


def tn_dot(left, right):
    return lax.dot_general(
        left, right, (((0,), (0,)), ((), ())), preferred_element_type=jnp.float32
    )


def plain_dot(left, right):
    return jnp.dot(left, right, preferred_element_type=jnp.float32)


def lower_mask():
    row_pos = lax.broadcasted_iota(jnp.int32, (ABLK, ABLK), 0)
    key_pos = lax.broadcasted_iota(jnp.int32, (ABLK, ABLK), 1)
    return key_pos <= row_pos


def attend_forward_kernel(head_count, qkv_ref, out_ref, log_ref):
    width = head_count * HEAD
    for head in range(head_count):
        cols = slice(head * HEAD, (head + 1) * HEAD)
        keys = qkv_ref[:, width + head * HEAD : width + (head + 1) * HEAD]
        values = qkv_ref[:, 2 * width + head * HEAD : 2 * width + (head + 1) * HEAD]
        for block in range(LEN // ABLK):
            low, high = block * ABLK, (block + 1) * ABLK
            query = qkv_ref[low:high, cols]
            near = nt_dot(query, keys[low:high]) * HEAD ** (-0.5)
            near = jnp.where(lower_mask(), near, NEG_FILL)
            row_top = jnp.max(near, axis=-1, keepdims=True)
            if block:
                far = nt_dot(query, keys[:low]) * HEAD ** (-0.5)
                row_top = jnp.maximum(row_top, jnp.max(far, axis=-1, keepdims=True))
            near = jnp.exp(near - row_top)
            row_total = jnp.sum(near, axis=-1, keepdims=True)
            if block:
                far = jnp.exp(far - row_top)
                row_total = row_total + jnp.sum(far, axis=-1, keepdims=True)
            inverse = 1.0 / row_total
            mixed = plain_dot((near * inverse).astype(jnp.bfloat16), values[low:high])
            if block:
                mixed = mixed + plain_dot((far * inverse).astype(jnp.bfloat16), values[:low])
            out_ref[low:high, cols] = mixed.astype(out_ref.dtype)
            log_ref[low:high, head : head + 1] = row_top + jnp.log(row_total)


def attend_forward(mixed_qkv, head_count):
    width = head_count * HEAD
    return pl.pallas_call(
        functools.partial(attend_forward_kernel, head_count),
        out_shape=(
            jax.ShapeDtypeStruct((LEN, width), jnp.bfloat16),
            jax.ShapeDtypeStruct((LEN, 128), jnp.float32),
        ),
        in_specs=[whole_vmem()],
        out_specs=(whole_vmem(), whole_vmem()),
        compiler_params=pltpu.CompilerParams(vmem_limit_bytes=40 * 2**20),
        cost_estimate=pl.CostEstimate(
            flops=4 * head_count * LEN * LEN * HEAD * 4,
            bytes_accessed=LEN * width * 8,
            transcendentals=head_count * LEN * LEN // 2,
        ),
    )(mixed_qkv)


def attend_backward_kernel(
    head_count, qkv_ref, log_ref, grad_ref, out_ref, key_acc, value_acc
):
    width = head_count * HEAD
    scale = HEAD ** (-0.5)
    for head in range(head_count):
        cols = slice(head * HEAD, (head + 1) * HEAD)
        key_cols = slice(width + head * HEAD, width + (head + 1) * HEAD)
        value_cols = slice(2 * width + head * HEAD, 2 * width + (head + 1) * HEAD)
        keys = qkv_ref[:, key_cols]
        values = qkv_ref[:, value_cols]
        for block in range(LEN // ABLK - 1, -1, -1):
            low, high = block * ABLK, (block + 1) * ABLK
            query = qkv_ref[low:high, cols]
            grad = grad_ref[low:high, cols]
            log_sum = log_ref[low:high, head : head + 1]
            near = nt_dot(query, keys[low:high]) * scale
            near = jnp.exp(jnp.where(lower_mask(), near, NEG_FILL) - log_sum)
            near_back = nt_dot(grad, values[low:high])
            inner = jnp.sum(near * near_back, axis=-1, keepdims=True)
            if block:
                far = jnp.exp(nt_dot(query, keys[:low]) * scale - log_sum)
                far_back = nt_dot(grad, values[:low])
                inner = inner + jnp.sum(far * far_back, axis=-1, keepdims=True)
            near_score = (near * (near_back - inner)).astype(jnp.bfloat16)
            grad_query = plain_dot(near_score, keys[low:high])
            near_key = tn_dot(near_score, query)
            near_value = tn_dot(near.astype(jnp.bfloat16), grad)
            if block == LEN // ABLK - 1:
                key_acc[low:high, :] = near_key
                value_acc[low:high, :] = near_value
            else:
                key_acc[low:high, :] += near_key
                value_acc[low:high, :] += near_value
            if block:
                far_score = (far * (far_back - inner)).astype(jnp.bfloat16)
                grad_query = grad_query + plain_dot(far_score, keys[:low])
                far_key = tn_dot(far_score, query)
                far_value = tn_dot(far.astype(jnp.bfloat16), grad)
                if block == LEN // ABLK - 1:
                    key_acc[:low, :] = far_key
                    value_acc[:low, :] = far_value
                else:
                    key_acc[:low, :] += far_key
                    value_acc[:low, :] += far_value
            out_ref[low:high, cols] = (grad_query * scale).astype(jnp.bfloat16)
        out_ref[:, key_cols] = (key_acc[...] * scale).astype(jnp.bfloat16)
        out_ref[:, value_cols] = value_acc[...].astype(jnp.bfloat16)


def attend_backward(mixed_qkv, log_sums, grad_heads, head_count):
    width = head_count * HEAD
    return pl.pallas_call(
        functools.partial(attend_backward_kernel, head_count),
        out_shape=jax.ShapeDtypeStruct((LEN, 3 * width), jnp.bfloat16),
        in_specs=[whole_vmem()] * 3,
        out_specs=whole_vmem(),
        scratch_shapes=[pltpu.VMEM((LEN, HEAD), jnp.float32)] * 2,
        compiler_params=pltpu.CompilerParams(vmem_limit_bytes=40 * 2**20),
        cost_estimate=pl.CostEstimate(
            flops=10 * head_count * LEN * LEN * HEAD * 4,
            bytes_accessed=LEN * width * 16,
            transcendentals=head_count * LEN * LEN // 2,
        ),
    )(mixed_qkv, log_sums, grad_heads)


MESH_ID = pl.DeviceIdType.MESH


def place_of():
    dp_count = lax.axis_size("dp")
    rank = lax.axis_index("dp")
    return dp_count // 2, rank // 2, rank % 2, lax.axis_index("tensor")


def greet(peers):
    barrier = pltpu.get_barrier_semaphore()
    for peer in peers:
        pl.semaphore_signal(barrier, inc=1, device_id=peer, device_id_type=MESH_ID)
    pl.semaphore_wait(barrier, len(peers))


def send_to(src, dst, send_sem, recv_sem, peer):
    return pltpu.make_async_remote_copy(
        src_ref=src,
        dst_ref=dst,
        send_sem=send_sem,
        recv_sem=recv_sem,
        device_id=peer,
        device_id_type=MESH_ID,
    )


def small_peers():
    chips, chip, core, depth = place_of()
    depths = lax.axis_size("tensor")
    flat = [((lax.rem(chip + k, chips)) * 2 + core, depth) for k in range(1, chips)]
    deep = [(chip * 2 + core, lax.rem(depth + k, depths)) for k in range(1, depths)]
    return [(chip * 2 + 1 - core, depth)] + flat + deep


def exchange_small(
    x_ref, out_ref, pair, plane, line, pair_sems, plane_sems, line_sems
):
    chips, chip, core, depth = place_of()
    depths = lax.axis_size("tensor")
    sibling = (chip * 2 + 1 - core, depth)
    flat = [((lax.rem(chip + k, chips)) * 2 + core, depth) for k in range(1, chips)]
    deep = [(chip * 2 + core, lax.rem(depth + k, depths)) for k in range(1, depths)]
    copy = send_to(x_ref, pair, pair_sems.at[0], pair_sems.at[1], sibling)
    copy.start()
    copy.wait()
    plane[chip] = x_ref[...] + pair[...]
    copies = []
    for k in range(1, chips):
        copies.append(
            send_to(
                plane.at[chip], plane.at[chip], plane_sems.at[0, k], plane_sems.at[1, k], flat[k - 1]
            )
        )
    for copy in copies:
        copy.start()
    for copy in copies:
        copy.wait()
    total = plane[0]
    for k in range(1, chips):
        total = total + plane[k]
    line[depth] = total
    copies = []
    for k in range(1, depths):
        copies.append(
            send_to(
                line.at[depth], line.at[depth], line_sems.at[0, k], line_sems.at[1, k], deep[k - 1]
            )
        )
    for copy in copies:
        copy.start()
    for copy in copies:
        copy.wait()
    total = line[0]
    for k in range(1, depths):
        total = total + line[k]
    out_ref[...] = total


def sum_small_kernel(*refs):
    greet(small_peers())
    exchange_small(*refs)


def small_scratch(shape, chips, depths):
    return [
        pltpu.VMEM(shape, jnp.float32),
        pltpu.VMEM((chips,) + shape, jnp.float32),
        pltpu.VMEM((depths,) + shape, jnp.float32),
        pltpu.SemaphoreType.DMA((2,)),
        pltpu.SemaphoreType.DMA((2, chips)),
        pltpu.SemaphoreType.DMA((2, depths)),
    ]


def sum_small(block, collective):
    chips, depths = lax.axis_size("dp") // 2, lax.axis_size("tensor")
    return pl.pallas_call(
        sum_small_kernel,
        out_shape=jax.ShapeDtypeStruct(block.shape, jnp.float32),
        in_specs=[whole_vmem()],
        out_specs=whole_vmem(),
        scratch_shapes=small_scratch(block.shape, chips, depths),
        compiler_params=pltpu.CompilerParams(
            collective_id=collective, has_side_effects=True, vmem_limit_bytes=16 * 2**20
        ),
        cost_estimate=pl.CostEstimate(flops=10**10, bytes_accessed=10**6, transcendentals=0),
    )(block)


def sum_and_spread_kernel(
    x_ref,
    y_ref,
    x_out,
    y_out,
    pair_in,
    pair_sum,
    plane_in,
    total,
    line_in,
    line_out,
    pair_sems,
    plane_sems,
    line_sems,
    spread_sems,
    share_sems,
):
    chips, chip, core, depth = place_of()
    depths = lax.axis_size("tensor")
    rank = chip * 2 + core
    other = 1 - core
    sibling = (chip * 2 + other, depth)
    chip_at = [lax.rem(chip + k, chips) for k in range(chips)]
    flat = [(chip_at[k] * 2 + core, depth) for k in range(chips)]
    deep = [(rank, lax.rem(depth + k, depths)) for k in range(depths)]
    greet([sibling] + flat[1:] + deep[1:])
    part = y_ref.shape[0] // depths
    part_of = [
        pl.ds(pl.multiple_of(lax.rem(depth + k, depths) * part, 8), part) for k in range(depths)
    ]
    halves = [slice(0, y_ref.shape[1] // 2), slice(y_ref.shape[1] // 2, y_ref.shape[1])]
    firsts, seconds = {}, {}
    for c in range(2):
        for k in range(1, depths):
            firsts[c, k] = send_to(
                y_ref.at[part_of[k], halves[c]],
                line_in.at[k, :, halves[c]],
                line_sems.at[c, 0, k],
                line_sems.at[c, 1, k],
                deep[k],
            )
            firsts[c, k].start()
    order = list(range(1, chips)) + [0]
    pair_copies, plane_copies = {}, {}
    for k in order:
        pair_copies[k] = send_to(
            x_ref.at[chip_at[k] * 2 + other],
            pair_in.at[k],
            pair_sems.at[0, k],
            pair_sems.at[1, k],
            sibling,
        )
        pair_copies[k].start()
    for k in order:
        pair_copies[k].wait_recv()
        pair_sum[k] = x_ref[chip_at[k] * 2 + core] + pair_in[k]
        if k:
            plane_copies[k] = send_to(
                pair_sum.at[k], plane_in.at[k], plane_sems.at[0, k], plane_sems.at[1, k], flat[k]
            )
            plane_copies[k].start()
    for c in range(2):
        value = y_ref[part_of[0], halves[c]]
        for k in range(1, depths):
            firsts[c, k].wait_recv()
            value = value + line_in[k, :, halves[c]]
        line_out[part_of[0], halves[c]] = value
        for k in range(1, depths):
            seconds[c, k] = send_to(
                line_out.at[part_of[0], halves[c]],
                line_out.at[part_of[0], halves[c]],
                line_sems.at[c, 2, k],
                line_sems.at[c, 3, k],
                deep[k],
            )
            seconds[c, k].start()
    value = pair_sum[0]
    for k in range(1, chips):
        plane_copies[k].wait_recv()
        value = value + plane_in[k]
    total[...] = value
    x_spread = start_spread(total, x_out, spread_sems.at[2], flat, rank)
    x_out[rank] = value
    y_spread, y_share = {}, {}
    for c in range(2):
        for k in range(1, depths):
            seconds[c, k].wait_recv()
        y_spread[c] = start_spread(
            line_out, y_out, spread_sems.at[c], flat, rank, halves[c]
        )
        y_out[rank, :, halves[c]] = line_out[:, halves[c]]
    place = (chips, chip, core)
    x_share = start_share(x_out, x_spread, share_sems.at[2], place, sibling)
    for c in range(2):
        y_share[c] = start_share(
            y_out, y_spread[c], share_sems.at[c], place, sibling, halves[c]
        )
    for k in range(chips):
        x_share[k].wait_recv()
        y_share[0][k].wait_recv()
        y_share[1][k].wait_recv()
    for copies in (
        pair_copies,
        plane_copies,
        firsts,
        seconds,
        y_spread[0],
        y_spread[1],
        x_spread,
        y_share[0],
        y_share[1],
        x_share,
    ):
        for copy in copies.values():
            copy.wait_send()


def sum_and_spread(rows, slab_y, collective):
    dp_count, depths = lax.axis_size("dp"), lax.axis_size("tensor")
    chips = dp_count // 2
    count, width = rows.shape
    slab = (count // dp_count, width)
    out_x, out_y = pl.pallas_call(
        sum_and_spread_kernel,
        out_shape=(
            jax.ShapeDtypeStruct((dp_count,) + slab, jnp.float32),
            jax.ShapeDtypeStruct((dp_count,) + slab_y.shape, jnp.float32),
        ),
        in_specs=[whole_vmem()] * 2,
        out_specs=(whole_vmem(), whole_vmem()),
        scratch_shapes=[
            pltpu.VMEM((chips,) + slab, jnp.float32),
            pltpu.VMEM((chips,) + slab, jnp.float32),
            pltpu.VMEM((chips,) + slab, jnp.float32),
            pltpu.VMEM(slab, jnp.float32),
            pltpu.VMEM((depths, slab_y.shape[0] // depths, width), jnp.float32),
            pltpu.VMEM(slab_y.shape, jnp.float32),
            pltpu.SemaphoreType.DMA((2, chips)),
            pltpu.SemaphoreType.DMA((2, chips)),
            pltpu.SemaphoreType.DMA((2, 4, depths)),
            pltpu.SemaphoreType.DMA((3, 2, chips)),
            pltpu.SemaphoreType.DMA((3, 2, chips)),
        ],
        compiler_params=pltpu.CompilerParams(
            collective_id=collective, has_side_effects=True, vmem_limit_bytes=32 * 2**20
        ),
        cost_estimate=pl.CostEstimate(
            flops=60 * 10**9, bytes_accessed=count * width * 16, transcendentals=0
        ),
    )(rows.reshape((dp_count,) + slab), slab_y)
    return out_x.reshape(count, width), out_y.reshape(-1, width)


def scatter_rows_kernel(
    x_ref, out_ref, pair_in, pair_sum, plane_in, pair_sems, plane_sems
):
    chips, chip, core, depth = place_of()
    other = 1 - core
    sibling = (chip * 2 + other, depth)
    chip_at = [lax.rem(chip + k, chips) for k in range(chips)]
    flat = [(chip_at[k] * 2 + core, depth) for k in range(chips)]
    greet([sibling] + flat[1:])
    order = list(range(1, chips)) + [0]
    pair_copies, plane_copies = {}, {}
    for k in order:
        pair_copies[k] = send_to(
            x_ref.at[chip_at[k] * 2 + other],
            pair_in.at[k],
            pair_sems.at[0, k],
            pair_sems.at[1, k],
            sibling,
        )
        pair_copies[k].start()
    for k in order:
        pair_copies[k].wait_recv()
        pair_sum[k] = x_ref[chip_at[k] * 2 + core] + pair_in[k]
        if k:
            plane_copies[k] = send_to(
                pair_sum.at[k], plane_in.at[k], plane_sems.at[0, k], plane_sems.at[1, k], flat[k]
            )
            plane_copies[k].start()
    value = pair_sum[0]
    for k in range(1, chips):
        plane_copies[k].wait_recv()
        value = value + plane_in[k]
    out_ref[...] = value
    for copies in (pair_copies, plane_copies):
        for copy in copies.values():
            copy.wait_send()


def pad_rows(rows, unit):
    have, width = rows.shape
    padded = -(-have // unit) * unit
    if padded == have:
        return rows
    return jnp.concatenate([rows, jnp.zeros((padded - have, width), rows.dtype)], axis=0)


def scatter_rows(rows, collective):
    dp_count = lax.axis_size("dp")
    chips = dp_count // 2
    slab = (rows.shape[0] // dp_count, rows.shape[1])
    return pl.pallas_call(
        scatter_rows_kernel,
        out_shape=jax.ShapeDtypeStruct(slab, jnp.float32),
        in_specs=[whole_vmem()],
        out_specs=whole_vmem(),
        scratch_shapes=[
            pltpu.VMEM((chips,) + slab, jnp.float32),
            pltpu.VMEM((chips,) + slab, jnp.float32),
            pltpu.VMEM((chips,) + slab, jnp.float32),
            pltpu.SemaphoreType.DMA((2, chips)),
            pltpu.SemaphoreType.DMA((2, chips)),
        ],
        compiler_params=pltpu.CompilerParams(
            collective_id=collective, has_side_effects=True, vmem_limit_bytes=32 * 2**20
        ),
        cost_estimate=pl.CostEstimate(
            flops=rows.shape[0] * 15 * 10**6,
            bytes_accessed=rows.shape[0] * rows.shape[1] * 4,
            transcendentals=0,
        ),
    )(rows.reshape((dp_count,) + slab))


def start_spread(src, out_ref, sems, flat, rank, cols=slice(None)):
    copies = {}
    for k in range(1, len(flat)):
        copies[k] = send_to(
            src.at[:, cols], out_ref.at[rank, :, cols], sems.at[0, k], sems.at[1, k], flat[k]
        )
        copies[k].start()
    return copies


def start_share(out_ref, spread_copies, sems, place, sibling, cols=slice(None)):
    chips, chip, core = place
    copies = {}
    for k in range(chips):
        if k:
            spread_copies[k].wait_recv()
        held = lax.rem(chip + chips - k, chips) * 2 + core
        copies[k] = send_to(
            out_ref.at[held, :, cols],
            out_ref.at[held, :, cols],
            sems.at[0, k],
            sems.at[1, k],
            sibling,
        )
        copies[k].start()
    return copies


def spread_kernel(x_ref, out_ref, spread_sems, share_sems):
    chips, chip, core, depth = place_of()
    rank = chip * 2 + core
    sibling = (chip * 2 + 1 - core, depth)
    flat = [(lax.rem(chip + k, chips) * 2 + core, depth) for k in range(chips)]
    greet([sibling] + flat[1:])
    spread_copies = start_spread(x_ref, out_ref, spread_sems, flat, rank)
    out_ref[rank] = x_ref[...]
    share_copies = start_share(out_ref, spread_copies, share_sems, (chips, chip, core), sibling)
    for k in range(chips):
        share_copies[k].wait_recv()
    for copies in (spread_copies, share_copies):
        for copy in copies.values():
            copy.wait_send()


def spread(slab, collective):
    dp_count = lax.axis_size("dp")
    chips = dp_count // 2
    each, width = slab.shape
    full = pl.pallas_call(
        spread_kernel,
        out_shape=jax.ShapeDtypeStruct((dp_count, each, width), slab.dtype),
        in_specs=[whole_vmem()],
        out_specs=whole_vmem(),
        scratch_shapes=[
            pltpu.SemaphoreType.DMA((2, chips)),
            pltpu.SemaphoreType.DMA((2, chips)),
        ],
        compiler_params=pltpu.CompilerParams(
            collective_id=collective, has_side_effects=True, vmem_limit_bytes=16 * 2**20
        ),
        cost_estimate=pl.CostEstimate(
            flops=35 * 10**9, bytes_accessed=dp_count * each * width * 4, transcendentals=0
        ),
    )(slab)
    return full.reshape(dp_count * each, width)


def line_steps(x_ref, out_ref, right_send, right_recv, left_send, left_recv):
    rank = lax.axis_index("dp")
    depth = lax.axis_index("tensor")
    last = lax.axis_size("tensor") - 1
    right, left = (rank, depth + 1), (rank, depth - 1)

    def to_right(step):
        src = x_ref if step == 0 else out_ref.at[depth - step]
        return send_to(
            src, out_ref.at[depth - step], right_send.at[step], right_recv.at[step], right
        )

    def to_left(step):
        src = x_ref if step == 0 else out_ref.at[depth + step]
        return send_to(src, out_ref.at[depth + step], left_send.at[step], left_recv.at[step], left)

    def send(step):
        @pl.when((depth < last) & (depth >= step))
        def _():
            to_right(step).start()

        @pl.when((depth > 0) & (depth + step <= last))
        def _():
            to_left(step).start()

        if step == 0:
            out_ref[depth] = x_ref[...]

    def receive(step):
        @pl.when(depth - 1 >= step)
        def _():
            send_to(
                x_ref,
                out_ref.at[depth - 1 - step],
                right_send.at[step],
                right_recv.at[step],
                left,
            ).wait_recv()

        @pl.when(depth + 1 + step <= last)
        def _():
            send_to(
                x_ref, out_ref.at[depth + 1 + step], left_send.at[step], left_recv.at[step], right
            ).wait_recv()

    def finish():
        for step in range(last):

            @pl.when((depth < last) & (depth >= step))
            def _():
                to_right(step).wait_send()

            @pl.when((depth > 0) & (depth + step <= last))
            def _():
                to_left(step).wait_send()

    return send, receive, finish


def line_gather_kernel(x_ref, out_ref, *sems):
    last = lax.axis_size("tensor") - 1
    greet_line(lax.axis_index("tensor"), last, lax.axis_index("dp"))
    send, receive, finish = line_steps(x_ref, out_ref, *sems)
    for step in range(last):
        send(step)
        receive(step)
    finish()


def first_gather_kernel(
    head_count,
    x_ref,
    y_ref,
    t_ref,
    weight_ref,
    rows_ref,
    small_ref,
    tall_ref,
    qkv_ref,
    heads_ref,
    log_ref,
    pair,
    plane,
    line,
    pair_sems,
    plane_sems,
    line_sems,
    *sems,
):
    last = lax.axis_size("tensor") - 1
    greet(small_peers())
    send, receive, finish = line_steps(x_ref, rows_ref, *sems[:4])
    send_tall, receive_tall, finish_tall = line_steps(t_ref, tall_ref, *sems[4:])
    count = x_ref.shape[0]
    for step in range(last):
        send(step)
        if step == 0:
            exchange_small(y_ref, small_ref, pair, plane, line, pair_sems, plane_sems, line_sems)
        if step == 1:
            send_tall(0)
        receive(step)
    receive_tall(0)
    send_tall(1)
    for j in range(last + 1):
        qkv_ref[j * count : (j + 1) * count, :] = plain_dot(
            rows_ref[j], weight_ref[...]
        ).astype(jnp.bfloat16)
    attend_forward_kernel(head_count, qkv_ref, heads_ref, log_ref)
    for step in range(1, last):
        receive_tall(step)
        if step + 1 < last:
            send_tall(step + 1)
    finish()
    finish_tall()


def first_gather(block, small, tall, weight, head_count, collective):
    chips, depths = lax.axis_size("dp") // 2, lax.axis_size("tensor")
    rows, width = block.shape
    outs = pl.pallas_call(
        functools.partial(first_gather_kernel, head_count),
        out_shape=(
            jax.ShapeDtypeStruct((depths, rows, width), block.dtype),
            jax.ShapeDtypeStruct(small.shape, jnp.float32),
            jax.ShapeDtypeStruct((depths,) + tall.shape, tall.dtype),
            jax.ShapeDtypeStruct((LEN, weight.shape[1]), jnp.bfloat16),
            jax.ShapeDtypeStruct((LEN, head_count * HEAD), jnp.bfloat16),
            jax.ShapeDtypeStruct((LEN, 128), jnp.float32),
        ),
        in_specs=[whole_vmem()] * 4,
        out_specs=tuple(whole_vmem() for _ in range(6)),
        scratch_shapes=small_scratch(small.shape, chips, depths)
        + [pltpu.SemaphoreType.DMA((depths,))] * 8,
        compiler_params=pltpu.CompilerParams(
            collective_id=collective, has_side_effects=True, vmem_limit_bytes=40 * 2**20
        ),
        cost_estimate=pl.CostEstimate(
            flops=80 * 10**9, bytes_accessed=depths * tall.size * 4, transcendentals=0
        ),
    )(block, small, tall, weight)
    return (
        outs[0].reshape(depths * rows, width),
        outs[1],
        outs[2].reshape(depths * rows, tall.shape[1]),
    ) + tuple(outs[3:])


def line_gather(block, collective):
    depths = lax.axis_size("tensor")
    rows, width = block.shape
    out = pl.pallas_call(
        line_gather_kernel,
        out_shape=jax.ShapeDtypeStruct((depths, rows, width), block.dtype),
        in_specs=[whole_vmem()],
        out_specs=whole_vmem(),
        scratch_shapes=[pltpu.SemaphoreType.DMA((depths,))] * 4,
        compiler_params=pltpu.CompilerParams(
            collective_id=collective, has_side_effects=True, vmem_limit_bytes=16 * 2**20
        ),
        cost_estimate=pl.CostEstimate(
            flops=25 * 10**9, bytes_accessed=depths * rows * width * 4, transcendentals=0
        ),
    )(block)
    return out.reshape(depths * rows, width)


def renew_kernel(widths, flips, gains, group_ref, map_ref, *refs):
    olds, news = refs[: len(widths)], refs[len(widths) :]
    keep_rate = 1.0 - MUON_RATE * MUON_DECAY
    offset = 0
    total = group_ref.shape[1]
    for width, flip, gain, old, new in zip(widths, flips, gains, olds, news):
        iterate_ref = group_ref
        if offset == total:
            iterate_ref, offset = map_ref, 0
        if flip:
            for first in range(0, width, 128):
                size = min(128, width - first)
                piece = iterate_ref[:, offset + first : offset + first + size]
                rows = slice(first, first + size)
                new[rows, :] = keep_rate * old[rows, :] - MUON_RATE * gain * (
                    piece.astype(jnp.float32).T
                )
        else:
            for first in range(0, old.shape[0], 128):
                rows = slice(first, first + 128)
                piece = iterate_ref[rows, offset : offset + width]
                new[rows, :] = keep_rate * old[rows, :] - MUON_RATE * gain * (
                    piece.astype(jnp.float32)
                )
        offset += width


def renew(iterate, map_iterate, olds, widths, flips, gains):
    return pl.pallas_call(
        functools.partial(renew_kernel, widths, flips, gains),
        out_shape=tuple(jax.ShapeDtypeStruct(old.shape, jnp.float32) for old in olds),
        in_specs=[whole_vmem()] * (2 + len(olds)),
        out_specs=tuple(whole_vmem() for _ in olds),
        compiler_params=pltpu.CompilerParams(vmem_limit_bytes=48 * 2**20),
        cost_estimate=pl.CostEstimate(
            flops=10**9, bytes_accessed=iterate.size * 10, transcendentals=0
        ),
    )(iterate, map_iterate, *olds)


HALF = 128
QUARTER = 64


def greet_line(depth, last, rank):
    barrier = pltpu.get_barrier_semaphore()

    @pl.when(depth < last)
    def _():
        pl.semaphore_signal(
            barrier, inc=1, device_id=(rank, depth + 1), device_id_type=MESH_ID
        )

    @pl.when(depth > 0)
    def _():
        pl.semaphore_signal(
            barrier, inc=1, device_id=(rank, depth - 1), device_id_type=MESH_ID
        )

    @pl.when((depth > 0) & (depth < last))
    def _():
        pl.semaphore_wait(barrier, 2)

    @pl.when((depth == 0) | (depth == last))
    def _():
        pl.semaphore_wait(barrier, 1)


def line_mlp_kernel(
    x_ref,
    first_ref,
    second_ref,
    out_ref,
    rows,
    parts,
    from_left,
    from_right,
    stage,
    right_sems,
    left_sems,
    row_sems,
    sum_sems,
    from_left_sems,
    from_right_sems,
):
    rank = lax.axis_index("dp")
    depth = lax.axis_index("tensor")
    last = lax.axis_size("tensor") - 1
    right, left = (rank, depth + 1), (rank, depth - 1)
    greet_line(depth, last, rank)

    def rows_right(j, h):
        return send_to(rows.at[j, h], rows.at[j, h], right_sems.at[j, h], row_sems.at[j, h], right)

    def rows_left(j, h):
        return send_to(rows.at[j, h], rows.at[j, h], left_sems.at[j, h], row_sems.at[j, h], left)

    def sum_right(j, h):
        return send_to(
            stage.at[j, h], from_left.at[j, h], sum_sems.at[j, h], from_left_sems.at[j, h], right
        )

    def sum_left(j, h):
        return send_to(
            stage.at[j, h], from_right.at[j, h], sum_sems.at[j, h], from_right_sems.at[j, h], left
        )

    for q in range(4):
        rows[depth, q] = x_ref[q * QUARTER : (q + 1) * QUARTER, :]

        @pl.when(depth < last)
        def _():
            rows_right(depth, q).start()

        @pl.when(depth > 0)
        def _():
            rows_left(depth, q).start()

    inner = depth * (last - depth) // 2
    side = depth // 2
    for step, shift in enumerate((1, 1, -2, 0)):
        base = step + inner * shift
        j = base + side * (last - 2 * base)

        def half_step(h, carry):
            for q in (2 * h, 2 * h + 1):
                if step:

                    @pl.when(j < depth)
                    def _():
                        rows_right(j, q).wait_recv()

                    @pl.when(j > depth)
                    def _():
                        rows_left(j, q).wait_recv()

                    @pl.when((j < depth) & (depth < last))
                    def _():
                        rows_right(j, q).start()

                    @pl.when((j > depth) & (depth > 0))
                    def _():
                        rows_left(j, q).start()

            block = jnp.concatenate([rows[j, 2 * h], rows[j, 2 * h + 1]], axis=0)
            hidden = smooth_gelu(plain_dot(block, first_ref[...])).astype(jnp.bfloat16)
            part = plain_dot(hidden, second_ref[...])
            for i in range(2):
                q = 2 * h + i
                piece = part[i * QUARTER : (i + 1) * QUARTER, :]
                parts[j, q] = piece
                if step:

                    @pl.when((depth == 0) | (depth == last))
                    def _():
                        stage[j, q] = piece.astype(jnp.bfloat16)

                    @pl.when(depth == 0)
                    def _():
                        sum_right(j, q).start()

                    @pl.when(depth == last)
                    def _():
                        sum_left(j, q).start()

            return carry

        lax.fori_loop(0, 2, half_step, 0)

    def relay_right(j):
        for h in range(4):
            sum_right(j, h).wait_recv()
            stage[j, h] = (parts[j, h] + from_left[j, h].astype(jnp.float32)).astype(jnp.bfloat16)
            sum_right(j, h).start()

    def relay_left(j):
        for h in range(4):
            sum_left(j, h).wait_recv()
            stage[j, h] = (parts[j, h] + from_right[j, h].astype(jnp.float32)).astype(jnp.bfloat16)
            sum_left(j, h).start()

    @pl.when(depth == 1)
    def _():
        relay_right(2)
        relay_right(3)
        relay_left(0)

    @pl.when(depth == 2)
    def _():
        relay_left(1)
        relay_left(0)
        relay_right(3)

    for h in range(4):
        span = slice(h * QUARTER, (h + 1) * QUARTER)
        out_ref[span, :] = parts[depth, h]

        @pl.when(depth > 0)
        def _():
            sum_right(depth, h).wait_recv()
            out_ref[span, :] += from_left[depth, h].astype(jnp.float32)

        @pl.when(depth < last)
        def _():
            sum_left(depth, h).wait_recv()
            out_ref[span, :] += from_right[depth, h].astype(jnp.float32)

    for j in range(4):
        for h in range(4):

            @pl.when((depth >= j) & (depth < last))
            def _():
                rows_right(j, h).wait_send()

            @pl.when((depth <= j) & (depth > 0))
            def _():
                rows_left(j, h).wait_send()

            @pl.when(depth < j)
            def _():
                sum_right(j, h).wait_send()

            @pl.when(depth > j)
            def _():
                sum_left(j, h).wait_send()


def line_mlp(block, first, second, collective):
    count, width = block.shape
    slots = (4, 4, QUARTER, width)
    return pl.pallas_call(
        line_mlp_kernel,
        out_shape=jax.ShapeDtypeStruct((count, width), jnp.float32),
        in_specs=[whole_vmem()] * 3,
        out_specs=whole_vmem(),
        scratch_shapes=[
            pltpu.VMEM(slots, jnp.bfloat16),
            pltpu.VMEM(slots, jnp.float32),
            pltpu.VMEM(slots, jnp.bfloat16),
            pltpu.VMEM(slots, jnp.bfloat16),
            pltpu.VMEM(slots, jnp.bfloat16),
        ]
        + [pltpu.SemaphoreType.DMA((4, 4))] * 6,
        compiler_params=pltpu.CompilerParams(
            collective_id=collective, has_side_effects=True, vmem_limit_bytes=48 * 2**20
        ),
        cost_estimate=pl.CostEstimate(
            flops=16 * count * width * first.shape[1] * 4,
            bytes_accessed=16 * count * width,
            transcendentals=4 * count * first.shape[1],
        ),
    )(block, first, second)


def share_gram_kernel(
    parts_ref, extra_ref, out_ref, line_in, pair_in, line_sems, pair_sems, plane_sems
):
    chips, chip, core, depth = place_of()
    depths = lax.axis_size("tensor")
    rank = chip * 2 + core
    sibling = (chip * 2 + 1 - core, depth)
    flat = [(lax.rem(chip + k, chips) * 2 + core, depth) for k in range(chips)]
    line = [lax.rem(depth + k, depths) for k in range(depths)]
    deep = [(rank, line[k]) for k in range(depths)]
    greet([sibling] + flat[1:] + deep[1:])
    copies = {}
    for k in range(1, depths):
        copies[k] = send_to(
            parts_ref.at[line[k]], line_in.at[k], line_sems.at[0, k], line_sems.at[1, k], deep[k]
        )
        copies[k].start()
    extra = send_to(extra_ref, out_ref.at[rank], pair_sems.at[0], pair_sems.at[1], sibling)
    main = send_to(pair_in, out_ref.at[rank], pair_sems.at[2], pair_sems.at[3], sibling)
    plane = {}
    for k in range(1, chips):
        plane[k] = [
            send_to(
                out_ref.at[chip * 2 + i],
                out_ref.at[chip * 2 + i],
                plane_sems.at[0, i, k],
                plane_sems.at[1, i, k],
                flat[k],
            )
            for i in range(2)
        ]

    @pl.when(core == 0)
    def _():
        extra.start()

    @pl.when(core == 1)
    def _():
        out_ref[rank] = extra_ref[...]
        extra.wait_recv()
        for k in range(1, chips):
            for i in range(2):
                plane[k][i].start()

    value = parts_ref[depth]
    for k in range(1, depths):
        copies[k].wait_recv()
        value = value + line_in[k]

    @pl.when(core == 1)
    def _():
        pair_in[...] = value
        main.start()

    @pl.when(core == 0)
    def _():
        out_ref[rank] = value
        main.wait_recv()
        for k in range(1, chips):
            for i in range(2):
                plane[k][i].start()

    for k in range(1, chips):
        for i in range(2):
            plane[k][i].wait_recv()
    for k in range(1, chips):
        for i in range(2):
            plane[k][i].wait_send()
    for k in range(1, depths):
        copies[k].wait_send()

    @pl.when(core == 0)
    def _():
        extra.wait_send()

    @pl.when(core == 1)
    def _():
        main.wait_send()


def share_gram(parts, extra, collective):
    dp_count, depths = lax.axis_size("dp"), lax.axis_size("tensor")
    chips = dp_count // 2
    slab = extra.shape
    out = pl.pallas_call(
        share_gram_kernel,
        out_shape=jax.ShapeDtypeStruct((dp_count,) + slab, jnp.float32),
        in_specs=[whole_vmem()] * 2,
        out_specs=whole_vmem(),
        scratch_shapes=[
            pltpu.VMEM((depths,) + slab, jnp.float32),
            pltpu.VMEM(slab, jnp.float32),
            pltpu.SemaphoreType.DMA((2, depths)),
            pltpu.SemaphoreType.DMA((4,)),
            pltpu.SemaphoreType.DMA((2, 2, chips)),
        ],
        compiler_params=pltpu.CompilerParams(
            collective_id=collective, has_side_effects=True, vmem_limit_bytes=16 * 2**20
        ),
        cost_estimate=pl.CostEstimate(
            flops=45 * 10**9, bytes_accessed=dp_count * slab[0] * slab[1] * 8, transcendentals=0
        ),
    )(parts.reshape((depths,) + slab), extra)
    return out.reshape(dp_count * slab[0], slab[1])


def line_exchange_kernel(
    heads_ref,
    weight_ref,
    x_ref,
    sum_ref,
    all_ref,
    y_ref,
    from_left,
    from_right,
    stage,
    right_sems,
    left_sems,
    row_sems,
    sum_sems,
    from_left_sems,
    from_right_sems,
):
    rank = lax.axis_index("dp")
    depth = lax.axis_index("tensor")
    last = lax.axis_size("tensor") - 1
    right, left = (rank, depth + 1), (rank, depth - 1)
    greet_line(depth, last, rank)

    def rows_right(j):
        return send_to(all_ref.at[j], all_ref.at[j], right_sems.at[j], row_sems.at[j], right)

    def rows_left(j):
        return send_to(all_ref.at[j], all_ref.at[j], left_sems.at[j], row_sems.at[j], left)

    def sum_right(j, h, src):
        return send_to(
            src.at[j, h], from_left.at[j, h], sum_sems.at[j, h], from_left_sems.at[j, h], right
        )

    def sum_left(j, h, src):
        return send_to(
            src.at[j, h], from_right.at[j, h], sum_sems.at[j, h], from_right_sems.at[j, h], left
        )

    all_ref[depth] = x_ref[...]

    @pl.when(depth < last)
    def _():
        rows_right(depth).start()

    @pl.when(depth > 0)
    def _():
        rows_left(depth).start()

    for j in range(4):
        for h in range(2):
            first = (2 * j + h) * HALF
            y_ref[j, h] = plain_dot(
                heads_ref[first : first + HALF, :], weight_ref[...]
            ).astype(jnp.bfloat16)

    @pl.when(depth == 0)
    def _():
        for j in (3, 2, 1):
            for h in range(2):
                sum_right(j, h, y_ref).start()
        for j in (1, 2, 3):
            rows_left(j).wait_recv()

    @pl.when(depth == last)
    def _():
        for j in (0, 1, 2):
            for h in range(2):
                sum_left(j, h, y_ref).start()
        for j in (2, 1, 0):
            rows_right(j).wait_recv()

    def relay_right(j):
        for h in range(2):
            sum_right(j, h, stage).wait_recv()
            stage[j, h] = (
                y_ref[j, h].astype(jnp.float32) + from_left[j, h].astype(jnp.float32)
            ).astype(jnp.bfloat16)
            sum_right(j, h, stage).start()

    def relay_left(j):
        for h in range(2):
            sum_left(j, h, stage).wait_recv()
            stage[j, h] = (
                y_ref[j, h].astype(jnp.float32) + from_right[j, h].astype(jnp.float32)
            ).astype(jnp.bfloat16)
            sum_left(j, h, stage).start()

    def pass_right(j):
        rows_right(j).wait_recv()
        rows_right(j).start()

    def pass_left(j):
        rows_left(j).wait_recv()
        rows_left(j).start()

    @pl.when(depth == 1)
    def _():
        pass_left(2)
        pass_right(0)
        relay_right(3)
        pass_left(3)
        relay_left(0)
        relay_right(2)

    @pl.when(depth == 2)
    def _():
        pass_right(1)
        pass_left(3)
        relay_left(0)
        pass_right(0)
        relay_right(3)
        relay_left(1)

    for h in range(2):
        span = slice(h * HALF, (h + 1) * HALF)
        sum_ref[span, :] = y_ref[depth, h].astype(jnp.float32)

        @pl.when(depth > 0)
        def _():
            sum_right(depth, h, stage).wait_recv()
            sum_ref[span, :] += from_left[depth, h].astype(jnp.float32)

        @pl.when(depth < last)
        def _():
            sum_left(depth, h, stage).wait_recv()
            sum_ref[span, :] += from_right[depth, h].astype(jnp.float32)

    for j in range(4):

        @pl.when((depth >= j) & (depth < last))
        def _():
            rows_right(j).wait_send()

        @pl.when((depth <= j) & (depth > 0))
        def _():
            rows_left(j).wait_send()

        for h in range(2):

            @pl.when(depth < j)
            def _():
                sum_right(j, h, stage).wait_send()

            @pl.when(depth > j)
            def _():
                sum_left(j, h, stage).wait_send()


def line_exchange(heads, weight, block, collective):
    width = weight.shape[1]
    slots = (4, 2, HALF, width)
    total, rows = pl.pallas_call(
        line_exchange_kernel,
        out_shape=(
            jax.ShapeDtypeStruct((2 * HALF, width), jnp.float32),
            jax.ShapeDtypeStruct((4,) + block.shape, block.dtype),
        ),
        in_specs=[whole_vmem()] * 3,
        out_specs=(whole_vmem(), whole_vmem()),
        scratch_shapes=[pltpu.VMEM(slots, jnp.bfloat16)] * 4
        + [pltpu.SemaphoreType.DMA((4,))] * 3
        + [pltpu.SemaphoreType.DMA((4, 2))] * 3,
        compiler_params=pltpu.CompilerParams(
            collective_id=collective, has_side_effects=True, vmem_limit_bytes=32 * 2**20
        ),
        cost_estimate=pl.CostEstimate(
            flops=60 * 10**9, bytes_accessed=heads.size * 16, transcendentals=0
        ),
    )(heads, weight, block)
    return total, rows.reshape(-1, block.shape[1])


NBLK = 256


def split_store(value, high_ref, low_ref, rows, cols):
    high = value.astype(jnp.bfloat16)
    high_ref[rows, cols] = high
    low_ref[rows, cols] = (value - high.astype(jnp.float32)).astype(jnp.bfloat16)


def polynomial_kernel(gram_ref, out_ref, full_g, full_h, full_m, *pairs):
    gram_pair, half_pair, poly_pair, prod_pair = (
        pairs[0:2], pairs[2:4], pairs[4:6], pairs[6:8]
    )
    size = gram_ref.shape[0]
    blocks = size // NBLK
    spans = [slice(i * NBLK, (i + 1) * NBLK) for i in range(blocks)]
    upper = [(i, j) for i in range(blocks) for j in range(i, blocks)]

    def eye(i, j):
        if i != j:
            return 0.0
        row = lax.broadcasted_iota(jnp.int32, (NBLK, NBLK), 0)
        col = lax.broadcasted_iota(jnp.int32, (NBLK, NBLK), 1)
        return jnp.where(row == col, 1.0, 0.0)

    def place(i, j, value, full, pair):
        if full is not None:
            full[spans[i], spans[j]] = value
        if pair is not None:
            split_store(value, *pair, spans[i], spans[j])
        if i != j:
            flip = value.T
            if full is not None:
                full[spans[j], spans[i]] = flip
            if pair is not None:
                split_store(flip, *pair, spans[j], spans[i])

    def product(left, right, i, j):
        return plain_dot(left[0][spans[i], :], right[0][:, spans[j]]) + (
            plain_dot(left[0][spans[i], :], right[1][:, spans[j]])
            + plain_dot(left[1][spans[i], :], right[0][:, spans[j]])
        )

    trace = 0.0
    for i in range(blocks):
        trace = trace + jnp.sum(gram_ref[spans[i], spans[i]] * eye(i, i))
    root = jnp.sqrt(jnp.full((1, 1), trace, jnp.float32)) + 1e-07
    inverse = 1.0 / root
    for i, j in upper:
        place(i, j, gram_ref[spans[i], spans[j]] * (inverse * inverse), full_g, gram_pair)

    def make_poly():
        for i, j in upper:
            value = NS_B * full_g[spans[i], spans[j]] + NS_C * product(gram_pair, gram_pair, i, j)
            place(i, j, value, None, poly_pair)

    def advance():
        for i, j in upper:
            value = NS_A * full_g[spans[i], spans[j]] + product(poly_pair, gram_pair, i, j)
            place(i, j, value, full_h, half_pair)
        for i, j in upper:
            value = NS_A * full_h[spans[i], spans[j]] + product(poly_pair, half_pair, i, j)
            place(i, j, value, full_g, gram_pair)

    make_poly()
    for i, j in upper:
        value = (
            poly_pair[0][spans[i], spans[j]].astype(jnp.float32)
            + poly_pair[1][spans[i], spans[j]].astype(jnp.float32)
            + NS_A * eye(i, j)
        )
        place(i, j, value, full_m, prod_pair)
    advance()

    def sweep(index, carry):
        make_poly()
        for i, j in upper:
            value = NS_A * full_m[spans[i], spans[j]] + product(poly_pair, prod_pair, i, j)
            place(i, j, value, full_h, None)
        for i in range(blocks):
            full_m[spans[i], :] = full_h[spans[i], :]
            split_store(full_h[spans[i], :], *prod_pair, spans[i], slice(None))
        advance()
        return carry

    lax.fori_loop(0, 3, sweep, 0)
    make_poly()
    for i, j in upper:
        value = NS_A * full_m[spans[i], spans[j]] + product(poly_pair, prod_pair, i, j)
        place(i, j, value * inverse, out_ref, None)


def orthogonal_factor(gram_mat):
    size = gram_mat.shape[0]
    return pl.pallas_call(
        polynomial_kernel,
        out_shape=jax.ShapeDtypeStruct((size, size), jnp.float32),
        in_specs=[whole_vmem()],
        out_specs=whole_vmem(),
        scratch_shapes=[pltpu.VMEM((size, size), jnp.float32)] * 3
        + [pltpu.VMEM((size, size), jnp.bfloat16)] * 8,
        compiler_params=pltpu.CompilerParams(vmem_limit_bytes=48 * 2**20),
        cost_estimate=pl.CostEstimate(
            flops=17 * 2 * 2 * size**3, bytes_accessed=8 * size * size, transcendentals=0
        ),
    )(gram_mat)


def contract_rows(left, right):
    return lax.dot_general(
        left, right, (((0,), (0,)), ((), ())), preferred_element_type=jnp.float32
    )


def contract_cols(left, right):
    return lax.dot_general(
        left, right, (((1,), (1,)), ((), ())), preferred_element_type=jnp.float32
    )


def body(
    teacher_in,
    student_in,
    resp_mask,
    replay,
    t_gains,
    t_shifts,
    t_qkv,
    t_out,
    t_fc,
    t_proj,
    s_norms,
    s_qkv,
    s_out,
    s_fc,
    s_proj,
    s_map,
    mom_qkv,
    mom_out,
    mom_fc,
    mom_proj,
    mom_map,
    adam_first,
    adam_second,
):
    groups = lax.axis_size("tensor")
    tensor_rank = lax.axis_index("tensor")
    row_count = student_in.shape[0]
    seq_count = replay.shape[0]
    total_rows = row_count * groups
    count_block = jnp.full((8, 128), jnp.sum(resp_mask), jnp.int32).astype(jnp.float32)
    tokens_all = lax.axis_size("dp") * seq_count * LEN

    def student_gather(local_rows):
        return lax.all_gather(local_rows, "tensor", axis=0, tiled=True)

    def student_reduce(left, right, right_dim):
        return lax.psum_scatter(
            lax.dot_general(
                left, right, (((1,), (right_dim,)), ((), ())), preferred_element_type=jnp.float32
            ).astype(jnp.bfloat16),
            "tensor",
            scatter_dimension=0,
            tiled=True,
        ).astype(jnp.float32)

    teacher_x = teacher_in.astype(jnp.float32)
    slot_width = t_qkv.shape[2]
    slot_count = slot_width // HEAD
    live_count = HT // groups + (tensor_rank < HT % groups).astype(jnp.int32)
    live_slots = (jnp.arange(slot_count, dtype=jnp.int32) < live_count).astype(jnp.float32)
    teacher_normed = norm_parts(teacher_x, t_gains[0], t_shifts[0])[0].astype(jnp.bfloat16)
    student_x = student_in.astype(jnp.float32)
    shard_width = s_qkv.shape[2]
    shard_hidden = s_fc.shape[1]
    head_count = shard_width // HEAD
    w_qkv = s_qkv.astype(jnp.bfloat16).reshape(DS, 3 * shard_width)
    w_out = s_out.astype(jnp.bfloat16)
    w_fc = s_fc.astype(jnp.bfloat16)
    w_proj = s_proj.astype(jnp.bfloat16)
    w_map = s_map.astype(jnp.bfloat16)
    normed_one, unit_one, scale_one = norm_parts(student_x, s_norms[0], s_norms[1])
    low_one = normed_one.astype(jnp.bfloat16)
    rows_one, count_sum, teacher_all, mixed_qkv, head_out, log_sums = first_gather(
        low_one, count_block, teacher_normed, w_qkv, head_count, 5
    )
    count_val = count_sum[0, 0]
    factor = tokens_all / (2.0 * count_val)
    resid = student_x + student_reduce(head_out, w_out, 0)
    teacher_mixed = jnp.dot(
        teacher_all, t_qkv.reshape(DT, 3 * slot_width), preferred_element_type=jnp.float32
    ).astype(jnp.bfloat16)
    teacher_head_out = attend_forward(teacher_mixed, slot_count)[0]
    slot_mask = jnp.repeat(live_slots, HEAD)[None, :] > 0.0
    teacher_head_out = jnp.where(slot_mask, teacher_head_out, jnp.zeros_like(teacher_head_out))
    normed_two, unit_two, scale_two = norm_parts(resid, s_norms[2], s_norms[3])
    low_two = normed_two.astype(jnp.bfloat16)
    attn_part, rows_two = line_exchange(teacher_head_out, t_out, low_two, 6)
    teacher_resid = teacher_x + attn_part
    teacher_normed_two = norm_parts(teacher_resid, t_gains[1], t_shifts[1])[0].astype(jnp.bfloat16)
    mlp_part = line_mlp(teacher_normed_two, t_fc, t_proj, 8)
    teacher_out = (teacher_resid + mlp_part).astype(jnp.bfloat16)
    before = jnp.dot(rows_two, w_fc, preferred_element_type=jnp.float32)
    before, hidden = (before, smooth_gelu(before).astype(jnp.bfloat16))
    output = resid + student_reduce(hidden, w_proj, 0)
    student_out = output.astype(jnp.bfloat16)
    guess_vec = jnp.dot(student_out, w_map, preferred_element_type=jnp.float32)
    miss_vec = guess_vec - teacher_out.astype(jnp.float32)
    position = tensor_rank * row_count + jnp.arange(row_count, dtype=jnp.int32)
    seq_owner = position // LEN
    seq_pick = (seq_owner[:, None] == jnp.arange(seq_count, dtype=jnp.int32)[None, :]).astype(
        jnp.float32
    )
    flag_tok = jnp.sum(seq_pick * replay.astype(jnp.float32)[None, :], axis=1)
    weight = resp_mask.astype(jnp.float32) * (1.0 - REPLAY_CUT * flag_tok)
    loss_part = jnp.sum(weight[:, None] * miss_vec * miss_vec)
    grad_guess = (2.0 * factor * weight[:, None] * miss_vec).astype(jnp.bfloat16)
    row_unit = 8 * lax.axis_size("dp") * groups
    map_slab = scatter_rows(pad_rows(contract_rows(grad_guess, student_out), row_unit), 1)
    grad_output = contract_cols(grad_guess, w_map)
    rows_two_back, before_back, hidden_back = (rows_two, before, hidden)
    rows_one_back, mixed_back, heads_back, logs_back = (rows_one, mixed_qkv, head_out, log_sums)
    grad_mlp = student_gather(grad_output.astype(jnp.bfloat16))
    grad_mlp, map_slab = lax.optimization_barrier((grad_mlp, map_slab))
    grad_proj = contract_rows(hidden_back, grad_mlp)
    grad_hidden = contract_cols(grad_mlp, w_proj)
    gelu_vals, gelu_pull = jax.vjp(smooth_gelu, before_back)
    grad_before = gelu_pull(grad_hidden)[0].astype(jnp.bfloat16)
    grad_fc = contract_rows(rows_two_back, grad_before).reshape(-1, DS)
    mlp_slab = scatter_rows(jnp.concatenate([grad_proj, grad_fc], axis=0), 2)
    grad_normed_two = student_reduce(grad_before, w_fc, 1)
    grad_normed_two, mlp_slab = lax.optimization_barrier((grad_normed_two, mlp_slab))
    grad_resid = grad_output + norm_back(grad_normed_two, unit_two, scale_two, s_norms[2])
    grad_attn = student_gather(grad_resid.astype(jnp.bfloat16))
    grad_mlp_rows = spread(mlp_slab, 7)
    grad_attn, grad_mlp_rows = lax.optimization_barrier((grad_attn, grad_mlp_rows))
    grad_proj, grad_fc = grad_mlp_rows[:shard_hidden], grad_mlp_rows[shard_hidden:]
    grad_out = contract_rows(heads_back, grad_attn)
    grad_heads = contract_cols(grad_attn, w_out).astype(jnp.bfloat16)

    grad_mixed = attend_backward(mixed_back, logs_back, grad_heads, head_count)
    grad_qkv = contract_rows(grad_mixed, rows_one_back)
    grad_attn_rows, grad_map = sum_and_spread(
        jnp.concatenate([grad_out, grad_qkv], axis=0), map_slab, 3
    )
    grad_map = grad_map[:DT]
    grad_out, grad_qkv = grad_attn_rows[:shard_width], grad_attn_rows[shard_width:]
    grad_fc = grad_fc.reshape(DS, shard_hidden)
    def to_tall(mat):
        return mat.transpose(1, 2, 0).reshape(-1, DS)

    def from_tall(mat):
        return mat.reshape(3, shard_width, DS).transpose(2, 0, 1)

    moments = [
        MOMENTUM * to_tall(mom_qkv) + grad_qkv,
        MOMENTUM * mom_out + grad_out,
        MOMENTUM * mom_fc + grad_fc,
        MOMENTUM * mom_proj + grad_proj,
    ]
    moment_map = MOMENTUM * mom_map.T + grad_map
    dp_count = lax.axis_size("dp")
    dp_rank = lax.axis_index("dp")
    slice_rows = DS // dp_count
    first_row = dp_rank * slice_rows
    talls = [moments[0], moments[1], moments[2], moments[3], moment_map]
    sums = [0, 0, 1, 0, 0]

    def gram_rows(tall, axis):
        return lax.dot_general(
            lax.dynamic_slice_in_dim(tall, first_row, slice_rows, 1 - axis),
            tall,
            (((axis,), (axis,)), ((), ())),
            precision=HIGH,
            preferred_element_type=jnp.float32,
        )

    parts = jnp.concatenate([gram_rows(talls[i], sums[i]) for i in range(4)], axis=0)
    gram_mat = share_gram(parts, gram_rows(talls[4], sums[4]), 9)
    gram_mat, grad_mixed = lax.optimization_barrier((gram_mat, grad_mixed))
    grad_normed_one = student_reduce(grad_mixed, w_qkv, 1)
    mine = dp_rank % 2
    factor_mat = orthogonal_factor(gram_mat)
    pair_rows = lax.dynamic_slice_in_dim(factor_mat, (dp_rank // 2) * 2 * slice_rows, 2 * slice_rows, 0)
    other_rows = lax.ppermute(
        pair_rows, "dp", [(i, i ^ 1) for i in range(dp_count)]
    )
    even_rows = jnp.where(mine == 0, pair_rows, other_rows)
    odd_rows = jnp.where(mine == 0, other_rows, pair_rows)
    even_rows = lax.dynamic_slice_in_dim(even_rows, mine * slice_rows, slice_rows, 0)
    odd_rows = lax.dynamic_slice_in_dim(odd_rows, mine * slice_rows, slice_rows, 0)
    even_rows, grad_normed_one = lax.optimization_barrier((even_rows, grad_normed_one))
    factor_rows = line_gather(even_rows, 10).reshape(groups, slice_rows, DS)
    input_grad = grad_resid + norm_back(grad_normed_one, unit_one, scale_one, s_norms[0])
    norm_grads = jnp.stack(
        [
            jnp.sum(grad_normed_one * unit_one, axis=0),
            jnp.sum(grad_normed_one, axis=0),
            jnp.sum(grad_normed_two * unit_two, axis=0),
            jnp.sum(grad_normed_two, axis=0),
        ]
    )
    small = jnp.concatenate(
        [norm_grads, jnp.full((4, DS), loss_part, jnp.float32)], axis=0
    )
    small = sum_small(small, 4)
    norm_grads = small[:4]
    loss = small[4, 0] / (count_val * DT)

    def piece_of(index, rows):
        return lax.dot_general(
            rows,
            talls[index],
            (((1,), (1 - sums[index],)), ((), ())),
            precision=lax.Precision.HIGH,
            preferred_element_type=jnp.float32,
        ).astype(jnp.bfloat16)

    map_all = lax.all_gather(piece_of(4, odd_rows), "dp", axis=0, tiled=True)
    pieces = [piece_of(i, factor_rows[i]) for i in (2, 3, 1, 0)]
    iterate_all = lax.all_gather(jnp.concatenate(pieces, axis=1), "dp", axis=0, tiled=True)
    weight_fc, weight_proj, weight_out, weight_qkv, weight_map = renew(
        iterate_all,
        map_all,
        (s_fc, s_proj, s_out, to_tall(s_qkv), s_map.T),
        [piece.shape[1] for piece in pieces] + [DT],
        [False, True, True, True, True],
        [math.sqrt(FS / DS), 1.0, 1.0, math.sqrt(3.0), math.sqrt(DT / DS)],
    )
    norm_first = BETA_ONE * adam_first + (1.0 - BETA_ONE) * norm_grads
    norm_second = BETA_TWO * adam_second + (1.0 - BETA_TWO) * norm_grads * norm_grads
    fix_one = 1.0 - BETA_ONE**STEP
    fix_two = 1.0 - BETA_TWO**STEP
    norm_values = s_norms - ADAM_RATE * (
        norm_first / fix_one / (jnp.sqrt(norm_second / fix_two) + ADAM_EPS) + ADAM_DECAY * s_norms
    )
    return (
        teacher_out,
        student_out,
        input_grad,
        loss,
        from_tall(grad_qkv),
        grad_out,
        grad_fc,
        grad_proj,
        grad_map.T,
        from_tall(moments[0]),
        moments[1],
        moments[2],
        moments[3],
        moment_map.T,
        from_tall(weight_qkv),
        weight_out,
        weight_fc,
        weight_proj,
        weight_map.T,
        norm_first,
        norm_second,
        norm_values,
    )


def solution(mesh):
    return jax.shard_map(
        body,
        mesh=mesh,
        in_specs=(
            P(("dp", "tensor"), None),
            P(("dp", "tensor"), None),
            P(("dp", "tensor")),
            P("dp"),
            P(),
            P(),
            P(None, None, "tensor"),
            P("tensor", None),
            P(None, "tensor"),
            P("tensor", None),
            P(),
            P(None, None, "tensor"),
            P("tensor", None),
            P(None, "tensor"),
            P("tensor", None),
            P(),
            P(None, None, "tensor"),
            P("tensor", None),
            P(None, "tensor"),
            P("tensor", None),
            P(),
            P(),
            P(),
        ),
        out_specs=(
            P(("dp", "tensor"), None),
            P(("dp", "tensor"), None),
            P(("dp", "tensor"), None),
            P(),
            P(None, None, "tensor"),
            P("tensor", None),
            P(None, "tensor"),
            P("tensor", None),
            P(),
            P(None, None, "tensor"),
            P("tensor", None),
            P(None, "tensor"),
            P("tensor", None),
            P(),
            P(None, None, "tensor"),
            P("tensor", None),
            P(None, "tensor"),
            P("tensor", None),
            P(),
            P(),
            P(),
            P(),
        ),
        check_vma=False,
    )
```

```python
import functools
import math

import jax
import jax.numpy as jnp
from jax import lax
from jax.experimental import pallas as pl
from jax.experimental.pallas import tpu as pltpu
from jax.sharding import PartitionSpec as P

DT = 1600
HT = 25
DS = 768
FS = 3072
HEAD = 64
LEN = 1024
STEP = 10
ABLK = 256


EPS = 1e-05
NS_A = 3.4445
NS_B = -4.775
NS_C = 2.0315
MOMENTUM = 0.95
MUON_RATE = 0.5
MUON_DECAY = 0.01
ADAM_RATE = 0.3
BETA_ONE = 0.9
BETA_TWO = 0.999
ADAM_EPS = 1e-08
ADAM_DECAY = 0.01
REPLAY_CUT = 0.5
NEG_FILL = -1e30
HIGH = lax.Precision.HIGHEST


def norm_parts(v, gain_vec, shift_vec):
    row_mean = jnp.mean(v, axis=-1, keepdims=True)
    centred = v - row_mean
    row_var = jnp.mean(centred * centred, axis=-1, keepdims=True)
    inv_scale = lax.rsqrt(row_var + EPS)
    unit_val = centred * inv_scale
    return (unit_val * gain_vec + shift_vec, unit_val, inv_scale)


def norm_back(grad_norm, unit_val, inv_scale, gain_vec):
    grad_unit = grad_norm * gain_vec
    first_mean = jnp.mean(grad_unit, axis=-1, keepdims=True)
    second_mean = jnp.mean(grad_unit * unit_val, axis=-1, keepdims=True)
    return inv_scale * (grad_unit - first_mean - unit_val * second_mean)


def smooth_gelu(v):
    return 0.5 * v * (1.0 + jnp.tanh(0.7978845608028654 * (v + 0.044715 * v * v * v)))


def whole_vmem():
    return pl.BlockSpec(memory_space=pltpu.VMEM)


def nt_dot(left, right):
    return lax.dot_general(
        left, right, (((1,), (1,)), ((), ())), preferred_element_type=jnp.float32
    )


def tn_dot(left, right):
    return lax.dot_general(
        left, right, (((0,), (0,)), ((), ())), preferred_element_type=jnp.float32
    )


def plain_dot(left, right):
    return jnp.dot(left, right, preferred_element_type=jnp.float32)


def lower_mask():
    row_pos = lax.broadcasted_iota(jnp.int32, (ABLK, ABLK), 0)
    key_pos = lax.broadcasted_iota(jnp.int32, (ABLK, ABLK), 1)
    return key_pos <= row_pos


def attend_forward_kernel(head_count, qkv_ref, out_ref, log_ref):
    width = head_count * HEAD
    for head in range(head_count):
        cols = slice(head * HEAD, (head + 1) * HEAD)
        keys = qkv_ref[:, width + head * HEAD : width + (head + 1) * HEAD]
        values = qkv_ref[:, 2 * width + head * HEAD : 2 * width + (head + 1) * HEAD]
        for block in range(LEN // ABLK):
            low, high = block * ABLK, (block + 1) * ABLK
            query = qkv_ref[low:high, cols]
            near = nt_dot(query, keys[low:high]) * HEAD ** (-0.5)
            near = jnp.where(lower_mask(), near, NEG_FILL)
            row_top = jnp.max(near, axis=-1, keepdims=True)
            if block:
                far = nt_dot(query, keys[:low]) * HEAD ** (-0.5)
                row_top = jnp.maximum(row_top, jnp.max(far, axis=-1, keepdims=True))
            near = jnp.exp(near - row_top)
            row_total = jnp.sum(near, axis=-1, keepdims=True)
            if block:
                far = jnp.exp(far - row_top)
                row_total = row_total + jnp.sum(far, axis=-1, keepdims=True)
            inverse = 1.0 / row_total
            mixed = plain_dot((near * inverse).astype(jnp.bfloat16), values[low:high])
            if block:
                mixed = mixed + plain_dot((far * inverse).astype(jnp.bfloat16), values[:low])
            out_ref[low:high, cols] = mixed.astype(out_ref.dtype)
            log_ref[low:high, head : head + 1] = row_top + jnp.log(row_total)


def attend_forward(mixed_qkv, head_count):
    width = head_count * HEAD
    return pl.pallas_call(
        functools.partial(attend_forward_kernel, head_count),
        out_shape=(
            jax.ShapeDtypeStruct((LEN, width), jnp.bfloat16),
            jax.ShapeDtypeStruct((LEN, 128), jnp.float32),
        ),
        in_specs=[whole_vmem()],
        out_specs=(whole_vmem(), whole_vmem()),
        compiler_params=pltpu.CompilerParams(vmem_limit_bytes=40 * 2**20),
        cost_estimate=pl.CostEstimate(
            flops=4 * head_count * LEN * LEN * HEAD * 4,
            bytes_accessed=LEN * width * 8,
            transcendentals=head_count * LEN * LEN // 2,
        ),
    )(mixed_qkv)


def attend_backward_kernel(
    head_count, qkv_ref, log_ref, grad_ref, out_ref, key_acc, value_acc
):
    width = head_count * HEAD
    scale = HEAD ** (-0.5)
    for head in range(head_count):
        cols = slice(head * HEAD, (head + 1) * HEAD)
        key_cols = slice(width + head * HEAD, width + (head + 1) * HEAD)
        value_cols = slice(2 * width + head * HEAD, 2 * width + (head + 1) * HEAD)
        keys = qkv_ref[:, key_cols]
        values = qkv_ref[:, value_cols]
        for block in range(LEN // ABLK - 1, -1, -1):
            low, high = block * ABLK, (block + 1) * ABLK
            query = qkv_ref[low:high, cols]
            grad = grad_ref[low:high, cols]
            log_sum = log_ref[low:high, head : head + 1]
            near = nt_dot(query, keys[low:high]) * scale
            near = jnp.exp(jnp.where(lower_mask(), near, NEG_FILL) - log_sum)
            near_back = nt_dot(grad, values[low:high])
            inner = jnp.sum(near * near_back, axis=-1, keepdims=True)
            if block:
                far = jnp.exp(nt_dot(query, keys[:low]) * scale - log_sum)
                far_back = nt_dot(grad, values[:low])
                inner = inner + jnp.sum(far * far_back, axis=-1, keepdims=True)
            near_score = (near * (near_back - inner)).astype(jnp.bfloat16)
            grad_query = plain_dot(near_score, keys[low:high])
            near_key = tn_dot(near_score, query)
            near_value = tn_dot(near.astype(jnp.bfloat16), grad)
            if block == LEN // ABLK - 1:
                key_acc[low:high, :] = near_key
                value_acc[low:high, :] = near_value
            else:
                key_acc[low:high, :] += near_key
                value_acc[low:high, :] += near_value
            if block:
                far_score = (far * (far_back - inner)).astype(jnp.bfloat16)
                grad_query = grad_query + plain_dot(far_score, keys[:low])
                far_key = tn_dot(far_score, query)
                far_value = tn_dot(far.astype(jnp.bfloat16), grad)
                if block == LEN // ABLK - 1:
                    key_acc[:low, :] = far_key
                    value_acc[:low, :] = far_value
                else:
                    key_acc[:low, :] += far_key
                    value_acc[:low, :] += far_value
            out_ref[low:high, cols] = (grad_query * scale).astype(jnp.bfloat16)
        out_ref[:, key_cols] = (key_acc[...] * scale).astype(jnp.bfloat16)
        out_ref[:, value_cols] = value_acc[...].astype(jnp.bfloat16)


def attend_backward(mixed_qkv, log_sums, grad_heads, head_count):
    width = head_count * HEAD
    return pl.pallas_call(
        functools.partial(attend_backward_kernel, head_count),
        out_shape=jax.ShapeDtypeStruct((LEN, 3 * width), jnp.bfloat16),
        in_specs=[whole_vmem()] * 3,
        out_specs=whole_vmem(),
        scratch_shapes=[pltpu.VMEM((LEN, HEAD), jnp.float32)] * 2,
        compiler_params=pltpu.CompilerParams(vmem_limit_bytes=40 * 2**20),
        cost_estimate=pl.CostEstimate(
            flops=10 * head_count * LEN * LEN * HEAD * 4,
            bytes_accessed=LEN * width * 16,
            transcendentals=head_count * LEN * LEN // 2,
        ),
    )(mixed_qkv, log_sums, grad_heads)


MESH_ID = pl.DeviceIdType.MESH


def place_of():
    dp_count = lax.axis_size("dp")
    rank = lax.axis_index("dp")
    return dp_count // 2, rank // 2, rank % 2, lax.axis_index("tensor")


def greet(peers):
    barrier = pltpu.get_barrier_semaphore()
    for peer in peers:
        pl.semaphore_signal(barrier, inc=1, device_id=peer, device_id_type=MESH_ID)
    pl.semaphore_wait(barrier, len(peers))


def send_to(src, dst, send_sem, recv_sem, peer):
    return pltpu.make_async_remote_copy(
        src_ref=src,
        dst_ref=dst,
        send_sem=send_sem,
        recv_sem=recv_sem,
        device_id=peer,
        device_id_type=MESH_ID,
    )


def small_peers():
    chips, chip, core, depth = place_of()
    depths = lax.axis_size("tensor")
    flat = [((lax.rem(chip + k, chips)) * 2 + core, depth) for k in range(1, chips)]
    deep = [(chip * 2 + core, lax.rem(depth + k, depths)) for k in range(1, depths)]
    return [(chip * 2 + 1 - core, depth)] + flat + deep


def exchange_small(
    x_ref, out_ref, pair, plane, line, pair_sems, plane_sems, line_sems
):
    chips, chip, core, depth = place_of()
    depths = lax.axis_size("tensor")
    sibling = (chip * 2 + 1 - core, depth)
    flat = [((lax.rem(chip + k, chips)) * 2 + core, depth) for k in range(1, chips)]
    deep = [(chip * 2 + core, lax.rem(depth + k, depths)) for k in range(1, depths)]
    copy = send_to(x_ref, pair, pair_sems.at[0], pair_sems.at[1], sibling)
    copy.start()
    copy.wait()
    plane[chip] = x_ref[...] + pair[...]
    copies = []
    for k in range(1, chips):
        copies.append(
            send_to(
                plane.at[chip], plane.at[chip], plane_sems.at[0, k], plane_sems.at[1, k], flat[k - 1]
            )
        )
    for copy in copies:
        copy.start()
    for copy in copies:
        copy.wait()
    total = plane[0]
    for k in range(1, chips):
        total = total + plane[k]
    line[depth] = total
    copies = []
    for k in range(1, depths):
        copies.append(
            send_to(
                line.at[depth], line.at[depth], line_sems.at[0, k], line_sems.at[1, k], deep[k - 1]
            )
        )
    for copy in copies:
        copy.start()
    for copy in copies:
        copy.wait()
    total = line[0]
    for k in range(1, depths):
        total = total + line[k]
    out_ref[...] = total


def sum_small_kernel(*refs):
    greet(small_peers())
    exchange_small(*refs)


def small_scratch(shape, chips, depths):
    return [
        pltpu.VMEM(shape, jnp.float32),
        pltpu.VMEM((chips,) + shape, jnp.float32),
        pltpu.VMEM((depths,) + shape, jnp.float32),
        pltpu.SemaphoreType.DMA((2,)),
        pltpu.SemaphoreType.DMA((2, chips)),
        pltpu.SemaphoreType.DMA((2, depths)),
    ]


def sum_small(block, collective):
    chips, depths = lax.axis_size("dp") // 2, lax.axis_size("tensor")
    return pl.pallas_call(
        sum_small_kernel,
        out_shape=jax.ShapeDtypeStruct(block.shape, jnp.float32),
        in_specs=[whole_vmem()],
        out_specs=whole_vmem(),
        scratch_shapes=small_scratch(block.shape, chips, depths),
        compiler_params=pltpu.CompilerParams(
            collective_id=collective, has_side_effects=True, vmem_limit_bytes=16 * 2**20
        ),
        cost_estimate=pl.CostEstimate(flops=10**10, bytes_accessed=10**6, transcendentals=0),
    )(block)


def sum_and_spread_kernel(
    x_ref,
    y_ref,
    x_out,
    y_out,
    pair_in,
    pair_sum,
    plane_in,
    total,
    line_in,
    line_out,
    pair_sems,
    plane_sems,
    line_sems,
    spread_sems,
    share_sems,
):
    chips, chip, core, depth = place_of()
    depths = lax.axis_size("tensor")
    rank = chip * 2 + core
    other = 1 - core
    sibling = (chip * 2 + other, depth)
    chip_at = [lax.rem(chip + k, chips) for k in range(chips)]
    flat = [(chip_at[k] * 2 + core, depth) for k in range(chips)]
    deep = [(rank, lax.rem(depth + k, depths)) for k in range(depths)]
    greet([sibling] + flat[1:] + deep[1:])
    part = y_ref.shape[0] // depths
    part_of = [
        pl.ds(pl.multiple_of(lax.rem(depth + k, depths) * part, 8), part) for k in range(depths)
    ]
    halves = [slice(0, y_ref.shape[1] // 2), slice(y_ref.shape[1] // 2, y_ref.shape[1])]
    firsts, seconds = {}, {}
    for c in range(2):
        for k in range(1, depths):
            firsts[c, k] = send_to(
                y_ref.at[part_of[k], halves[c]],
                line_in.at[k, :, halves[c]],
                line_sems.at[c, 0, k],
                line_sems.at[c, 1, k],
                deep[k],
            )
            firsts[c, k].start()
    order = list(range(1, chips)) + [0]
    pair_copies, plane_copies = {}, {}
    for k in order:
        pair_copies[k] = send_to(
            x_ref.at[chip_at[k] * 2 + other],
            pair_in.at[k],
            pair_sems.at[0, k],
            pair_sems.at[1, k],
            sibling,
        )
        pair_copies[k].start()
    for k in order:
        pair_copies[k].wait_recv()
        pair_sum[k] = x_ref[chip_at[k] * 2 + core] + pair_in[k]
        if k:
            plane_copies[k] = send_to(
                pair_sum.at[k], plane_in.at[k], plane_sems.at[0, k], plane_sems.at[1, k], flat[k]
            )
            plane_copies[k].start()
    for c in range(2):
        value = y_ref[part_of[0], halves[c]]
        for k in range(1, depths):
            firsts[c, k].wait_recv()
            value = value + line_in[k, :, halves[c]]
        line_out[part_of[0], halves[c]] = value
        for k in range(1, depths):
            seconds[c, k] = send_to(
                line_out.at[part_of[0], halves[c]],
                line_out.at[part_of[0], halves[c]],
                line_sems.at[c, 2, k],
                line_sems.at[c, 3, k],
                deep[k],
            )
            seconds[c, k].start()
    value = pair_sum[0]
    for k in range(1, chips):
        plane_copies[k].wait_recv()
        value = value + plane_in[k]
    total[...] = value
    square = chips == 4
    row, col = chip // 2, lax.rem(chip, 2)
    if square:
        from_chip = [chip, 2 * row + 1 - col, 2 * (1 - row) + col, 2 * (1 - row) + 1 - col]
        peers = [(c * 2 + core, depth) for c in from_chip]
    else:
        from_chip = [lax.rem(chip + chips - k, chips) for k in range(chips)]
        peers = flat

    def begin(src, dst, sems, cols):
        copies = {}
        for k in (1, 2) if square else range(1, chips):
            copies[k] = send_to(
                src.at[:, cols], dst.at[rank, :, cols], sems.at[0, k], sems.at[1, k], peers[k]
            )
            copies[k].start()
        return copies

    def pass_on(dst, copies, sems, cols, via):
        if square:
            copies[via].wait_recv()
            held = dst.at[from_chip[via] * 2 + core, :, cols]
            copies[3] = send_to(held, held, sems.at[0, 3], sems.at[1, 3], peers[3 - via])
            copies[3].start()

    def share(dst, copies, sems, cols, via):
        shares = {}
        for k in (0, via, 3 - via, 3) if square else range(chips):
            if k and not (square and k == via):
                copies[k].wait_recv()
            held = dst.at[from_chip[k] * 2 + core, :, cols]
            shares[k] = send_to(held, held, sems.at[0, k], sems.at[1, k], sibling)
            shares[k].start()
        return shares

    x_out[rank] = value
    x_spread = [begin(total, x_out, spread_sems.at[2 + c], halves[c]) for c in range(2)]
    y_spread = []
    for c in range(2):
        for k in range(1, depths):
            seconds[c, k].wait_recv()
        y_out[rank, :, halves[c]] = line_out[:, halves[c]]
        y_spread.append(begin(line_out, y_out, spread_sems.at[c], halves[c]))
        if c == 0:
            for i in range(2):
                pass_on(x_out, x_spread[i], spread_sems.at[2 + i], halves[i], 1 + i)
    for c in range(2):
        pass_on(y_out, y_spread[c], spread_sems.at[c], halves[c], 1 + c)
    shares = [
        share(x_out, x_spread[c], share_sems.at[2 + c], halves[c], 1 + c) for c in range(2)
    ] + [share(y_out, y_spread[c], share_sems.at[c], halves[c], 1 + c) for c in range(2)]
    for k in range(chips):
        for copies in shares:
            copies[k].wait_recv()
    for copies in [pair_copies, plane_copies, firsts, seconds] + x_spread + y_spread + shares:
        for copy in copies.values():
            copy.wait_send()


def sum_and_spread(rows, slab_y, collective):
    dp_count, depths = lax.axis_size("dp"), lax.axis_size("tensor")
    chips = dp_count // 2
    count, width = rows.shape
    slab = (count // dp_count, width)
    out_x, out_y = pl.pallas_call(
        sum_and_spread_kernel,
        out_shape=(
            jax.ShapeDtypeStruct((dp_count,) + slab, jnp.float32),
            jax.ShapeDtypeStruct((dp_count,) + slab_y.shape, jnp.float32),
        ),
        in_specs=[whole_vmem()] * 2,
        out_specs=(whole_vmem(), whole_vmem()),
        scratch_shapes=[
            pltpu.VMEM((chips,) + slab, jnp.float32),
            pltpu.VMEM((chips,) + slab, jnp.float32),
            pltpu.VMEM((chips,) + slab, jnp.float32),
            pltpu.VMEM(slab, jnp.float32),
            pltpu.VMEM((depths, slab_y.shape[0] // depths, width), jnp.float32),
            pltpu.VMEM(slab_y.shape, jnp.float32),
            pltpu.SemaphoreType.DMA((2, chips)),
            pltpu.SemaphoreType.DMA((2, chips)),
            pltpu.SemaphoreType.DMA((2, 4, depths)),
            pltpu.SemaphoreType.DMA((4, 2, chips)),
            pltpu.SemaphoreType.DMA((4, 2, chips)),
        ],
        compiler_params=pltpu.CompilerParams(
            collective_id=collective, has_side_effects=True, vmem_limit_bytes=32 * 2**20
        ),
        cost_estimate=pl.CostEstimate(
            flops=60 * 10**9, bytes_accessed=count * width * 16, transcendentals=0
        ),
    )(rows.reshape((dp_count,) + slab), slab_y)
    return out_x.reshape(count, width), out_y.reshape(-1, width)


def scatter_rows_kernel(
    x_ref, out_ref, pair_in, pair_sum, plane_in, pair_sems, plane_sems
):
    chips, chip, core, depth = place_of()
    other = 1 - core
    sibling = (chip * 2 + other, depth)
    chip_at = [lax.rem(chip + k, chips) for k in range(chips)]
    flat = [(chip_at[k] * 2 + core, depth) for k in range(chips)]
    greet([sibling] + flat[1:])
    order = list(range(1, chips)) + [0]
    pair_copies, plane_copies = {}, {}
    for k in order:
        pair_copies[k] = send_to(
            x_ref.at[chip_at[k] * 2 + other],
            pair_in.at[k],
            pair_sems.at[0, k],
            pair_sems.at[1, k],
            sibling,
        )
        pair_copies[k].start()
    for k in order:
        pair_copies[k].wait_recv()
        pair_sum[k] = x_ref[chip_at[k] * 2 + core] + pair_in[k]
        if k:
            plane_copies[k] = send_to(
                pair_sum.at[k], plane_in.at[k], plane_sems.at[0, k], plane_sems.at[1, k], flat[k]
            )
            plane_copies[k].start()
    value = pair_sum[0]
    for k in range(1, chips):
        plane_copies[k].wait_recv()
        value = value + plane_in[k]
    out_ref[...] = value
    for copies in (pair_copies, plane_copies):
        for copy in copies.values():
            copy.wait_send()


def pad_rows(rows, unit):
    have, width = rows.shape
    padded = -(-have // unit) * unit
    if padded == have:
        return rows
    return jnp.concatenate([rows, jnp.zeros((padded - have, width), rows.dtype)], axis=0)


def scatter_rows(rows, collective):
    dp_count = lax.axis_size("dp")
    chips = dp_count // 2
    slab = (rows.shape[0] // dp_count, rows.shape[1])
    return pl.pallas_call(
        scatter_rows_kernel,
        out_shape=jax.ShapeDtypeStruct(slab, jnp.float32),
        in_specs=[whole_vmem()],
        out_specs=whole_vmem(),
        scratch_shapes=[
            pltpu.VMEM((chips,) + slab, jnp.float32),
            pltpu.VMEM((chips,) + slab, jnp.float32),
            pltpu.VMEM((chips,) + slab, jnp.float32),
            pltpu.SemaphoreType.DMA((2, chips)),
            pltpu.SemaphoreType.DMA((2, chips)),
        ],
        compiler_params=pltpu.CompilerParams(
            collective_id=collective, has_side_effects=True, vmem_limit_bytes=32 * 2**20
        ),
        cost_estimate=pl.CostEstimate(
            flops=rows.shape[0] * 15 * 10**6,
            bytes_accessed=rows.shape[0] * rows.shape[1] * 4,
            transcendentals=0,
        ),
    )(rows.reshape((dp_count,) + slab))


def start_spread(src, out_ref, sems, flat, rank, cols=slice(None)):
    copies = {}
    for k in range(1, len(flat)):
        copies[k] = send_to(
            src.at[:, cols], out_ref.at[rank, :, cols], sems.at[0, k], sems.at[1, k], flat[k]
        )
        copies[k].start()
    return copies


def start_share(out_ref, spread_copies, sems, place, sibling, cols=slice(None)):
    chips, chip, core = place
    copies = {}
    for k in range(chips):
        if k:
            spread_copies[k].wait_recv()
        held = lax.rem(chip + chips - k, chips) * 2 + core
        copies[k] = send_to(
            out_ref.at[held, :, cols],
            out_ref.at[held, :, cols],
            sems.at[0, k],
            sems.at[1, k],
            sibling,
        )
        copies[k].start()
    return copies


def spread_kernel(x_ref, out_ref, spread_sems, share_sems):
    chips, chip, core, depth = place_of()
    rank = chip * 2 + core
    sibling = (chip * 2 + 1 - core, depth)
    flat = [(lax.rem(chip + k, chips) * 2 + core, depth) for k in range(chips)]
    greet([sibling] + flat[1:])
    spread_copies = start_spread(x_ref, out_ref, spread_sems, flat, rank)
    out_ref[rank] = x_ref[...]
    share_copies = start_share(out_ref, spread_copies, share_sems, (chips, chip, core), sibling)
    for k in range(chips):
        share_copies[k].wait_recv()
    for copies in (spread_copies, share_copies):
        for copy in copies.values():
            copy.wait_send()


def spread(slab, collective):
    dp_count = lax.axis_size("dp")
    chips = dp_count // 2
    each, width = slab.shape
    full = pl.pallas_call(
        spread_kernel,
        out_shape=jax.ShapeDtypeStruct((dp_count, each, width), slab.dtype),
        in_specs=[whole_vmem()],
        out_specs=whole_vmem(),
        scratch_shapes=[
            pltpu.SemaphoreType.DMA((2, chips)),
            pltpu.SemaphoreType.DMA((2, chips)),
        ],
        compiler_params=pltpu.CompilerParams(
            collective_id=collective, has_side_effects=True, vmem_limit_bytes=16 * 2**20
        ),
        cost_estimate=pl.CostEstimate(
            flops=35 * 10**9, bytes_accessed=dp_count * each * width * 4, transcendentals=0
        ),
    )(slab)
    return full.reshape(dp_count * each, width)


def line_steps(x_ref, out_ref, right_send, right_recv, left_send, left_recv):
    rank = lax.axis_index("dp")
    depth = lax.axis_index("tensor")
    last = lax.axis_size("tensor") - 1
    right, left = (rank, depth + 1), (rank, depth - 1)

    def to_right(step):
        src = x_ref if step == 0 else out_ref.at[depth - step]
        return send_to(
            src, out_ref.at[depth - step], right_send.at[step], right_recv.at[step], right
        )

    def to_left(step):
        src = x_ref if step == 0 else out_ref.at[depth + step]
        return send_to(src, out_ref.at[depth + step], left_send.at[step], left_recv.at[step], left)

    def send(step):
        @pl.when((depth < last) & (depth >= step))
        def _():
            to_right(step).start()

        @pl.when((depth > 0) & (depth + step <= last))
        def _():
            to_left(step).start()

        if step == 0:
            out_ref[depth] = x_ref[...]

    def receive(step):
        @pl.when(depth - 1 >= step)
        def _():
            send_to(
                x_ref,
                out_ref.at[depth - 1 - step],
                right_send.at[step],
                right_recv.at[step],
                left,
            ).wait_recv()

        @pl.when(depth + 1 + step <= last)
        def _():
            send_to(
                x_ref, out_ref.at[depth + 1 + step], left_send.at[step], left_recv.at[step], right
            ).wait_recv()

    def finish():
        for step in range(last):

            @pl.when((depth < last) & (depth >= step))
            def _():
                to_right(step).wait_send()

            @pl.when((depth > 0) & (depth + step <= last))
            def _():
                to_left(step).wait_send()

    return send, receive, finish


def line_gather_kernel(x_ref, out_ref, *sems):
    last = lax.axis_size("tensor") - 1
    greet_line(lax.axis_index("tensor"), last, lax.axis_index("dp"))
    send, receive, finish = line_steps(x_ref, out_ref, *sems)
    for step in range(last):
        send(step)
        receive(step)
    finish()


def first_gather_kernel(
    head_count,
    x_ref,
    y_ref,
    t_ref,
    weight_ref,
    rows_ref,
    small_ref,
    tall_ref,
    qkv_ref,
    heads_ref,
    log_ref,
    pair,
    plane,
    line,
    pair_sems,
    plane_sems,
    line_sems,
    *sems,
):
    last = lax.axis_size("tensor") - 1
    greet(small_peers())
    send, receive, finish = line_steps(x_ref, rows_ref, *sems[:4])
    send_tall, receive_tall, finish_tall = line_steps(t_ref, tall_ref, *sems[4:])
    count = x_ref.shape[0]
    for step in range(last):
        send(step)
        if step == 0:
            exchange_small(y_ref, small_ref, pair, plane, line, pair_sems, plane_sems, line_sems)
        if step == 1:
            send_tall(0)
        receive(step)
    receive_tall(0)
    send_tall(1)
    for j in range(last + 1):
        qkv_ref[j * count : (j + 1) * count, :] = plain_dot(
            rows_ref[j], weight_ref[...]
        ).astype(jnp.bfloat16)
    attend_forward_kernel(head_count, qkv_ref, heads_ref, log_ref)
    for step in range(1, last):
        receive_tall(step)
        if step + 1 < last:
            send_tall(step + 1)
    finish()
    finish_tall()


def first_gather(block, small, tall, weight, head_count, collective):
    chips, depths = lax.axis_size("dp") // 2, lax.axis_size("tensor")
    rows, width = block.shape
    outs = pl.pallas_call(
        functools.partial(first_gather_kernel, head_count),
        out_shape=(
            jax.ShapeDtypeStruct((depths, rows, width), block.dtype),
            jax.ShapeDtypeStruct(small.shape, jnp.float32),
            jax.ShapeDtypeStruct((depths,) + tall.shape, tall.dtype),
            jax.ShapeDtypeStruct((LEN, weight.shape[1]), jnp.bfloat16),
            jax.ShapeDtypeStruct((LEN, head_count * HEAD), jnp.bfloat16),
            jax.ShapeDtypeStruct((LEN, 128), jnp.float32),
        ),
        in_specs=[whole_vmem()] * 4,
        out_specs=tuple(whole_vmem() for _ in range(6)),
        scratch_shapes=small_scratch(small.shape, chips, depths)
        + [pltpu.SemaphoreType.DMA((depths,))] * 8,
        compiler_params=pltpu.CompilerParams(
            collective_id=collective, has_side_effects=True, vmem_limit_bytes=40 * 2**20
        ),
        cost_estimate=pl.CostEstimate(
            flops=80 * 10**9, bytes_accessed=depths * tall.size * 4, transcendentals=0
        ),
    )(block, small, tall, weight)
    return (
        outs[0].reshape(depths * rows, width),
        outs[1],
        outs[2].reshape(depths * rows, tall.shape[1]),
    ) + tuple(outs[3:])


def line_gather(block, collective):
    depths = lax.axis_size("tensor")
    rows, width = block.shape
    out = pl.pallas_call(
        line_gather_kernel,
        out_shape=jax.ShapeDtypeStruct((depths, rows, width), block.dtype),
        in_specs=[whole_vmem()],
        out_specs=whole_vmem(),
        scratch_shapes=[pltpu.SemaphoreType.DMA((depths,))] * 4,
        compiler_params=pltpu.CompilerParams(
            collective_id=collective, has_side_effects=True, vmem_limit_bytes=16 * 2**20
        ),
        cost_estimate=pl.CostEstimate(
            flops=25 * 10**9, bytes_accessed=depths * rows * width * 4, transcendentals=0
        ),
    )(block)
    return out.reshape(depths * rows, width)


def renew_kernel(widths, flips, gains, group_ref, map_ref, *refs):
    olds, news = refs[: len(widths)], refs[len(widths) :]
    keep_rate = 1.0 - MUON_RATE * MUON_DECAY
    offset = 0
    total = group_ref.shape[1]
    for width, flip, gain, old, new in zip(widths, flips, gains, olds, news):
        iterate_ref = group_ref
        if offset == total:
            iterate_ref, offset = map_ref, 0
        if flip:
            for first in range(0, width, 128):
                size = min(128, width - first)
                piece = iterate_ref[:, offset + first : offset + first + size]
                rows = slice(first, first + size)
                new[rows, :] = keep_rate * old[rows, :] - MUON_RATE * gain * (
                    piece.astype(jnp.float32).T
                )
        else:
            for first in range(0, old.shape[0], 128):
                rows = slice(first, first + 128)
                piece = iterate_ref[rows, offset : offset + width]
                new[rows, :] = keep_rate * old[rows, :] - MUON_RATE * gain * (
                    piece.astype(jnp.float32)
                )
        offset += width


def renew(iterate, map_iterate, olds, widths, flips, gains):
    return pl.pallas_call(
        functools.partial(renew_kernel, widths, flips, gains),
        out_shape=tuple(jax.ShapeDtypeStruct(old.shape, jnp.float32) for old in olds),
        in_specs=[whole_vmem()] * (2 + len(olds)),
        out_specs=tuple(whole_vmem() for _ in olds),
        compiler_params=pltpu.CompilerParams(vmem_limit_bytes=48 * 2**20),
        cost_estimate=pl.CostEstimate(
            flops=10**9, bytes_accessed=iterate.size * 10, transcendentals=0
        ),
    )(iterate, map_iterate, *olds)


HALF = 128
QUARTER = 64


def greet_line(depth, last, rank):
    barrier = pltpu.get_barrier_semaphore()

    @pl.when(depth < last)
    def _():
        pl.semaphore_signal(
            barrier, inc=1, device_id=(rank, depth + 1), device_id_type=MESH_ID
        )

    @pl.when(depth > 0)
    def _():
        pl.semaphore_signal(
            barrier, inc=1, device_id=(rank, depth - 1), device_id_type=MESH_ID
        )

    @pl.when((depth > 0) & (depth < last))
    def _():
        pl.semaphore_wait(barrier, 2)

    @pl.when((depth == 0) | (depth == last))
    def _():
        pl.semaphore_wait(barrier, 1)


def line_mlp_kernel(
    x_ref,
    first_ref,
    second_ref,
    out_ref,
    rows,
    parts,
    from_left,
    from_right,
    stage,
    right_sems,
    left_sems,
    row_sems,
    sum_sems,
    from_left_sems,
    from_right_sems,
):
    rank = lax.axis_index("dp")
    depth = lax.axis_index("tensor")
    last = lax.axis_size("tensor") - 1
    right, left = (rank, depth + 1), (rank, depth - 1)
    greet_line(depth, last, rank)

    def rows_right(j, h):
        return send_to(rows.at[j, h], rows.at[j, h], right_sems.at[j, h], row_sems.at[j, h], right)

    def rows_left(j, h):
        return send_to(rows.at[j, h], rows.at[j, h], left_sems.at[j, h], row_sems.at[j, h], left)

    def sum_right(j, h):
        return send_to(
            stage.at[j, h], from_left.at[j, h], sum_sems.at[j, h], from_left_sems.at[j, h], right
        )

    def sum_left(j, h):
        return send_to(
            stage.at[j, h], from_right.at[j, h], sum_sems.at[j, h], from_right_sems.at[j, h], left
        )

    for q in range(4):
        rows[depth, q] = x_ref[q * QUARTER : (q + 1) * QUARTER, :]

        @pl.when(depth < last)
        def _():
            rows_right(depth, q).start()

        @pl.when(depth > 0)
        def _():
            rows_left(depth, q).start()

    inner = depth * (last - depth) // 2
    side = depth // 2
    for step, shift in enumerate((1, 1, -2, 0)):
        base = step + inner * shift
        j = base + side * (last - 2 * base)

        def half_step(h, carry):
            for q in (2 * h, 2 * h + 1):
                if step:

                    @pl.when(j < depth)
                    def _():
                        rows_right(j, q).wait_recv()

                    @pl.when(j > depth)
                    def _():
                        rows_left(j, q).wait_recv()

                    @pl.when((j < depth) & (depth < last))
                    def _():
                        rows_right(j, q).start()

                    @pl.when((j > depth) & (depth > 0))
                    def _():
                        rows_left(j, q).start()

            block = jnp.concatenate([rows[j, 2 * h], rows[j, 2 * h + 1]], axis=0)
            hidden = smooth_gelu(plain_dot(block, first_ref[...])).astype(jnp.bfloat16)
            part = plain_dot(hidden, second_ref[...])
            for i in range(2):
                q = 2 * h + i
                piece = part[i * QUARTER : (i + 1) * QUARTER, :]
                parts[j, q] = piece
                if step:

                    @pl.when((depth == 0) | (depth == last))
                    def _():
                        stage[j, q] = piece.astype(jnp.bfloat16)

                    @pl.when(depth == 0)
                    def _():
                        sum_right(j, q).start()

                    @pl.when(depth == last)
                    def _():
                        sum_left(j, q).start()

            return carry

        lax.fori_loop(0, 2, half_step, 0)

    def relay_right(j):
        for h in range(4):
            sum_right(j, h).wait_recv()
            stage[j, h] = (parts[j, h] + from_left[j, h].astype(jnp.float32)).astype(jnp.bfloat16)
            sum_right(j, h).start()

    def relay_left(j):
        for h in range(4):
            sum_left(j, h).wait_recv()
            stage[j, h] = (parts[j, h] + from_right[j, h].astype(jnp.float32)).astype(jnp.bfloat16)
            sum_left(j, h).start()

    @pl.when(depth == 1)
    def _():
        relay_right(2)
        relay_right(3)
        relay_left(0)

    @pl.when(depth == 2)
    def _():
        relay_left(1)
        relay_left(0)
        relay_right(3)

    for h in range(4):
        span = slice(h * QUARTER, (h + 1) * QUARTER)
        out_ref[span, :] = parts[depth, h]

        @pl.when(depth > 0)
        def _():
            sum_right(depth, h).wait_recv()
            out_ref[span, :] += from_left[depth, h].astype(jnp.float32)

        @pl.when(depth < last)
        def _():
            sum_left(depth, h).wait_recv()
            out_ref[span, :] += from_right[depth, h].astype(jnp.float32)

    for j in range(4):
        for h in range(4):

            @pl.when((depth >= j) & (depth < last))
            def _():
                rows_right(j, h).wait_send()

            @pl.when((depth <= j) & (depth > 0))
            def _():
                rows_left(j, h).wait_send()

            @pl.when(depth < j)
            def _():
                sum_right(j, h).wait_send()

            @pl.when(depth > j)
            def _():
                sum_left(j, h).wait_send()


def line_mlp(block, first, second, collective):
    count, width = block.shape
    slots = (4, 4, QUARTER, width)
    return pl.pallas_call(
        line_mlp_kernel,
        out_shape=jax.ShapeDtypeStruct((count, width), jnp.float32),
        in_specs=[whole_vmem()] * 3,
        out_specs=whole_vmem(),
        scratch_shapes=[
            pltpu.VMEM(slots, jnp.bfloat16),
            pltpu.VMEM(slots, jnp.float32),
            pltpu.VMEM(slots, jnp.bfloat16),
            pltpu.VMEM(slots, jnp.bfloat16),
            pltpu.VMEM(slots, jnp.bfloat16),
        ]
        + [pltpu.SemaphoreType.DMA((4, 4))] * 6,
        compiler_params=pltpu.CompilerParams(
            collective_id=collective, has_side_effects=True, vmem_limit_bytes=48 * 2**20
        ),
        cost_estimate=pl.CostEstimate(
            flops=16 * count * width * first.shape[1] * 4,
            bytes_accessed=16 * count * width,
            transcendentals=4 * count * first.shape[1],
        ),
    )(block, first, second)


def share_gram_kernel(
    parts_ref, extra_ref, out_ref, line_in, pair_in, line_sems, pair_sems, plane_sems
):
    chips, chip, core, depth = place_of()
    depths = lax.axis_size("tensor")
    rank = chip * 2 + core
    sibling = (chip * 2 + 1 - core, depth)
    flat = [(lax.rem(chip + k, chips) * 2 + core, depth) for k in range(chips)]
    line = [lax.rem(depth + k, depths) for k in range(depths)]
    deep = [(rank, line[k]) for k in range(depths)]
    greet([sibling] + flat[1:] + deep[1:])
    copies = {}
    for k in range(1, depths):
        copies[k] = send_to(
            parts_ref.at[line[k]], line_in.at[k], line_sems.at[0, k], line_sems.at[1, k], deep[k]
        )
        copies[k].start()
    extra = send_to(extra_ref, out_ref.at[rank], pair_sems.at[0], pair_sems.at[1], sibling)
    main = send_to(pair_in, out_ref.at[rank], pair_sems.at[2], pair_sems.at[3], sibling)
    plane = {}
    for k in range(1, chips):
        plane[k] = [
            send_to(
                out_ref.at[chip * 2 + i],
                out_ref.at[chip * 2 + i],
                plane_sems.at[0, i, k],
                plane_sems.at[1, i, k],
                flat[k],
            )
            for i in range(2)
        ]

    @pl.when(core == 0)
    def _():
        extra.start()

    @pl.when(core == 1)
    def _():
        out_ref[rank] = extra_ref[...]
        extra.wait_recv()
        for k in range(1, chips):
            for i in range(2):
                plane[k][i].start()

    value = parts_ref[depth]
    for k in range(1, depths):
        copies[k].wait_recv()
        value = value + line_in[k]

    @pl.when(core == 1)
    def _():
        pair_in[...] = value
        main.start()

    @pl.when(core == 0)
    def _():
        out_ref[rank] = value
        main.wait_recv()
        for k in range(1, chips):
            for i in range(2):
                plane[k][i].start()

    for k in range(1, chips):
        for i in range(2):
            plane[k][i].wait_recv()
    for k in range(1, chips):
        for i in range(2):
            plane[k][i].wait_send()
    for k in range(1, depths):
        copies[k].wait_send()

    @pl.when(core == 0)
    def _():
        extra.wait_send()

    @pl.when(core == 1)
    def _():
        main.wait_send()


def share_gram(parts, extra, collective):
    dp_count, depths = lax.axis_size("dp"), lax.axis_size("tensor")
    chips = dp_count // 2
    slab = extra.shape
    out = pl.pallas_call(
        share_gram_kernel,
        out_shape=jax.ShapeDtypeStruct((dp_count,) + slab, jnp.float32),
        in_specs=[whole_vmem()] * 2,
        out_specs=whole_vmem(),
        scratch_shapes=[
            pltpu.VMEM((depths,) + slab, jnp.float32),
            pltpu.VMEM(slab, jnp.float32),
            pltpu.SemaphoreType.DMA((2, depths)),
            pltpu.SemaphoreType.DMA((4,)),
            pltpu.SemaphoreType.DMA((2, 2, chips)),
        ],
        compiler_params=pltpu.CompilerParams(
            collective_id=collective, has_side_effects=True, vmem_limit_bytes=16 * 2**20
        ),
        cost_estimate=pl.CostEstimate(
            flops=45 * 10**9, bytes_accessed=dp_count * slab[0] * slab[1] * 8, transcendentals=0
        ),
    )(parts.reshape((depths,) + slab), extra)
    return out.reshape(dp_count * slab[0], slab[1])


def line_exchange_kernel(
    heads_ref,
    weight_ref,
    x_ref,
    sum_ref,
    all_ref,
    y_ref,
    from_left,
    from_right,
    stage,
    right_sems,
    left_sems,
    row_sems,
    sum_sems,
    from_left_sems,
    from_right_sems,
):
    rank = lax.axis_index("dp")
    depth = lax.axis_index("tensor")
    last = lax.axis_size("tensor") - 1
    right, left = (rank, depth + 1), (rank, depth - 1)
    greet_line(depth, last, rank)

    def rows_right(j):
        return send_to(all_ref.at[j], all_ref.at[j], right_sems.at[j], row_sems.at[j], right)

    def rows_left(j):
        return send_to(all_ref.at[j], all_ref.at[j], left_sems.at[j], row_sems.at[j], left)

    def sum_right(j, h, src):
        return send_to(
            src.at[j, h], from_left.at[j, h], sum_sems.at[j, h], from_left_sems.at[j, h], right
        )

    def sum_left(j, h, src):
        return send_to(
            src.at[j, h], from_right.at[j, h], sum_sems.at[j, h], from_right_sems.at[j, h], left
        )

    all_ref[depth] = x_ref[...]

    @pl.when(depth < last)
    def _():
        rows_right(depth).start()

    @pl.when(depth > 0)
    def _():
        rows_left(depth).start()

    for j in range(4):
        for h in range(2):
            first = (2 * j + h) * HALF
            y_ref[j, h] = plain_dot(
                heads_ref[first : first + HALF, :], weight_ref[...]
            ).astype(jnp.bfloat16)

    @pl.when(depth == 0)
    def _():
        for j in (3, 2, 1):
            for h in range(2):
                sum_right(j, h, y_ref).start()
        for j in (1, 2, 3):
            rows_left(j).wait_recv()

    @pl.when(depth == last)
    def _():
        for j in (0, 1, 2):
            for h in range(2):
                sum_left(j, h, y_ref).start()
        for j in (2, 1, 0):
            rows_right(j).wait_recv()

    def relay_right(j):
        for h in range(2):
            sum_right(j, h, stage).wait_recv()
            stage[j, h] = (
                y_ref[j, h].astype(jnp.float32) + from_left[j, h].astype(jnp.float32)
            ).astype(jnp.bfloat16)
            sum_right(j, h, stage).start()

    def relay_left(j):
        for h in range(2):
            sum_left(j, h, stage).wait_recv()
            stage[j, h] = (
                y_ref[j, h].astype(jnp.float32) + from_right[j, h].astype(jnp.float32)
            ).astype(jnp.bfloat16)
            sum_left(j, h, stage).start()

    def pass_right(j):
        rows_right(j).wait_recv()
        rows_right(j).start()

    def pass_left(j):
        rows_left(j).wait_recv()
        rows_left(j).start()

    @pl.when(depth == 1)
    def _():
        pass_left(2)
        pass_right(0)
        relay_right(3)
        pass_left(3)
        relay_left(0)
        relay_right(2)

    @pl.when(depth == 2)
    def _():
        pass_right(1)
        pass_left(3)
        relay_left(0)
        pass_right(0)
        relay_right(3)
        relay_left(1)

    for h in range(2):
        span = slice(h * HALF, (h + 1) * HALF)
        sum_ref[span, :] = y_ref[depth, h].astype(jnp.float32)

        @pl.when(depth > 0)
        def _():
            sum_right(depth, h, stage).wait_recv()
            sum_ref[span, :] += from_left[depth, h].astype(jnp.float32)

        @pl.when(depth < last)
        def _():
            sum_left(depth, h, stage).wait_recv()
            sum_ref[span, :] += from_right[depth, h].astype(jnp.float32)

    for j in range(4):

        @pl.when((depth >= j) & (depth < last))
        def _():
            rows_right(j).wait_send()

        @pl.when((depth <= j) & (depth > 0))
        def _():
            rows_left(j).wait_send()

        for h in range(2):

            @pl.when(depth < j)
            def _():
                sum_right(j, h, stage).wait_send()

            @pl.when(depth > j)
            def _():
                sum_left(j, h, stage).wait_send()


def line_exchange(heads, weight, block, collective):
    width = weight.shape[1]
    slots = (4, 2, HALF, width)
    total, rows = pl.pallas_call(
        line_exchange_kernel,
        out_shape=(
            jax.ShapeDtypeStruct((2 * HALF, width), jnp.float32),
            jax.ShapeDtypeStruct((4,) + block.shape, block.dtype),
        ),
        in_specs=[whole_vmem()] * 3,
        out_specs=(whole_vmem(), whole_vmem()),
        scratch_shapes=[pltpu.VMEM(slots, jnp.bfloat16)] * 4
        + [pltpu.SemaphoreType.DMA((4,))] * 3
        + [pltpu.SemaphoreType.DMA((4, 2))] * 3,
        compiler_params=pltpu.CompilerParams(
            collective_id=collective, has_side_effects=True, vmem_limit_bytes=32 * 2**20
        ),
        cost_estimate=pl.CostEstimate(
            flops=60 * 10**9, bytes_accessed=heads.size * 16, transcendentals=0
        ),
    )(heads, weight, block)
    return total, rows.reshape(-1, block.shape[1])


NBLK = 256


def split_store(value, high_ref, low_ref, rows, cols):
    high = value.astype(jnp.bfloat16)
    high_ref[rows, cols] = high
    low_ref[rows, cols] = (value - high.astype(jnp.float32)).astype(jnp.bfloat16)


def polynomial_kernel(gram_ref, out_ref, full_g, full_h, full_m, *pairs):
    gram_pair, half_pair, poly_pair, prod_pair = (
        pairs[0:2], pairs[2:4], pairs[4:6], pairs[6:8]
    )
    size = gram_ref.shape[0]
    blocks = size // NBLK
    spans = [slice(i * NBLK, (i + 1) * NBLK) for i in range(blocks)]
    upper = [(i, j) for i in range(blocks) for j in range(i, blocks)]

    def eye(i, j):
        if i != j:
            return 0.0
        row = lax.broadcasted_iota(jnp.int32, (NBLK, NBLK), 0)
        col = lax.broadcasted_iota(jnp.int32, (NBLK, NBLK), 1)
        return jnp.where(row == col, 1.0, 0.0)

    def place(i, j, value, full, pair):
        if full is not None:
            full[spans[i], spans[j]] = value
        if pair is not None:
            split_store(value, *pair, spans[i], spans[j])
        if i != j:
            flip = value.T
            if full is not None:
                full[spans[j], spans[i]] = flip
            if pair is not None:
                split_store(flip, *pair, spans[j], spans[i])

    def product(left, right, i, j):
        return plain_dot(left[0][spans[i], :], right[0][:, spans[j]]) + (
            plain_dot(left[0][spans[i], :], right[1][:, spans[j]])
            + plain_dot(left[1][spans[i], :], right[0][:, spans[j]])
        )

    trace = 0.0
    for i in range(blocks):
        trace = trace + jnp.sum(gram_ref[spans[i], spans[i]] * eye(i, i))
    root = jnp.sqrt(jnp.full((1, 1), trace, jnp.float32)) + 1e-07
    inverse = 1.0 / root
    for i, j in upper:
        place(i, j, gram_ref[spans[i], spans[j]] * (inverse * inverse), full_g, gram_pair)

    def make_poly():
        for i, j in upper:
            value = NS_B * full_g[spans[i], spans[j]] + NS_C * product(gram_pair, gram_pair, i, j)
            place(i, j, value, None, poly_pair)

    def advance():
        for i, j in upper:
            value = NS_A * full_g[spans[i], spans[j]] + product(poly_pair, gram_pair, i, j)
            place(i, j, value, full_h, half_pair)
        for i, j in upper:
            value = NS_A * full_h[spans[i], spans[j]] + product(poly_pair, half_pair, i, j)
            place(i, j, value, full_g, gram_pair)

    make_poly()
    for i, j in upper:
        value = (
            poly_pair[0][spans[i], spans[j]].astype(jnp.float32)
            + poly_pair[1][spans[i], spans[j]].astype(jnp.float32)
            + NS_A * eye(i, j)
        )
        place(i, j, value, full_m, prod_pair)
    advance()

    def sweep(index, carry):
        make_poly()
        for i, j in upper:
            value = NS_A * full_m[spans[i], spans[j]] + product(poly_pair, prod_pair, i, j)
            place(i, j, value, full_h, None)
        for i in range(blocks):
            full_m[spans[i], :] = full_h[spans[i], :]
            split_store(full_h[spans[i], :], *prod_pair, spans[i], slice(None))
        advance()
        return carry

    lax.fori_loop(0, 3, sweep, 0)
    make_poly()
    for i, j in upper:
        value = NS_A * full_m[spans[i], spans[j]] + product(poly_pair, prod_pair, i, j)
        place(i, j, value * inverse, out_ref, None)


def orthogonal_factor(gram_mat):
    size = gram_mat.shape[0]
    return pl.pallas_call(
        polynomial_kernel,
        out_shape=jax.ShapeDtypeStruct((size, size), jnp.float32),
        in_specs=[whole_vmem()],
        out_specs=whole_vmem(),
        scratch_shapes=[pltpu.VMEM((size, size), jnp.float32)] * 3
        + [pltpu.VMEM((size, size), jnp.bfloat16)] * 8,
        compiler_params=pltpu.CompilerParams(vmem_limit_bytes=48 * 2**20),
        cost_estimate=pl.CostEstimate(
            flops=17 * 2 * 2 * size**3, bytes_accessed=8 * size * size, transcendentals=0
        ),
    )(gram_mat)


def contract_rows(left, right):
    return lax.dot_general(
        left, right, (((0,), (0,)), ((), ())), preferred_element_type=jnp.float32
    )


def contract_cols(left, right):
    return lax.dot_general(
        left, right, (((1,), (1,)), ((), ())), preferred_element_type=jnp.float32
    )


def body(
    teacher_in,
    student_in,
    resp_mask,
    replay,
    t_gains,
    t_shifts,
    t_qkv,
    t_out,
    t_fc,
    t_proj,
    s_norms,
    s_qkv,
    s_out,
    s_fc,
    s_proj,
    s_map,
    mom_qkv,
    mom_out,
    mom_fc,
    mom_proj,
    mom_map,
    adam_first,
    adam_second,
):
    groups = lax.axis_size("tensor")
    tensor_rank = lax.axis_index("tensor")
    row_count = student_in.shape[0]
    seq_count = replay.shape[0]
    total_rows = row_count * groups
    count_block = jnp.full((8, 128), jnp.sum(resp_mask), jnp.int32).astype(jnp.float32)
    tokens_all = lax.axis_size("dp") * seq_count * LEN

    def student_gather(local_rows):
        return lax.all_gather(local_rows, "tensor", axis=0, tiled=True)

    def student_reduce(left, right, right_dim):
        return lax.psum_scatter(
            lax.dot_general(
                left, right, (((1,), (right_dim,)), ((), ())), preferred_element_type=jnp.float32
            ).astype(jnp.bfloat16),
            "tensor",
            scatter_dimension=0,
            tiled=True,
        ).astype(jnp.float32)

    teacher_x = teacher_in.astype(jnp.float32)
    slot_width = t_qkv.shape[2]
    slot_count = slot_width // HEAD
    live_count = HT // groups + (tensor_rank < HT % groups).astype(jnp.int32)
    live_slots = (jnp.arange(slot_count, dtype=jnp.int32) < live_count).astype(jnp.float32)
    teacher_normed = norm_parts(teacher_x, t_gains[0], t_shifts[0])[0].astype(jnp.bfloat16)
    student_x = student_in.astype(jnp.float32)
    shard_width = s_qkv.shape[2]
    shard_hidden = s_fc.shape[1]
    head_count = shard_width // HEAD
    w_qkv = s_qkv.astype(jnp.bfloat16).reshape(DS, 3 * shard_width)
    w_out = s_out.astype(jnp.bfloat16)
    w_fc = s_fc.astype(jnp.bfloat16)
    w_proj = s_proj.astype(jnp.bfloat16)
    w_map = s_map.astype(jnp.bfloat16)
    normed_one, unit_one, scale_one = norm_parts(student_x, s_norms[0], s_norms[1])
    low_one = normed_one.astype(jnp.bfloat16)
    rows_one, count_sum, teacher_all, mixed_qkv, head_out, log_sums = first_gather(
        low_one, count_block, teacher_normed, w_qkv, head_count, 5
    )
    count_val = count_sum[0, 0]
    factor = tokens_all / (2.0 * count_val)
    resid = student_x + student_reduce(head_out, w_out, 0)
    teacher_mixed = jnp.dot(
        teacher_all, t_qkv.reshape(DT, 3 * slot_width), preferred_element_type=jnp.float32
    ).astype(jnp.bfloat16)
    teacher_head_out = attend_forward(teacher_mixed, slot_count)[0]
    slot_mask = jnp.repeat(live_slots, HEAD)[None, :] > 0.0
    teacher_head_out = jnp.where(slot_mask, teacher_head_out, jnp.zeros_like(teacher_head_out))
    normed_two, unit_two, scale_two = norm_parts(resid, s_norms[2], s_norms[3])
    low_two = normed_two.astype(jnp.bfloat16)
    attn_part, rows_two = line_exchange(teacher_head_out, t_out, low_two, 6)
    teacher_resid = teacher_x + attn_part
    teacher_normed_two = norm_parts(teacher_resid, t_gains[1], t_shifts[1])[0].astype(jnp.bfloat16)
    mlp_part = line_mlp(teacher_normed_two, t_fc, t_proj, 8)
    teacher_out = (teacher_resid + mlp_part).astype(jnp.bfloat16)
    before = jnp.dot(rows_two, w_fc, preferred_element_type=jnp.float32)
    before, hidden = (before, smooth_gelu(before).astype(jnp.bfloat16))
    output = resid + student_reduce(hidden, w_proj, 0)
    student_out = output.astype(jnp.bfloat16)
    guess_vec = jnp.dot(student_out, w_map, preferred_element_type=jnp.float32)
    miss_vec = guess_vec - teacher_out.astype(jnp.float32)
    position = tensor_rank * row_count + jnp.arange(row_count, dtype=jnp.int32)
    seq_owner = position // LEN
    seq_pick = (seq_owner[:, None] == jnp.arange(seq_count, dtype=jnp.int32)[None, :]).astype(
        jnp.float32
    )
    flag_tok = jnp.sum(seq_pick * replay.astype(jnp.float32)[None, :], axis=1)
    weight = resp_mask.astype(jnp.float32) * (1.0 - REPLAY_CUT * flag_tok)
    loss_part = jnp.sum(weight[:, None] * miss_vec * miss_vec)
    grad_guess = (2.0 * factor * weight[:, None] * miss_vec).astype(jnp.bfloat16)
    row_unit = 8 * lax.axis_size("dp") * groups
    map_slab = scatter_rows(pad_rows(contract_rows(grad_guess, student_out), row_unit), 1)
    grad_output = contract_cols(grad_guess, w_map)
    rows_two_back, before_back, hidden_back = (rows_two, before, hidden)
    rows_one_back, mixed_back, heads_back, logs_back = (rows_one, mixed_qkv, head_out, log_sums)
    grad_mlp = student_gather(grad_output.astype(jnp.bfloat16))
    grad_mlp, map_slab = lax.optimization_barrier((grad_mlp, map_slab))
    grad_proj = contract_rows(hidden_back, grad_mlp)
    grad_hidden = contract_cols(grad_mlp, w_proj)
    gelu_vals, gelu_pull = jax.vjp(smooth_gelu, before_back)
    grad_before = gelu_pull(grad_hidden)[0].astype(jnp.bfloat16)
    grad_fc = contract_rows(rows_two_back, grad_before).reshape(-1, DS)
    mlp_slab = scatter_rows(jnp.concatenate([grad_proj, grad_fc], axis=0), 2)
    grad_normed_two = student_reduce(grad_before, w_fc, 1)
    grad_normed_two, mlp_slab = lax.optimization_barrier((grad_normed_two, mlp_slab))
    grad_resid = grad_output + norm_back(grad_normed_two, unit_two, scale_two, s_norms[2])
    grad_attn = student_gather(grad_resid.astype(jnp.bfloat16))
    grad_mlp_rows = spread(mlp_slab, 7)
    grad_attn, grad_mlp_rows = lax.optimization_barrier((grad_attn, grad_mlp_rows))
    grad_proj, grad_fc = grad_mlp_rows[:shard_hidden], grad_mlp_rows[shard_hidden:]
    grad_out = contract_rows(heads_back, grad_attn)
    grad_heads = contract_cols(grad_attn, w_out).astype(jnp.bfloat16)

    grad_mixed = attend_backward(mixed_back, logs_back, grad_heads, head_count)
    grad_qkv = contract_rows(grad_mixed, rows_one_back)
    grad_attn_rows, grad_map = sum_and_spread(
        jnp.concatenate([grad_out, grad_qkv], axis=0), map_slab, 3
    )
    grad_map = grad_map[:DT]
    grad_out, grad_qkv = grad_attn_rows[:shard_width], grad_attn_rows[shard_width:]
    grad_fc = grad_fc.reshape(DS, shard_hidden)
    def to_tall(mat):
        return mat.transpose(1, 2, 0).reshape(-1, DS)

    def from_tall(mat):
        return mat.reshape(3, shard_width, DS).transpose(2, 0, 1)

    moments = [
        MOMENTUM * to_tall(mom_qkv) + grad_qkv,
        MOMENTUM * mom_out + grad_out,
        MOMENTUM * mom_fc + grad_fc,
        MOMENTUM * mom_proj + grad_proj,
    ]
    moment_map = MOMENTUM * mom_map.T + grad_map
    dp_count = lax.axis_size("dp")
    dp_rank = lax.axis_index("dp")
    slice_rows = DS // dp_count
    first_row = dp_rank * slice_rows
    talls = [moments[0], moments[1], moments[2], moments[3], moment_map]
    sums = [0, 0, 1, 0, 0]

    def gram_rows(tall, axis):
        return lax.dot_general(
            lax.dynamic_slice_in_dim(tall, first_row, slice_rows, 1 - axis),
            tall,
            (((axis,), (axis,)), ((), ())),
            precision=HIGH,
            preferred_element_type=jnp.float32,
        )

    parts = jnp.concatenate([gram_rows(talls[i], sums[i]) for i in range(4)], axis=0)
    gram_mat = share_gram(parts, gram_rows(talls[4], sums[4]), 9)
    gram_mat, grad_mixed = lax.optimization_barrier((gram_mat, grad_mixed))
    grad_normed_one = student_reduce(grad_mixed, w_qkv, 1)
    mine = dp_rank % 2
    factor_mat = orthogonal_factor(gram_mat)
    pair_rows = lax.dynamic_slice_in_dim(factor_mat, (dp_rank // 2) * 2 * slice_rows, 2 * slice_rows, 0)
    other_rows = lax.ppermute(
        pair_rows, "dp", [(i, i ^ 1) for i in range(dp_count)]
    )
    even_rows = jnp.where(mine == 0, pair_rows, other_rows)
    odd_rows = jnp.where(mine == 0, other_rows, pair_rows)
    even_rows = lax.dynamic_slice_in_dim(even_rows, mine * slice_rows, slice_rows, 0)
    odd_rows = lax.dynamic_slice_in_dim(odd_rows, mine * slice_rows, slice_rows, 0)
    even_rows, grad_normed_one = lax.optimization_barrier((even_rows, grad_normed_one))
    factor_rows = line_gather(even_rows, 10).reshape(groups, slice_rows, DS)
    input_grad = grad_resid + norm_back(grad_normed_one, unit_one, scale_one, s_norms[0])
    norm_grads = jnp.stack(
        [
            jnp.sum(grad_normed_one * unit_one, axis=0),
            jnp.sum(grad_normed_one, axis=0),
            jnp.sum(grad_normed_two * unit_two, axis=0),
            jnp.sum(grad_normed_two, axis=0),
        ]
    )
    small = jnp.concatenate(
        [norm_grads, jnp.full((4, DS), loss_part, jnp.float32)], axis=0
    )
    small = sum_small(small, 4)
    norm_grads = small[:4]
    loss = small[4, 0] / (count_val * DT)

    def piece_of(index, rows):
        return lax.dot_general(
            rows,
            talls[index],
            (((1,), (1 - sums[index],)), ((), ())),
            precision=lax.Precision.HIGH,
            preferred_element_type=jnp.float32,
        ).astype(jnp.bfloat16)

    map_all = lax.all_gather(piece_of(4, odd_rows), "dp", axis=0, tiled=True)
    pieces = [piece_of(i, factor_rows[i]) for i in (2, 3, 1, 0)]
    iterate_all = lax.all_gather(jnp.concatenate(pieces, axis=1), "dp", axis=0, tiled=True)
    weight_fc, weight_proj, weight_out, weight_qkv, weight_map = renew(
        iterate_all,
        map_all,
        (s_fc, s_proj, s_out, to_tall(s_qkv), s_map.T),
        [piece.shape[1] for piece in pieces] + [DT],
        [False, True, True, True, True],
        [math.sqrt(FS / DS), 1.0, 1.0, math.sqrt(3.0), math.sqrt(DT / DS)],
    )
    norm_first = BETA_ONE * adam_first + (1.0 - BETA_ONE) * norm_grads
    norm_second = BETA_TWO * adam_second + (1.0 - BETA_TWO) * norm_grads * norm_grads
    fix_one = 1.0 - BETA_ONE**STEP
    fix_two = 1.0 - BETA_TWO**STEP
    norm_values = s_norms - ADAM_RATE * (
        norm_first / fix_one / (jnp.sqrt(norm_second / fix_two) + ADAM_EPS) + ADAM_DECAY * s_norms
    )
    return (
        teacher_out,
        student_out,
        input_grad,
        loss,
        from_tall(grad_qkv),
        grad_out,
        grad_fc,
        grad_proj,
        grad_map.T,
        from_tall(moments[0]),
        moments[1],
        moments[2],
        moments[3],
        moment_map.T,
        from_tall(weight_qkv),
        weight_out,
        weight_fc,
        weight_proj,
        weight_map.T,
        norm_first,
        norm_second,
        norm_values,
    )


def solution(mesh):
    return jax.shard_map(
        body,
        mesh=mesh,
        in_specs=(
            P(("dp", "tensor"), None),
            P(("dp", "tensor"), None),
            P(("dp", "tensor")),
            P("dp"),
            P(),
            P(),
            P(None, None, "tensor"),
            P("tensor", None),
            P(None, "tensor"),
            P("tensor", None),
            P(),
            P(None, None, "tensor"),
            P("tensor", None),
            P(None, "tensor"),
            P("tensor", None),
            P(),
            P(None, None, "tensor"),
            P("tensor", None),
            P(None, "tensor"),
            P("tensor", None),
            P(),
            P(),
            P(),
        ),
        out_specs=(
            P(("dp", "tensor"), None),
            P(("dp", "tensor"), None),
            P(("dp", "tensor"), None),
            P(),
            P(None, None, "tensor"),
            P("tensor", None),
            P(None, "tensor"),
            P("tensor", None),
            P(),
            P(None, None, "tensor"),
            P("tensor", None),
            P(None, "tensor"),
            P("tensor", None),
            P(),
            P(None, None, "tensor"),
            P("tensor", None),
            P(None, "tensor"),
            P("tensor", None),
            P(),
            P(),
            P(),
            P(),
        ),
        check_vma=False,
    )
```

```python
import functools
import math

import jax
import jax.numpy as jnp
from jax import lax
from jax.experimental import pallas as pl
from jax.experimental.pallas import tpu as pltpu
from jax.sharding import PartitionSpec as P

DT = 1600
HT = 25
DS = 768
FS = 3072
HEAD = 64
LEN = 1024
STEP = 10
ABLK = 256


EPS = 1e-05
NS_A = 3.4445
NS_B = -4.775
NS_C = 2.0315
MOMENTUM = 0.95
MUON_RATE = 0.5
MUON_DECAY = 0.01
ADAM_RATE = 0.3
BETA_ONE = 0.9
BETA_TWO = 0.999
ADAM_EPS = 1e-08
ADAM_DECAY = 0.01
REPLAY_CUT = 0.5
NEG_FILL = -1e30
HIGH = lax.Precision.HIGHEST


def norm_parts(v, gain_vec, shift_vec):
    row_mean = jnp.mean(v, axis=-1, keepdims=True)
    centred = v - row_mean
    row_var = jnp.mean(centred * centred, axis=-1, keepdims=True)
    inv_scale = lax.rsqrt(row_var + EPS)
    unit_val = centred * inv_scale
    return (unit_val * gain_vec + shift_vec, unit_val, inv_scale)


def norm_back(grad_norm, unit_val, inv_scale, gain_vec):
    grad_unit = grad_norm * gain_vec
    first_mean = jnp.mean(grad_unit, axis=-1, keepdims=True)
    second_mean = jnp.mean(grad_unit * unit_val, axis=-1, keepdims=True)
    return inv_scale * (grad_unit - first_mean - unit_val * second_mean)


def smooth_gelu(v):
    return 0.5 * v * (1.0 + jnp.tanh(0.7978845608028654 * (v + 0.044715 * v * v * v)))


def whole_vmem():
    return pl.BlockSpec(memory_space=pltpu.VMEM)


def nt_dot(left, right):
    return lax.dot_general(
        left, right, (((1,), (1,)), ((), ())), preferred_element_type=jnp.float32
    )


def tn_dot(left, right):
    return lax.dot_general(
        left, right, (((0,), (0,)), ((), ())), preferred_element_type=jnp.float32
    )


def plain_dot(left, right):
    return jnp.dot(left, right, preferred_element_type=jnp.float32)


def lower_mask():
    row_pos = lax.broadcasted_iota(jnp.int32, (ABLK, ABLK), 0)
    key_pos = lax.broadcasted_iota(jnp.int32, (ABLK, ABLK), 1)
    return key_pos <= row_pos


def attend_forward_kernel(head_count, qkv_ref, out_ref, log_ref):
    width = head_count * HEAD
    for head in range(head_count):
        cols = slice(head * HEAD, (head + 1) * HEAD)
        keys = qkv_ref[:, width + head * HEAD : width + (head + 1) * HEAD]
        values = qkv_ref[:, 2 * width + head * HEAD : 2 * width + (head + 1) * HEAD]
        for block in range(LEN // ABLK):
            low, high = block * ABLK, (block + 1) * ABLK
            query = qkv_ref[low:high, cols]
            near = nt_dot(query, keys[low:high]) * HEAD ** (-0.5)
            near = jnp.where(lower_mask(), near, NEG_FILL)
            row_top = jnp.max(near, axis=-1, keepdims=True)
            if block:
                far = nt_dot(query, keys[:low]) * HEAD ** (-0.5)
                row_top = jnp.maximum(row_top, jnp.max(far, axis=-1, keepdims=True))
            near = jnp.exp(near - row_top)
            row_total = jnp.sum(near, axis=-1, keepdims=True)
            if block:
                far = jnp.exp(far - row_top)
                row_total = row_total + jnp.sum(far, axis=-1, keepdims=True)
            inverse = 1.0 / row_total
            mixed = plain_dot((near * inverse).astype(jnp.bfloat16), values[low:high])
            if block:
                mixed = mixed + plain_dot((far * inverse).astype(jnp.bfloat16), values[:low])
            out_ref[low:high, cols] = mixed.astype(out_ref.dtype)
            log_ref[low:high, head : head + 1] = row_top + jnp.log(row_total)


def attend_forward(mixed_qkv, head_count):
    width = head_count * HEAD
    return pl.pallas_call(
        functools.partial(attend_forward_kernel, head_count),
        out_shape=(
            jax.ShapeDtypeStruct((LEN, width), jnp.bfloat16),
            jax.ShapeDtypeStruct((LEN, 128), jnp.float32),
        ),
        in_specs=[whole_vmem()],
        out_specs=(whole_vmem(), whole_vmem()),
        compiler_params=pltpu.CompilerParams(vmem_limit_bytes=40 * 2**20),
        cost_estimate=pl.CostEstimate(
            flops=4 * head_count * LEN * LEN * HEAD * 4,
            bytes_accessed=LEN * width * 8,
            transcendentals=head_count * LEN * LEN // 2,
        ),
    )(mixed_qkv)


def attend_backward_kernel(
    head_count, qkv_ref, log_ref, grad_ref, out_ref, key_acc, value_acc
):
    width = head_count * HEAD
    scale = HEAD ** (-0.5)
    for head in range(head_count):
        cols = slice(head * HEAD, (head + 1) * HEAD)
        key_cols = slice(width + head * HEAD, width + (head + 1) * HEAD)
        value_cols = slice(2 * width + head * HEAD, 2 * width + (head + 1) * HEAD)
        keys = qkv_ref[:, key_cols]
        values = qkv_ref[:, value_cols]
        for block in range(LEN // ABLK - 1, -1, -1):
            low, high = block * ABLK, (block + 1) * ABLK
            query = qkv_ref[low:high, cols]
            grad = grad_ref[low:high, cols]
            log_sum = log_ref[low:high, head : head + 1]
            near = nt_dot(query, keys[low:high]) * scale
            near = jnp.exp(jnp.where(lower_mask(), near, NEG_FILL) - log_sum)
            near_back = nt_dot(grad, values[low:high])
            inner = jnp.sum(near * near_back, axis=-1, keepdims=True)
            if block:
                far = jnp.exp(nt_dot(query, keys[:low]) * scale - log_sum)
                far_back = nt_dot(grad, values[:low])
                inner = inner + jnp.sum(far * far_back, axis=-1, keepdims=True)
            near_score = (near * (near_back - inner)).astype(jnp.bfloat16)
            grad_query = plain_dot(near_score, keys[low:high])
            near_key = tn_dot(near_score, query)
            near_value = tn_dot(near.astype(jnp.bfloat16), grad)
            if block == LEN // ABLK - 1:
                key_acc[low:high, :] = near_key
                value_acc[low:high, :] = near_value
            else:
                key_acc[low:high, :] += near_key
                value_acc[low:high, :] += near_value
            if block:
                far_score = (far * (far_back - inner)).astype(jnp.bfloat16)
                grad_query = grad_query + plain_dot(far_score, keys[:low])
                far_key = tn_dot(far_score, query)
                far_value = tn_dot(far.astype(jnp.bfloat16), grad)
                if block == LEN // ABLK - 1:
                    key_acc[:low, :] = far_key
                    value_acc[:low, :] = far_value
                else:
                    key_acc[:low, :] += far_key
                    value_acc[:low, :] += far_value
            out_ref[low:high, cols] = (grad_query * scale).astype(jnp.bfloat16)
        out_ref[:, key_cols] = (key_acc[...] * scale).astype(jnp.bfloat16)
        out_ref[:, value_cols] = value_acc[...].astype(jnp.bfloat16)


def attend_backward(mixed_qkv, log_sums, grad_heads, head_count):
    width = head_count * HEAD
    return pl.pallas_call(
        functools.partial(attend_backward_kernel, head_count),
        out_shape=jax.ShapeDtypeStruct((LEN, 3 * width), jnp.bfloat16),
        in_specs=[whole_vmem()] * 3,
        out_specs=whole_vmem(),
        scratch_shapes=[pltpu.VMEM((LEN, HEAD), jnp.float32)] * 2,
        compiler_params=pltpu.CompilerParams(vmem_limit_bytes=40 * 2**20),
        cost_estimate=pl.CostEstimate(
            flops=10 * head_count * LEN * LEN * HEAD * 4,
            bytes_accessed=LEN * width * 16,
            transcendentals=head_count * LEN * LEN // 2,
        ),
    )(mixed_qkv, log_sums, grad_heads)


MESH_ID = pl.DeviceIdType.MESH


def place_of():
    dp_count = lax.axis_size("dp")
    rank = lax.axis_index("dp")
    return dp_count // 2, rank // 2, rank % 2, lax.axis_index("tensor")


def greet(peers):
    barrier = pltpu.get_barrier_semaphore()
    for peer in peers:
        pl.semaphore_signal(barrier, inc=1, device_id=peer, device_id_type=MESH_ID)
    pl.semaphore_wait(barrier, len(peers))


def send_to(src, dst, send_sem, recv_sem, peer):
    return pltpu.make_async_remote_copy(
        src_ref=src,
        dst_ref=dst,
        send_sem=send_sem,
        recv_sem=recv_sem,
        device_id=peer,
        device_id_type=MESH_ID,
    )


def small_peers():
    chips, chip, core, depth = place_of()
    depths = lax.axis_size("tensor")
    flat = [((lax.rem(chip + k, chips)) * 2 + core, depth) for k in range(1, chips)]
    deep = [(chip * 2 + core, lax.rem(depth + k, depths)) for k in range(1, depths)]
    return [(chip * 2 + 1 - core, depth)] + flat + deep


def exchange_small(
    x_ref, out_ref, pair, plane, line, pair_sems, plane_sems, line_sems
):
    chips, chip, core, depth = place_of()
    depths = lax.axis_size("tensor")
    sibling = (chip * 2 + 1 - core, depth)
    flat = [((lax.rem(chip + k, chips)) * 2 + core, depth) for k in range(1, chips)]
    deep = [(chip * 2 + core, lax.rem(depth + k, depths)) for k in range(1, depths)]
    copy = send_to(x_ref, pair, pair_sems.at[0], pair_sems.at[1], sibling)
    copy.start()
    copy.wait()
    plane[chip] = x_ref[...] + pair[...]
    copies = []
    for k in range(1, chips):
        copies.append(
            send_to(
                plane.at[chip], plane.at[chip], plane_sems.at[0, k], plane_sems.at[1, k], flat[k - 1]
            )
        )
    for copy in copies:
        copy.start()
    for copy in copies:
        copy.wait()
    total = plane[0]
    for k in range(1, chips):
        total = total + plane[k]
    line[depth] = total
    copies = []
    for k in range(1, depths):
        copies.append(
            send_to(
                line.at[depth], line.at[depth], line_sems.at[0, k], line_sems.at[1, k], deep[k - 1]
            )
        )
    for copy in copies:
        copy.start()
    for copy in copies:
        copy.wait()
    total = line[0]
    for k in range(1, depths):
        total = total + line[k]
    out_ref[...] = total


def sum_small_kernel(*refs):
    greet(small_peers())
    exchange_small(*refs)


def small_scratch(shape, chips, depths):
    return [
        pltpu.VMEM(shape, jnp.float32),
        pltpu.VMEM((chips,) + shape, jnp.float32),
        pltpu.VMEM((depths,) + shape, jnp.float32),
        pltpu.SemaphoreType.DMA((2,)),
        pltpu.SemaphoreType.DMA((2, chips)),
        pltpu.SemaphoreType.DMA((2, depths)),
    ]


def sum_small(block, collective):
    chips, depths = lax.axis_size("dp") // 2, lax.axis_size("tensor")
    return pl.pallas_call(
        sum_small_kernel,
        out_shape=jax.ShapeDtypeStruct(block.shape, jnp.float32),
        in_specs=[whole_vmem()],
        out_specs=whole_vmem(),
        scratch_shapes=small_scratch(block.shape, chips, depths),
        compiler_params=pltpu.CompilerParams(
            collective_id=collective, has_side_effects=True, vmem_limit_bytes=16 * 2**20
        ),
        cost_estimate=pl.CostEstimate(flops=10**10, bytes_accessed=10**6, transcendentals=0),
    )(block)


def sum_and_spread_kernel(
    x_ref,
    y_ref,
    x_out,
    y_out,
    pair_in,
    pair_sum,
    plane_in,
    total,
    line_in,
    line_out,
    pair_sems,
    plane_sems,
    line_sems,
    spread_sems,
    share_sems,
):
    chips, chip, core, depth = place_of()
    depths = lax.axis_size("tensor")
    rank = chip * 2 + core
    other = 1 - core
    sibling = (chip * 2 + other, depth)
    chip_at = [lax.rem(chip + k, chips) for k in range(chips)]
    flat = [(chip_at[k] * 2 + core, depth) for k in range(chips)]
    deep = [(rank, lax.rem(depth + k, depths)) for k in range(depths)]
    greet([sibling] + flat[1:] + deep[1:])
    part = y_ref.shape[0] // depths
    part_of = [
        pl.ds(pl.multiple_of(lax.rem(depth + k, depths) * part, 8), part) for k in range(depths)
    ]
    halves = [slice(0, y_ref.shape[1] // 2), slice(y_ref.shape[1] // 2, y_ref.shape[1])]
    firsts, seconds = {}, {}
    for c in range(2):
        for k in range(1, depths):
            firsts[c, k] = send_to(
                y_ref.at[part_of[k], halves[c]],
                line_in.at[k, :, halves[c]],
                line_sems.at[c, 0, k],
                line_sems.at[c, 1, k],
                deep[k],
            )
            firsts[c, k].start()
    order = list(range(1, chips)) + [0]
    pair_copies, plane_copies = {}, {}
    for k in order:
        pair_copies[k] = send_to(
            x_ref.at[chip_at[k] * 2 + other],
            pair_in.at[k],
            pair_sems.at[0, k],
            pair_sems.at[1, k],
            sibling,
        )
        pair_copies[k].start()
    for k in order:
        pair_copies[k].wait_recv()
        pair_sum[k] = x_ref[chip_at[k] * 2 + core] + pair_in[k]
        if k:
            plane_copies[k] = send_to(
                pair_sum.at[k], plane_in.at[k], plane_sems.at[0, k], plane_sems.at[1, k], flat[k]
            )
            plane_copies[k].start()
    for c in range(2):
        value = y_ref[part_of[0], halves[c]]
        for k in range(1, depths):
            firsts[c, k].wait_recv()
            value = value + line_in[k, :, halves[c]]
        line_out[part_of[0], halves[c]] = value
        for k in range(1, depths):
            seconds[c, k] = send_to(
                line_out.at[part_of[0], halves[c]],
                line_out.at[part_of[0], halves[c]],
                line_sems.at[c, 2, k],
                line_sems.at[c, 3, k],
                deep[k],
            )
            seconds[c, k].start()
    value = pair_sum[0]
    for k in range(1, chips):
        plane_copies[k].wait_recv()
        value = value + plane_in[k]
    total[...] = value
    square = chips == 4
    row, col = chip // 2, lax.rem(chip, 2)
    if square:
        from_chip = [chip, 2 * row + 1 - col, 2 * (1 - row) + col, 2 * (1 - row) + 1 - col]
        peers = [(c * 2 + core, depth) for c in from_chip]
    else:
        from_chip = [lax.rem(chip + chips - k, chips) for k in range(chips)]
        peers = flat

    def begin(src, dst, sems, cols):
        copies = {}
        for k in (1, 2) if square else range(1, chips):
            copies[k] = send_to(
                src.at[:, cols], dst.at[rank, :, cols], sems.at[0, k], sems.at[1, k], peers[k]
            )
            copies[k].start()
        return copies

    def pass_on(dst, copies, sems, cols, via):
        if square:
            copies[via].wait_recv()
            held = dst.at[from_chip[via] * 2 + core, :, cols]
            copies[3] = send_to(held, held, sems.at[0, 3], sems.at[1, 3], peers[3 - via])
            copies[3].start()

    def share(dst, copies, sems, cols, via):
        shares = {}
        for k in (0, via, 3 - via, 3) if square else range(chips):
            if k and not (square and k == via):
                copies[k].wait_recv()
            held = dst.at[from_chip[k] * 2 + core, :, cols]
            shares[k] = send_to(held, held, sems.at[0, k], sems.at[1, k], sibling)
            shares[k].start()
        return shares

    x_out[rank] = value
    x_spread = [begin(total, x_out, spread_sems.at[2 + c], halves[c]) for c in range(2)]
    y_spread = []
    for c in range(2):
        for k in range(1, depths):
            seconds[c, k].wait_recv()
        y_out[rank, :, halves[c]] = line_out[:, halves[c]]
        y_spread.append(begin(line_out, y_out, spread_sems.at[c], halves[c]))
        if c == 0:
            for i in range(2):
                pass_on(x_out, x_spread[i], spread_sems.at[2 + i], halves[i], 1 + i)
    for c in range(2):
        pass_on(y_out, y_spread[c], spread_sems.at[c], halves[c], 1 + c)
    shares = [
        share(x_out, x_spread[c], share_sems.at[2 + c], halves[c], 1 + c) for c in range(2)
    ] + [share(y_out, y_spread[c], share_sems.at[c], halves[c], 1 + c) for c in range(2)]
    for k in range(chips):
        for copies in shares:
            copies[k].wait_recv()
    for copies in [pair_copies, plane_copies, firsts, seconds] + x_spread + y_spread + shares:
        for copy in copies.values():
            copy.wait_send()


def sum_and_spread(rows, slab_y, collective):
    dp_count, depths = lax.axis_size("dp"), lax.axis_size("tensor")
    chips = dp_count // 2
    count, width = rows.shape
    slab = (count // dp_count, width)
    out_x, out_y = pl.pallas_call(
        sum_and_spread_kernel,
        out_shape=(
            jax.ShapeDtypeStruct((dp_count,) + slab, jnp.float32),
            jax.ShapeDtypeStruct((dp_count,) + slab_y.shape, jnp.float32),
        ),
        in_specs=[whole_vmem()] * 2,
        out_specs=(whole_vmem(), whole_vmem()),
        scratch_shapes=[
            pltpu.VMEM((chips,) + slab, jnp.float32),
            pltpu.VMEM((chips,) + slab, jnp.float32),
            pltpu.VMEM((chips,) + slab, jnp.float32),
            pltpu.VMEM(slab, jnp.float32),
            pltpu.VMEM((depths, slab_y.shape[0] // depths, width), jnp.float32),
            pltpu.VMEM(slab_y.shape, jnp.float32),
            pltpu.SemaphoreType.DMA((2, chips)),
            pltpu.SemaphoreType.DMA((2, chips)),
            pltpu.SemaphoreType.DMA((2, 4, depths)),
            pltpu.SemaphoreType.DMA((4, 2, chips)),
            pltpu.SemaphoreType.DMA((4, 2, chips)),
        ],
        compiler_params=pltpu.CompilerParams(
            collective_id=collective, has_side_effects=True, vmem_limit_bytes=32 * 2**20
        ),
        cost_estimate=pl.CostEstimate(
            flops=60 * 10**9, bytes_accessed=count * width * 16, transcendentals=0
        ),
    )(rows.reshape((dp_count,) + slab), slab_y)
    return out_x.reshape(count, width), out_y.reshape(-1, width)


def scatter_rows_kernel(
    x_ref, out_ref, pair_in, pair_sum, plane_in, pair_sems, plane_sems
):
    chips, chip, core, depth = place_of()
    other = 1 - core
    sibling = (chip * 2 + other, depth)
    chip_at = [lax.rem(chip + k, chips) for k in range(chips)]
    flat = [(chip_at[k] * 2 + core, depth) for k in range(chips)]
    greet([sibling] + flat[1:])
    order = list(range(1, chips)) + [0]
    pair_copies, plane_copies = {}, {}
    for k in order:
        pair_copies[k] = send_to(
            x_ref.at[chip_at[k] * 2 + other],
            pair_in.at[k],
            pair_sems.at[0, k],
            pair_sems.at[1, k],
            sibling,
        )
        pair_copies[k].start()
    for k in order:
        pair_copies[k].wait_recv()
        pair_sum[k] = x_ref[chip_at[k] * 2 + core] + pair_in[k]
        if k:
            plane_copies[k] = send_to(
                pair_sum.at[k], plane_in.at[k], plane_sems.at[0, k], plane_sems.at[1, k], flat[k]
            )
            plane_copies[k].start()
    value = pair_sum[0]
    for k in range(1, chips):
        plane_copies[k].wait_recv()
        value = value + plane_in[k]
    out_ref[...] = value
    for copies in (pair_copies, plane_copies):
        for copy in copies.values():
            copy.wait_send()


def pad_rows(rows, unit):
    have, width = rows.shape
    padded = -(-have // unit) * unit
    if padded == have:
        return rows
    return jnp.concatenate([rows, jnp.zeros((padded - have, width), rows.dtype)], axis=0)


def scatter_rows(rows, collective):
    dp_count = lax.axis_size("dp")
    chips = dp_count // 2
    slab = (rows.shape[0] // dp_count, rows.shape[1])
    return pl.pallas_call(
        scatter_rows_kernel,
        out_shape=jax.ShapeDtypeStruct(slab, jnp.float32),
        in_specs=[whole_vmem()],
        out_specs=whole_vmem(),
        scratch_shapes=[
            pltpu.VMEM((chips,) + slab, jnp.float32),
            pltpu.VMEM((chips,) + slab, jnp.float32),
            pltpu.VMEM((chips,) + slab, jnp.float32),
            pltpu.SemaphoreType.DMA((2, chips)),
            pltpu.SemaphoreType.DMA((2, chips)),
        ],
        compiler_params=pltpu.CompilerParams(
            collective_id=collective, has_side_effects=True, vmem_limit_bytes=32 * 2**20
        ),
        cost_estimate=pl.CostEstimate(
            flops=rows.shape[0] * 15 * 10**6,
            bytes_accessed=rows.shape[0] * rows.shape[1] * 4,
            transcendentals=0,
        ),
    )(rows.reshape((dp_count,) + slab))


def start_spread(src, out_ref, sems, flat, rank, cols=slice(None)):
    copies = {}
    for k in range(1, len(flat)):
        copies[k] = send_to(
            src.at[:, cols], out_ref.at[rank, :, cols], sems.at[0, k], sems.at[1, k], flat[k]
        )
        copies[k].start()
    return copies


def start_share(out_ref, spread_copies, sems, place, sibling, cols=slice(None)):
    chips, chip, core = place
    copies = {}
    for k in range(chips):
        if k:
            spread_copies[k].wait_recv()
        held = lax.rem(chip + chips - k, chips) * 2 + core
        copies[k] = send_to(
            out_ref.at[held, :, cols],
            out_ref.at[held, :, cols],
            sems.at[0, k],
            sems.at[1, k],
            sibling,
        )
        copies[k].start()
    return copies


def spread_kernel(x_ref, out_ref, spread_sems, share_sems):
    chips, chip, core, depth = place_of()
    rank = chip * 2 + core
    sibling = (chip * 2 + 1 - core, depth)
    flat = [(lax.rem(chip + k, chips) * 2 + core, depth) for k in range(chips)]
    greet([sibling] + flat[1:])
    spread_copies = start_spread(x_ref, out_ref, spread_sems, flat, rank)
    out_ref[rank] = x_ref[...]
    share_copies = start_share(out_ref, spread_copies, share_sems, (chips, chip, core), sibling)
    for k in range(chips):
        share_copies[k].wait_recv()
    for copies in (spread_copies, share_copies):
        for copy in copies.values():
            copy.wait_send()


def spread(slab, collective):
    dp_count = lax.axis_size("dp")
    chips = dp_count // 2
    each, width = slab.shape
    full = pl.pallas_call(
        spread_kernel,
        out_shape=jax.ShapeDtypeStruct((dp_count, each, width), slab.dtype),
        in_specs=[whole_vmem()],
        out_specs=whole_vmem(),
        scratch_shapes=[
            pltpu.SemaphoreType.DMA((2, chips)),
            pltpu.SemaphoreType.DMA((2, chips)),
        ],
        compiler_params=pltpu.CompilerParams(
            collective_id=collective, has_side_effects=True, vmem_limit_bytes=16 * 2**20
        ),
        cost_estimate=pl.CostEstimate(
            flops=35 * 10**9, bytes_accessed=dp_count * each * width * 4, transcendentals=0
        ),
    )(slab)
    return full.reshape(dp_count * each, width)


def line_steps(x_ref, out_ref, right_send, right_recv, left_send, left_recv):
    rank = lax.axis_index("dp")
    depth = lax.axis_index("tensor")
    last = lax.axis_size("tensor") - 1
    right, left = (rank, depth + 1), (rank, depth - 1)

    def to_right(step):
        src = x_ref if step == 0 else out_ref.at[depth - step]
        return send_to(
            src, out_ref.at[depth - step], right_send.at[step], right_recv.at[step], right
        )

    def to_left(step):
        src = x_ref if step == 0 else out_ref.at[depth + step]
        return send_to(src, out_ref.at[depth + step], left_send.at[step], left_recv.at[step], left)

    def send(step):
        @pl.when((depth < last) & (depth >= step))
        def _():
            to_right(step).start()

        @pl.when((depth > 0) & (depth + step <= last))
        def _():
            to_left(step).start()

        if step == 0:
            out_ref[depth] = x_ref[...]

    def receive(step):
        @pl.when(depth - 1 >= step)
        def _():
            send_to(
                x_ref,
                out_ref.at[depth - 1 - step],
                right_send.at[step],
                right_recv.at[step],
                left,
            ).wait_recv()

        @pl.when(depth + 1 + step <= last)
        def _():
            send_to(
                x_ref, out_ref.at[depth + 1 + step], left_send.at[step], left_recv.at[step], right
            ).wait_recv()

    def finish():
        for step in range(last):

            @pl.when((depth < last) & (depth >= step))
            def _():
                to_right(step).wait_send()

            @pl.when((depth > 0) & (depth + step <= last))
            def _():
                to_left(step).wait_send()

    return send, receive, finish


def line_gather_kernel(x_ref, out_ref, *sems):
    last = lax.axis_size("tensor") - 1
    greet_line(lax.axis_index("tensor"), last, lax.axis_index("dp"))
    send, receive, finish = line_steps(x_ref, out_ref, *sems)
    for step in range(last):
        send(step)
        receive(step)
    finish()


def first_gather_kernel(
    head_count,
    x_ref,
    y_ref,
    t_ref,
    weight_ref,
    rows_ref,
    small_ref,
    tall_ref,
    qkv_ref,
    heads_ref,
    log_ref,
    pair,
    plane,
    line,
    pair_sems,
    plane_sems,
    line_sems,
    *sems,
):
    last = lax.axis_size("tensor") - 1
    greet(small_peers())
    send, receive, finish = line_steps(x_ref, rows_ref, *sems[:4])
    send_tall, receive_tall, finish_tall = line_steps(t_ref, tall_ref, *sems[4:])
    count = x_ref.shape[0]
    for step in range(last):
        send(step)
        if step == 0:
            exchange_small(y_ref, small_ref, pair, plane, line, pair_sems, plane_sems, line_sems)
        if step == 1:
            send_tall(0)
        receive(step)
    receive_tall(0)
    send_tall(1)
    for j in range(last + 1):
        qkv_ref[j * count : (j + 1) * count, :] = plain_dot(
            rows_ref[j], weight_ref[...]
        ).astype(jnp.bfloat16)
    attend_forward_kernel(head_count, qkv_ref, heads_ref, log_ref)
    for step in range(1, last):
        receive_tall(step)
        if step + 1 < last:
            send_tall(step + 1)
    finish()
    finish_tall()


def first_gather(block, small, tall, weight, head_count, collective):
    chips, depths = lax.axis_size("dp") // 2, lax.axis_size("tensor")
    rows, width = block.shape
    outs = pl.pallas_call(
        functools.partial(first_gather_kernel, head_count),
        out_shape=(
            jax.ShapeDtypeStruct((depths, rows, width), block.dtype),
            jax.ShapeDtypeStruct(small.shape, jnp.float32),
            jax.ShapeDtypeStruct((depths,) + tall.shape, tall.dtype),
            jax.ShapeDtypeStruct((LEN, weight.shape[1]), jnp.bfloat16),
            jax.ShapeDtypeStruct((LEN, head_count * HEAD), jnp.bfloat16),
            jax.ShapeDtypeStruct((LEN, 128), jnp.float32),
        ),
        in_specs=[whole_vmem()] * 4,
        out_specs=tuple(whole_vmem() for _ in range(6)),
        scratch_shapes=small_scratch(small.shape, chips, depths)
        + [pltpu.SemaphoreType.DMA((depths,))] * 8,
        compiler_params=pltpu.CompilerParams(
            collective_id=collective, has_side_effects=True, vmem_limit_bytes=40 * 2**20
        ),
        cost_estimate=pl.CostEstimate(
            flops=80 * 10**9, bytes_accessed=depths * tall.size * 4, transcendentals=0
        ),
    )(block, small, tall, weight)
    return (
        outs[0].reshape(depths * rows, width),
        outs[1],
        outs[2].reshape(depths * rows, tall.shape[1]),
    ) + tuple(outs[3:])


def line_gather(block, collective):
    depths = lax.axis_size("tensor")
    rows, width = block.shape
    out = pl.pallas_call(
        line_gather_kernel,
        out_shape=jax.ShapeDtypeStruct((depths, rows, width), block.dtype),
        in_specs=[whole_vmem()],
        out_specs=whole_vmem(),
        scratch_shapes=[pltpu.SemaphoreType.DMA((depths,))] * 4,
        compiler_params=pltpu.CompilerParams(
            collective_id=collective, has_side_effects=True, vmem_limit_bytes=16 * 2**20
        ),
        cost_estimate=pl.CostEstimate(
            flops=25 * 10**9, bytes_accessed=depths * rows * width * 4, transcendentals=0
        ),
    )(block)
    return out.reshape(depths * rows, width)


def renew_kernel(widths, flips, gains, group_ref, map_ref, *refs):
    olds, news = refs[: len(widths)], refs[len(widths) :]
    keep_rate = 1.0 - MUON_RATE * MUON_DECAY
    offset = 0
    total = group_ref.shape[1]
    for width, flip, gain, old, new in zip(widths, flips, gains, olds, news):
        iterate_ref = group_ref
        if offset == total:
            iterate_ref, offset = map_ref, 0
        if flip:
            for first in range(0, width, 128):
                size = min(128, width - first)
                piece = iterate_ref[:, offset + first : offset + first + size]
                rows = slice(first, first + size)
                new[rows, :] = keep_rate * old[rows, :] - MUON_RATE * gain * (
                    piece.astype(jnp.float32).T
                )
        else:
            for first in range(0, old.shape[0], 128):
                rows = slice(first, first + 128)
                piece = iterate_ref[rows, offset : offset + width]
                new[rows, :] = keep_rate * old[rows, :] - MUON_RATE * gain * (
                    piece.astype(jnp.float32)
                )
        offset += width


def renew(iterate, map_iterate, olds, widths, flips, gains):
    return pl.pallas_call(
        functools.partial(renew_kernel, widths, flips, gains),
        out_shape=tuple(jax.ShapeDtypeStruct(old.shape, jnp.float32) for old in olds),
        in_specs=[whole_vmem()] * (2 + len(olds)),
        out_specs=tuple(whole_vmem() for _ in olds),
        compiler_params=pltpu.CompilerParams(vmem_limit_bytes=48 * 2**20),
        cost_estimate=pl.CostEstimate(
            flops=10**9, bytes_accessed=iterate.size * 10, transcendentals=0
        ),
    )(iterate, map_iterate, *olds)


HALF = 128
QUARTER = 64


def greet_line(depth, last, rank):
    barrier = pltpu.get_barrier_semaphore()

    @pl.when(depth < last)
    def _():
        pl.semaphore_signal(
            barrier, inc=1, device_id=(rank, depth + 1), device_id_type=MESH_ID
        )

    @pl.when(depth > 0)
    def _():
        pl.semaphore_signal(
            barrier, inc=1, device_id=(rank, depth - 1), device_id_type=MESH_ID
        )

    @pl.when((depth > 0) & (depth < last))
    def _():
        pl.semaphore_wait(barrier, 2)

    @pl.when((depth == 0) | (depth == last))
    def _():
        pl.semaphore_wait(barrier, 1)


def line_mlp_kernel(
    x_ref,
    first_ref,
    second_ref,
    out_ref,
    rows,
    parts,
    from_left,
    from_right,
    stage,
    right_sems,
    left_sems,
    row_sems,
    sum_sems,
    from_left_sems,
    from_right_sems,
):
    rank = lax.axis_index("dp")
    depth = lax.axis_index("tensor")
    last = lax.axis_size("tensor") - 1
    right, left = (rank, depth + 1), (rank, depth - 1)
    greet_line(depth, last, rank)

    def rows_right(j, h):
        return send_to(rows.at[j, h], rows.at[j, h], right_sems.at[j, h], row_sems.at[j, h], right)

    def rows_left(j, h):
        return send_to(rows.at[j, h], rows.at[j, h], left_sems.at[j, h], row_sems.at[j, h], left)

    def sum_right(j, h):
        return send_to(
            stage.at[j, h], from_left.at[j, h], sum_sems.at[j, h], from_left_sems.at[j, h], right
        )

    def sum_left(j, h):
        return send_to(
            stage.at[j, h], from_right.at[j, h], sum_sems.at[j, h], from_right_sems.at[j, h], left
        )

    for q in range(4):
        rows[depth, q] = x_ref[q * QUARTER : (q + 1) * QUARTER, :]

        @pl.when(depth < last)
        def _():
            rows_right(depth, q).start()

        @pl.when(depth > 0)
        def _():
            rows_left(depth, q).start()

    inner = depth * (last - depth) // 2
    side = depth // 2
    for step, shift in enumerate((1, 1, -2, 0)):
        base = step + inner * shift
        j = base + side * (last - 2 * base)

        def half_step(h, carry):
            for q in (2 * h, 2 * h + 1):
                if step:

                    @pl.when(j < depth)
                    def _():
                        rows_right(j, q).wait_recv()

                    @pl.when(j > depth)
                    def _():
                        rows_left(j, q).wait_recv()

                    @pl.when((j < depth) & (depth < last))
                    def _():
                        rows_right(j, q).start()

                    @pl.when((j > depth) & (depth > 0))
                    def _():
                        rows_left(j, q).start()

            block = jnp.concatenate([rows[j, 2 * h], rows[j, 2 * h + 1]], axis=0)
            hidden = smooth_gelu(plain_dot(block, first_ref[...])).astype(jnp.bfloat16)
            part = plain_dot(hidden, second_ref[...])
            for i in range(2):
                q = 2 * h + i
                piece = part[i * QUARTER : (i + 1) * QUARTER, :]
                parts[j, q] = piece
                if step:

                    @pl.when((depth == 0) | (depth == last))
                    def _():
                        stage[j, q] = piece.astype(jnp.bfloat16)

                    @pl.when(depth == 0)
                    def _():
                        sum_right(j, q).start()

                    @pl.when(depth == last)
                    def _():
                        sum_left(j, q).start()

            return carry

        lax.fori_loop(0, 2, half_step, 0)

    def relay_right(j):
        for h in range(4):
            sum_right(j, h).wait_recv()
            stage[j, h] = (parts[j, h] + from_left[j, h].astype(jnp.float32)).astype(jnp.bfloat16)
            sum_right(j, h).start()

    def relay_left(j):
        for h in range(4):
            sum_left(j, h).wait_recv()
            stage[j, h] = (parts[j, h] + from_right[j, h].astype(jnp.float32)).astype(jnp.bfloat16)
            sum_left(j, h).start()

    @pl.when(depth == 1)
    def _():
        relay_right(2)
        relay_right(3)
        relay_left(0)

    @pl.when(depth == 2)
    def _():
        relay_left(1)
        relay_left(0)
        relay_right(3)

    for h in range(4):
        span = slice(h * QUARTER, (h + 1) * QUARTER)
        out_ref[span, :] = parts[depth, h]

        @pl.when(depth > 0)
        def _():
            sum_right(depth, h).wait_recv()
            out_ref[span, :] += from_left[depth, h].astype(jnp.float32)

        @pl.when(depth < last)
        def _():
            sum_left(depth, h).wait_recv()
            out_ref[span, :] += from_right[depth, h].astype(jnp.float32)

    for j in range(4):
        for h in range(4):

            @pl.when((depth >= j) & (depth < last))
            def _():
                rows_right(j, h).wait_send()

            @pl.when((depth <= j) & (depth > 0))
            def _():
                rows_left(j, h).wait_send()

            @pl.when(depth < j)
            def _():
                sum_right(j, h).wait_send()

            @pl.when(depth > j)
            def _():
                sum_left(j, h).wait_send()


def line_mlp(block, first, second, collective):
    count, width = block.shape
    slots = (4, 4, QUARTER, width)
    return pl.pallas_call(
        line_mlp_kernel,
        out_shape=jax.ShapeDtypeStruct((count, width), jnp.float32),
        in_specs=[whole_vmem()] * 3,
        out_specs=whole_vmem(),
        scratch_shapes=[
            pltpu.VMEM(slots, jnp.bfloat16),
            pltpu.VMEM(slots, jnp.float32),
            pltpu.VMEM(slots, jnp.bfloat16),
            pltpu.VMEM(slots, jnp.bfloat16),
            pltpu.VMEM(slots, jnp.bfloat16),
        ]
        + [pltpu.SemaphoreType.DMA((4, 4))] * 6,
        compiler_params=pltpu.CompilerParams(
            collective_id=collective, has_side_effects=True, vmem_limit_bytes=48 * 2**20
        ),
        cost_estimate=pl.CostEstimate(
            flops=16 * count * width * first.shape[1] * 4,
            bytes_accessed=16 * count * width,
            transcendentals=4 * count * first.shape[1],
        ),
    )(block, first, second)


def share_gram_kernel(
    parts_ref, extra_ref, out_ref, line_in, pair_in, line_sems, pair_sems, plane_sems
):
    chips, chip, core, depth = place_of()
    depths = lax.axis_size("tensor")
    rank = chip * 2 + core
    sibling = (chip * 2 + 1 - core, depth)
    flat = [(lax.rem(chip + k, chips) * 2 + core, depth) for k in range(chips)]
    line = [lax.rem(depth + k, depths) for k in range(depths)]
    deep = [(rank, line[k]) for k in range(depths)]
    greet([sibling] + flat[1:] + deep[1:])
    copies = {}
    for k in range(1, depths):
        copies[k] = send_to(
            parts_ref.at[line[k]], line_in.at[k], line_sems.at[0, k], line_sems.at[1, k], deep[k]
        )
        copies[k].start()
    extra = send_to(extra_ref, out_ref.at[rank], pair_sems.at[0], pair_sems.at[1], sibling)
    main = send_to(pair_in, out_ref.at[rank], pair_sems.at[2], pair_sems.at[3], sibling)
    plane = {}
    for k in range(1, chips):
        plane[k] = [
            send_to(
                out_ref.at[chip * 2 + i],
                out_ref.at[chip * 2 + i],
                plane_sems.at[0, i, k],
                plane_sems.at[1, i, k],
                flat[k],
            )
            for i in range(2)
        ]

    @pl.when(core == 0)
    def _():
        extra.start()

    @pl.when(core == 1)
    def _():
        out_ref[rank] = extra_ref[...]
        extra.wait_recv()
        for k in range(1, chips):
            for i in range(2):
                plane[k][i].start()

    value = parts_ref[depth]
    for k in range(1, depths):
        copies[k].wait_recv()
        value = value + line_in[k]

    @pl.when(core == 1)
    def _():
        pair_in[...] = value
        main.start()

    @pl.when(core == 0)
    def _():
        out_ref[rank] = value
        main.wait_recv()
        for k in range(1, chips):
            for i in range(2):
                plane[k][i].start()

    for k in range(1, chips):
        for i in range(2):
            plane[k][i].wait_recv()
    for k in range(1, chips):
        for i in range(2):
            plane[k][i].wait_send()
    for k in range(1, depths):
        copies[k].wait_send()

    @pl.when(core == 0)
    def _():
        extra.wait_send()

    @pl.when(core == 1)
    def _():
        main.wait_send()


def share_gram(parts, extra, collective):
    dp_count, depths = lax.axis_size("dp"), lax.axis_size("tensor")
    chips = dp_count // 2
    slab = extra.shape
    out = pl.pallas_call(
        share_gram_kernel,
        out_shape=jax.ShapeDtypeStruct((dp_count,) + slab, jnp.float32),
        in_specs=[whole_vmem()] * 2,
        out_specs=whole_vmem(),
        scratch_shapes=[
            pltpu.VMEM((depths,) + slab, jnp.float32),
            pltpu.VMEM(slab, jnp.float32),
            pltpu.SemaphoreType.DMA((2, depths)),
            pltpu.SemaphoreType.DMA((4,)),
            pltpu.SemaphoreType.DMA((2, 2, chips)),
        ],
        compiler_params=pltpu.CompilerParams(
            collective_id=collective, has_side_effects=True, vmem_limit_bytes=16 * 2**20
        ),
        cost_estimate=pl.CostEstimate(
            flops=45 * 10**9, bytes_accessed=dp_count * slab[0] * slab[1] * 8, transcendentals=0
        ),
    )(parts.reshape((depths,) + slab), extra)
    return out.reshape(dp_count * slab[0], slab[1])


def line_exchange_kernel(
    heads_ref,
    weight_ref,
    x_ref,
    sum_ref,
    all_ref,
    y_ref,
    from_left,
    from_right,
    stage,
    right_sems,
    left_sems,
    row_sems,
    sum_sems,
    from_left_sems,
    from_right_sems,
):
    rank = lax.axis_index("dp")
    depth = lax.axis_index("tensor")
    last = lax.axis_size("tensor") - 1
    right, left = (rank, depth + 1), (rank, depth - 1)
    greet_line(depth, last, rank)

    def rows_right(j):
        return send_to(all_ref.at[j], all_ref.at[j], right_sems.at[j], row_sems.at[j], right)

    def rows_left(j):
        return send_to(all_ref.at[j], all_ref.at[j], left_sems.at[j], row_sems.at[j], left)

    def sum_right(j, h, src):
        return send_to(
            src.at[j, h], from_left.at[j, h], sum_sems.at[j, h], from_left_sems.at[j, h], right
        )

    def sum_left(j, h, src):
        return send_to(
            src.at[j, h], from_right.at[j, h], sum_sems.at[j, h], from_right_sems.at[j, h], left
        )

    all_ref[depth] = x_ref[...]

    @pl.when(depth < last)
    def _():
        rows_right(depth).start()

    @pl.when(depth > 0)
    def _():
        rows_left(depth).start()

    for j in range(4):
        for h in range(2):
            first = (2 * j + h) * HALF
            y_ref[j, h] = plain_dot(
                heads_ref[first : first + HALF, :], weight_ref[...]
            ).astype(jnp.bfloat16)

    @pl.when(depth == 0)
    def _():
        for j in (3, 2, 1):
            for h in range(2):
                sum_right(j, h, y_ref).start()
        for j in (1, 2, 3):
            rows_left(j).wait_recv()

    @pl.when(depth == last)
    def _():
        for j in (0, 1, 2):
            for h in range(2):
                sum_left(j, h, y_ref).start()
        for j in (2, 1, 0):
            rows_right(j).wait_recv()

    def relay_right(j):
        for h in range(2):
            sum_right(j, h, stage).wait_recv()
            stage[j, h] = (
                y_ref[j, h].astype(jnp.float32) + from_left[j, h].astype(jnp.float32)
            ).astype(jnp.bfloat16)
            sum_right(j, h, stage).start()

    def relay_left(j):
        for h in range(2):
            sum_left(j, h, stage).wait_recv()
            stage[j, h] = (
                y_ref[j, h].astype(jnp.float32) + from_right[j, h].astype(jnp.float32)
            ).astype(jnp.bfloat16)
            sum_left(j, h, stage).start()

    def pass_right(j):
        rows_right(j).wait_recv()
        rows_right(j).start()

    def pass_left(j):
        rows_left(j).wait_recv()
        rows_left(j).start()

    @pl.when(depth == 1)
    def _():
        pass_left(2)
        pass_right(0)
        relay_right(3)
        pass_left(3)
        relay_left(0)
        relay_right(2)

    @pl.when(depth == 2)
    def _():
        pass_right(1)
        pass_left(3)
        relay_left(0)
        pass_right(0)
        relay_right(3)
        relay_left(1)

    for h in range(2):
        span = slice(h * HALF, (h + 1) * HALF)
        sum_ref[span, :] = y_ref[depth, h].astype(jnp.float32)

        @pl.when(depth > 0)
        def _():
            sum_right(depth, h, stage).wait_recv()
            sum_ref[span, :] += from_left[depth, h].astype(jnp.float32)

        @pl.when(depth < last)
        def _():
            sum_left(depth, h, stage).wait_recv()
            sum_ref[span, :] += from_right[depth, h].astype(jnp.float32)

    for j in range(4):

        @pl.when((depth >= j) & (depth < last))
        def _():
            rows_right(j).wait_send()

        @pl.when((depth <= j) & (depth > 0))
        def _():
            rows_left(j).wait_send()

        for h in range(2):

            @pl.when(depth < j)
            def _():
                sum_right(j, h, stage).wait_send()

            @pl.when(depth > j)
            def _():
                sum_left(j, h, stage).wait_send()


def line_exchange(heads, weight, block, collective):
    width = weight.shape[1]
    slots = (4, 2, HALF, width)
    total, rows = pl.pallas_call(
        line_exchange_kernel,
        out_shape=(
            jax.ShapeDtypeStruct((2 * HALF, width), jnp.float32),
            jax.ShapeDtypeStruct((4,) + block.shape, block.dtype),
        ),
        in_specs=[whole_vmem()] * 3,
        out_specs=(whole_vmem(), whole_vmem()),
        scratch_shapes=[pltpu.VMEM(slots, jnp.bfloat16)] * 4
        + [pltpu.SemaphoreType.DMA((4,))] * 3
        + [pltpu.SemaphoreType.DMA((4, 2))] * 3,
        compiler_params=pltpu.CompilerParams(
            collective_id=collective, has_side_effects=True, vmem_limit_bytes=32 * 2**20
        ),
        cost_estimate=pl.CostEstimate(
            flops=60 * 10**9, bytes_accessed=heads.size * 16, transcendentals=0
        ),
    )(heads, weight, block)
    return total, rows.reshape(-1, block.shape[1])


NBLK = 256


def split_store(value, high_ref, low_ref, rows, cols):
    high = value.astype(jnp.bfloat16)
    high_ref[rows, cols] = high
    low_ref[rows, cols] = (value - high.astype(jnp.float32)).astype(jnp.bfloat16)


def polynomial_kernel(gram_ref, out_ref, full_g, full_h, full_m, *pairs):
    gram_pair, half_pair, poly_pair, prod_pair = (
        pairs[0:2], pairs[2:4], pairs[4:6], pairs[6:8]
    )
    size = gram_ref.shape[0]
    blocks = size // NBLK
    spans = [slice(i * NBLK, (i + 1) * NBLK) for i in range(blocks)]
    upper = [(i, j) for i in range(blocks) for j in range(i, blocks)]

    def eye(i, j):
        if i != j:
            return 0.0
        row = lax.broadcasted_iota(jnp.int32, (NBLK, NBLK), 0)
        col = lax.broadcasted_iota(jnp.int32, (NBLK, NBLK), 1)
        return jnp.where(row == col, 1.0, 0.0)

    def place(i, j, value, full, pair):
        if full is not None:
            full[spans[i], spans[j]] = value
        if pair is not None:
            split_store(value, *pair, spans[i], spans[j])
        if i != j:
            flip = value.T
            if full is not None:
                full[spans[j], spans[i]] = flip
            if pair is not None:
                split_store(flip, *pair, spans[j], spans[i])

    def product(left, right, i, j):
        return plain_dot(left[0][spans[i], :], right[0][:, spans[j]]) + (
            plain_dot(left[0][spans[i], :], right[1][:, spans[j]])
            + plain_dot(left[1][spans[i], :], right[0][:, spans[j]])
        )

    trace = 0.0
    for i in range(blocks):
        trace = trace + jnp.sum(gram_ref[spans[i], spans[i]] * eye(i, i))
    root = jnp.sqrt(jnp.full((1, 1), trace, jnp.float32)) + 1e-07
    inverse = 1.0 / root
    for i, j in upper:
        place(i, j, gram_ref[spans[i], spans[j]] * (inverse * inverse), full_g, gram_pair)

    def make_poly():
        for i, j in upper:
            value = NS_B * full_g[spans[i], spans[j]] + NS_C * product(gram_pair, gram_pair, i, j)
            place(i, j, value, None, poly_pair)

    def advance():
        for i, j in upper:
            value = NS_A * full_g[spans[i], spans[j]] + product(poly_pair, gram_pair, i, j)
            place(i, j, value, full_h, half_pair)
        for i, j in upper:
            value = NS_A * full_h[spans[i], spans[j]] + product(poly_pair, half_pair, i, j)
            place(i, j, value, full_g, gram_pair)

    make_poly()
    for i, j in upper:
        value = (
            poly_pair[0][spans[i], spans[j]].astype(jnp.float32)
            + poly_pair[1][spans[i], spans[j]].astype(jnp.float32)
            + NS_A * eye(i, j)
        )
        place(i, j, value, full_m, prod_pair)
    advance()

    def sweep(index, carry):
        make_poly()
        for i, j in upper:
            value = NS_A * full_m[spans[i], spans[j]] + product(poly_pair, prod_pair, i, j)
            place(i, j, value, full_h, None)
        for i in range(blocks):
            full_m[spans[i], :] = full_h[spans[i], :]
            split_store(full_h[spans[i], :], *prod_pair, spans[i], slice(None))
        advance()
        return carry

    lax.fori_loop(0, 3, sweep, 0)
    make_poly()
    for i, j in upper:
        value = NS_A * full_m[spans[i], spans[j]] + product(poly_pair, prod_pair, i, j)
        place(i, j, value * inverse, out_ref, None)


def orthogonal_factor(gram_mat):
    size = gram_mat.shape[0]
    return pl.pallas_call(
        polynomial_kernel,
        out_shape=jax.ShapeDtypeStruct((size, size), jnp.float32),
        in_specs=[whole_vmem()],
        out_specs=whole_vmem(),
        scratch_shapes=[pltpu.VMEM((size, size), jnp.float32)] * 3
        + [pltpu.VMEM((size, size), jnp.bfloat16)] * 8,
        compiler_params=pltpu.CompilerParams(vmem_limit_bytes=48 * 2**20),
        cost_estimate=pl.CostEstimate(
            flops=17 * 2 * 2 * size**3, bytes_accessed=8 * size * size, transcendentals=0
        ),
    )(gram_mat)


def contract_rows(left, right):
    return lax.dot_general(
        left, right, (((0,), (0,)), ((), ())), preferred_element_type=jnp.float32
    )


def contract_cols(left, right):
    return lax.dot_general(
        left, right, (((1,), (1,)), ((), ())), preferred_element_type=jnp.float32
    )


def body(
    teacher_in,
    student_in,
    resp_mask,
    replay,
    t_gains,
    t_shifts,
    t_qkv,
    t_out,
    t_fc,
    t_proj,
    s_norms,
    s_qkv,
    s_out,
    s_fc,
    s_proj,
    s_map,
    mom_qkv,
    mom_out,
    mom_fc,
    mom_proj,
    mom_map,
    adam_first,
    adam_second,
):
    groups = lax.axis_size("tensor")
    tensor_rank = lax.axis_index("tensor")
    row_count = student_in.shape[0]
    seq_count = replay.shape[0]
    total_rows = row_count * groups
    count_block = jnp.full((8, 128), jnp.sum(resp_mask), jnp.int32).astype(jnp.float32)
    tokens_all = lax.axis_size("dp") * seq_count * LEN

    def student_gather(local_rows):
        return lax.all_gather(local_rows, "tensor", axis=0, tiled=True)

    def student_reduce(left, right, right_dim):
        return lax.psum_scatter(
            lax.dot_general(
                left, right, (((1,), (right_dim,)), ((), ())), preferred_element_type=jnp.float32
            ).astype(jnp.bfloat16),
            "tensor",
            scatter_dimension=0,
            tiled=True,
        ).astype(jnp.float32)

    teacher_x = teacher_in.astype(jnp.float32)
    slot_width = t_qkv.shape[2]
    slot_count = slot_width // HEAD
    live_count = HT // groups + (tensor_rank < HT % groups).astype(jnp.int32)
    live_slots = (jnp.arange(slot_count, dtype=jnp.int32) < live_count).astype(jnp.float32)
    teacher_normed = norm_parts(teacher_x, t_gains[0], t_shifts[0])[0].astype(jnp.bfloat16)
    student_x = student_in.astype(jnp.float32)
    shard_width = s_qkv.shape[2]
    shard_hidden = s_fc.shape[1]
    head_count = shard_width // HEAD
    w_qkv = s_qkv.astype(jnp.bfloat16).reshape(DS, 3 * shard_width)
    w_out = s_out.astype(jnp.bfloat16)
    w_fc = s_fc.astype(jnp.bfloat16)
    w_proj = s_proj.astype(jnp.bfloat16)
    w_map = s_map.astype(jnp.bfloat16)
    normed_one, unit_one, scale_one = norm_parts(student_x, s_norms[0], s_norms[1])
    low_one = normed_one.astype(jnp.bfloat16)
    rows_one, count_sum, teacher_all, mixed_qkv, head_out, log_sums = first_gather(
        low_one, count_block, teacher_normed, w_qkv, head_count, 5
    )
    count_val = count_sum[0, 0]
    factor = tokens_all / (2.0 * count_val)
    resid = student_x + student_reduce(head_out, w_out, 0)
    teacher_mixed = jnp.dot(
        teacher_all, t_qkv.reshape(DT, 3 * slot_width), preferred_element_type=jnp.float32
    ).astype(jnp.bfloat16)
    teacher_head_out = attend_forward(teacher_mixed, slot_count)[0]
    slot_mask = jnp.repeat(live_slots, HEAD)[None, :] > 0.0
    teacher_head_out = jnp.where(slot_mask, teacher_head_out, jnp.zeros_like(teacher_head_out))
    normed_two, unit_two, scale_two = norm_parts(resid, s_norms[2], s_norms[3])
    low_two = normed_two.astype(jnp.bfloat16)
    attn_part, rows_two = line_exchange(teacher_head_out, t_out, low_two, 6)
    teacher_resid = teacher_x + attn_part
    teacher_normed_two = norm_parts(teacher_resid, t_gains[1], t_shifts[1])[0].astype(jnp.bfloat16)
    mlp_part = line_mlp(teacher_normed_two, t_fc, t_proj, 8)
    teacher_out = (teacher_resid + mlp_part).astype(jnp.bfloat16)
    before = jnp.dot(rows_two, w_fc, preferred_element_type=jnp.float32)
    before, hidden = (before, smooth_gelu(before).astype(jnp.bfloat16))
    output = resid + student_reduce(hidden, w_proj, 0)
    student_out = output.astype(jnp.bfloat16)
    guess_vec = jnp.dot(student_out, w_map, preferred_element_type=jnp.float32)
    miss_vec = guess_vec - teacher_out.astype(jnp.float32)
    position = tensor_rank * row_count + jnp.arange(row_count, dtype=jnp.int32)
    seq_owner = position // LEN
    seq_pick = (seq_owner[:, None] == jnp.arange(seq_count, dtype=jnp.int32)[None, :]).astype(
        jnp.float32
    )
    flag_tok = jnp.sum(seq_pick * replay.astype(jnp.float32)[None, :], axis=1)
    weight = resp_mask.astype(jnp.float32) * (1.0 - REPLAY_CUT * flag_tok)
    loss_part = jnp.sum(weight[:, None] * miss_vec * miss_vec)
    grad_guess = (2.0 * factor * weight[:, None] * miss_vec).astype(jnp.bfloat16)
    row_unit = 8 * lax.axis_size("dp") * groups
    map_slab = scatter_rows(pad_rows(contract_rows(grad_guess, student_out), row_unit), 1)
    grad_output = contract_cols(grad_guess, w_map)
    rows_two_back, before_back, hidden_back = (rows_two, before, hidden)
    rows_one_back, mixed_back, heads_back, logs_back = (rows_one, mixed_qkv, head_out, log_sums)
    grad_mlp = student_gather(grad_output.astype(jnp.bfloat16))
    grad_mlp, map_slab = lax.optimization_barrier((grad_mlp, map_slab))
    grad_proj = contract_rows(hidden_back, grad_mlp)
    grad_hidden = contract_cols(grad_mlp, w_proj)
    gelu_vals, gelu_pull = jax.vjp(smooth_gelu, before_back)
    grad_before = gelu_pull(grad_hidden)[0].astype(jnp.bfloat16)
    grad_fc = contract_rows(rows_two_back, grad_before).reshape(-1, DS)
    mlp_slab = scatter_rows(jnp.concatenate([grad_proj, grad_fc], axis=0), 2)
    grad_normed_two = student_reduce(grad_before, w_fc, 1)
    grad_normed_two, mlp_slab = lax.optimization_barrier((grad_normed_two, mlp_slab))
    grad_resid = grad_output + norm_back(grad_normed_two, unit_two, scale_two, s_norms[2])
    grad_attn = student_gather(grad_resid.astype(jnp.bfloat16))
    grad_mlp_rows = spread(mlp_slab, 7)
    grad_attn, grad_mlp_rows = lax.optimization_barrier((grad_attn, grad_mlp_rows))
    grad_proj, grad_fc = grad_mlp_rows[:shard_hidden], grad_mlp_rows[shard_hidden:]
    grad_out = contract_rows(heads_back, grad_attn)
    grad_heads = contract_cols(grad_attn, w_out).astype(jnp.bfloat16)

    grad_mixed = attend_backward(mixed_back, logs_back, grad_heads, head_count)
    grad_qkv = contract_rows(grad_mixed, rows_one_back)
    grad_attn_rows, grad_map = sum_and_spread(
        jnp.concatenate([grad_out, grad_qkv], axis=0), map_slab, 3
    )
    raw_map, grad_map = grad_map, grad_map[:DT]
    grad_out, grad_qkv = grad_attn_rows[:shard_width], grad_attn_rows[shard_width:]
    grad_fc = grad_fc.reshape(DS, shard_hidden)
    def to_tall(mat):
        return mat.transpose(1, 2, 0).reshape(-1, DS)

    def from_tall(mat):
        return mat.reshape(3, shard_width, DS).transpose(2, 0, 1)

    moments = [
        MOMENTUM * to_tall(mom_qkv) + grad_qkv,
        MOMENTUM * mom_out + grad_out,
        MOMENTUM * mom_fc + grad_fc,
        MOMENTUM * mom_proj + grad_proj,
    ]
    moment_map = MOMENTUM * mom_map.T + grad_map
    dp_count = lax.axis_size("dp")
    dp_rank = lax.axis_index("dp")
    slice_rows = DS // dp_count
    first_row = dp_rank * slice_rows
    talls = [moments[0], moments[1], moments[2], moments[3], moment_map]
    sums = [0, 0, 1, 0, 0]

    def gram_rows(tall, axis):
        return lax.dot_general(
            lax.dynamic_slice_in_dim(tall, first_row, slice_rows, 1 - axis),
            tall,
            (((axis,), (axis,)), ((), ())),
            precision=lax.Precision.HIGH,
            preferred_element_type=jnp.float32,
        )

    parts = jnp.concatenate([gram_rows(talls[i], sums[i]) for i in range(4)], axis=0)
    gram_mat = share_gram(parts, gram_rows(talls[4], sums[4]), 9)
    gram_mat, grad_mixed = lax.optimization_barrier((gram_mat, grad_mixed))
    grad_normed_one = student_reduce(grad_mixed, w_qkv, 1)
    mine = dp_rank % 2
    factor_mat = orthogonal_factor(gram_mat)
    pair_rows = lax.dynamic_slice_in_dim(factor_mat, (dp_rank // 2) * 2 * slice_rows, 2 * slice_rows, 0)
    other_rows = lax.ppermute(
        pair_rows, "dp", [(i, i ^ 1) for i in range(dp_count)]
    )
    even_rows = jnp.where(mine == 0, pair_rows, other_rows)
    odd_rows = jnp.where(mine == 0, other_rows, pair_rows)
    even_rows = lax.dynamic_slice_in_dim(even_rows, mine * slice_rows, slice_rows, 0)
    odd_rows = lax.dynamic_slice_in_dim(odd_rows, mine * slice_rows, slice_rows, 0)
    even_rows, grad_normed_one = lax.optimization_barrier((even_rows, grad_normed_one))
    factor_rows = line_gather(even_rows, 10).reshape(groups, slice_rows, DS)
    input_grad = grad_resid + norm_back(grad_normed_one, unit_one, scale_one, s_norms[0])
    norm_grads = jnp.stack(
        [
            jnp.sum(grad_normed_one * unit_one, axis=0),
            jnp.sum(grad_normed_one, axis=0),
            jnp.sum(grad_normed_two * unit_two, axis=0),
            jnp.sum(grad_normed_two, axis=0),
        ]
    )
    small = jnp.concatenate(
        [norm_grads, jnp.full((4, DS), loss_part, jnp.float32)], axis=0
    )
    small = sum_small(small, 4)
    norm_grads = small[:4]
    loss = small[4, 0] / (count_val * DT)

    def piece_of(index, rows):
        return lax.dot_general(
            rows,
            talls[index],
            (((1,), (1 - sums[index],)), ((), ())),
            precision=lax.Precision.HIGH,
            preferred_element_type=jnp.float32,
        ).astype(jnp.bfloat16)

    map_all = lax.all_gather(piece_of(4, odd_rows), "dp", axis=0, tiled=True)
    pieces = [piece_of(i, factor_rows[i]) for i in (2, 3, 1, 0)]
    joined, grad_attn_rows, grad_mlp_rows, raw_map = lax.optimization_barrier(
        (jnp.concatenate(pieces, axis=1), grad_attn_rows, grad_mlp_rows, raw_map)
    )
    iterate_all = lax.all_gather(joined, "dp", axis=0, tiled=True)
    grad_out, grad_qkv = grad_attn_rows[:shard_width], grad_attn_rows[shard_width:]
    grad_proj = grad_mlp_rows[:shard_hidden]
    grad_fc = grad_mlp_rows[shard_hidden:].reshape(DS, shard_hidden)
    grad_map = raw_map[:DT]
    weight_fc, weight_proj, weight_out, weight_qkv, weight_map = renew(
        iterate_all,
        map_all,
        (s_fc, s_proj, s_out, to_tall(s_qkv), s_map.T),
        [piece.shape[1] for piece in pieces] + [DT],
        [False, True, True, True, True],
        [math.sqrt(FS / DS), 1.0, 1.0, math.sqrt(3.0), math.sqrt(DT / DS)],
    )
    norm_first = BETA_ONE * adam_first + (1.0 - BETA_ONE) * norm_grads
    norm_second = BETA_TWO * adam_second + (1.0 - BETA_TWO) * norm_grads * norm_grads
    fix_one = 1.0 - BETA_ONE**STEP
    fix_two = 1.0 - BETA_TWO**STEP
    norm_values = s_norms - ADAM_RATE * (
        norm_first / fix_one / (jnp.sqrt(norm_second / fix_two) + ADAM_EPS) + ADAM_DECAY * s_norms
    )
    return (
        teacher_out,
        student_out,
        input_grad,
        loss,
        from_tall(grad_qkv),
        grad_out,
        grad_fc,
        grad_proj,
        grad_map.T,
        from_tall(moments[0]),
        moments[1],
        moments[2],
        moments[3],
        moment_map.T,
        from_tall(weight_qkv),
        weight_out,
        weight_fc,
        weight_proj,
        weight_map.T,
        norm_first,
        norm_second,
        norm_values,
    )


def solution(mesh):
    return jax.shard_map(
        body,
        mesh=mesh,
        in_specs=(
            P(("dp", "tensor"), None),
            P(("dp", "tensor"), None),
            P(("dp", "tensor")),
            P("dp"),
            P(),
            P(),
            P(None, None, "tensor"),
            P("tensor", None),
            P(None, "tensor"),
            P("tensor", None),
            P(),
            P(None, None, "tensor"),
            P("tensor", None),
            P(None, "tensor"),
            P("tensor", None),
            P(),
            P(None, None, "tensor"),
            P("tensor", None),
            P(None, "tensor"),
            P("tensor", None),
            P(),
            P(),
            P(),
        ),
        out_specs=(
            P(("dp", "tensor"), None),
            P(("dp", "tensor"), None),
            P(("dp", "tensor"), None),
            P(),
            P(None, None, "tensor"),
            P("tensor", None),
            P(None, "tensor"),
            P("tensor", None),
            P(),
            P(None, None, "tensor"),
            P("tensor", None),
            P(None, "tensor"),
            P("tensor", None),
            P(),
            P(None, None, "tensor"),
            P("tensor", None),
            P(None, "tensor"),
            P("tensor", None),
            P(),
            P(),
            P(),
            P(),
        ),
        check_vma=False,
    )
```
